32 devices in a mesh: fsdp: 32 (over z, y, x, core).
Axes of the slice: x: 2, y: 2, z: 4, core: 2. Of those that a mesh axis runs over, the one named last changes fastest.
Arguments:
- latents: bfloat16 [256, 256, 384], P('fsdp'), may hold values from -6 to 6
- condition: bfloat16 [256, 384], P('fsdp'), may hold values from -6 to 6
- attn_params: bfloat16 [1477632], P('fsdp'), as said below
- mlp_params: bfloat16 [1181952], P('fsdp'), as said below
- counts: int32 [32], P('fsdp'), may hold values from 1 to 8, as said below
- cotangent: bfloat16 [256, 256, 384], P('fsdp'), may hold values from -6 to 6
Outputs:
- output: bfloat16 [256, 256, 384], P('fsdp')
- grad_latents: float32 [256, 256, 384], P('fsdp')
- grad_condition: float32 [256, 384], P('fsdp')
- grad_attn: float32 [1477632], P('fsdp')
- grad_mlp: float32 [1181952], P('fsdp')
The draws below stay inside these ranges and needn't reach their ends.
Inputs may be any that keep to these rules, and one draw needn't show every extreme that they name: Device i holds live latents in its first counts[i] slots; some device holds 8 and some device 1. `attn_params`: weights and biases in the layout of the steps. `mlp_params`: weights and biases in the layout of the steps.
All inputs are finite; a program needn't handle non-finite values.
Results may differ from the reference program's by a relative error of at most 0.009.
The reference program's roundings to bfloat16 on the way count: a program that leaves them out, or rounds other values in their place, can miss the bound.
Values may be sent and summed in bfloat16 or wider, within the bound.
No kernel may reach another device: no remote copies, remote signals or barrier semaphores. Data moves between devices by JAX's collectives and lax.ppermute only.
A program may use at most 128 MiB of HBM per device.

```python
import math
import jax
import jax.numpy as jnp
from jax import lax

D = 384
HEADS = 6
HEAD_DIM = 64
FF = 1536
SEQ = 256
LAT_DEV = 8
LATENTS = 256
N_FSDP = 32


def piece_scales(sizes_scales):
    return jnp.concatenate([jnp.full((count,), scale, jnp.float32) for count, scale in sizes_scales])


def draw_attn_params(key, part):
    key = jax.random.fold_in(key, 11)
    total = 10 * D * D + 8 * D
    base = jax.random.normal(key, (total,), jnp.float32)
    scales = piece_scales([(6 * D * D, D ** (-0.5)), (3 * D * D, D ** (-0.5)), (D * D, 3.0 * D ** (-0.5)), (6 * D, 0.5), (2 * D, 0.3)])
    shifted = piece_scales([(10 * D * D + 2 * D, 0.0), (D, 1.0), (2 * D, 0.0), (D, 1.0), (2 * D, 0.0)])
    return (base * scales + shifted).astype(jnp.bfloat16)


def draw_mlp_params(key, part):
    key = jax.random.fold_in(key, 13)
    total = 2 * D * FF + FF + 2 * D
    base = jax.random.normal(key, (total,), jnp.float32)
    scales = piece_scales([(D * FF, D ** (-0.5)), (FF * D, FF ** (-0.5)), (FF, 0.3), (D, 0.3), (D, 0.3)])
    return (base * scales).astype(jnp.bfloat16)


def draw_counts(key, part):
    key = jax.random.fold_in(key, 7)
    first_key, second_key = jax.random.split(key)
    drawn = jax.random.randint(first_key, (N_FSDP,), 1, LAT_DEV + 1)
    order = jax.random.permutation(second_key, N_FSDP)
    drawn = drawn.at[order[0]].set(LAT_DEV).at[order[1]].set(1)
    return drawn.astype(jnp.int32)


def level_of(stream_key, shape, cuts, low, top_value):
    factor_of = 1.0
    for axis_at, blocks in cuts:
        draws = jax.random.uniform(jax.random.fold_in(jax.random.fold_in(stream_key, 6), axis_at), (blocks,), jnp.float32, low / len(cuts), top_value / len(cuts))
        factor_of = factor_of * jnp.repeat(jnp.exp(draws), shape[axis_at] // blocks).reshape((-1,) + (1,) * (len(shape) - 1 - axis_at))
    return factor_of


def gaussian(own_key, extent, scale, limit, cuts=(), kind=jnp.bfloat16):
    entries = scale * jax.random.normal(own_key, extent, jnp.float32)
    if cuts:
        entries = entries * level_of(own_key, extent, cuts, -0.22, 0.18)
    return jnp.clip(entries, -limit, limit).astype(kind)


def setup_inputs(seed: int = 0) -> dict:
    key_list = jax.random.split(jax.random.key(seed), 7)
    return {
        "latents": gaussian(key_list[0], (LATENTS, SEQ, D), 1.0, 6.0, ((0, 32),)),
        "condition": gaussian(key_list[1], (LATENTS, D), 1.0, 6.0, ((0, 32),)),
        "attn_params": draw_attn_params(jax.random.fold_in(key_list[6], 71), 0),
        "mlp_params": draw_mlp_params(jax.random.fold_in(key_list[6], 71), 0),
        "counts": draw_counts(jax.random.fold_in(key_list[6], 71), 0),
        "cotangent": gaussian(key_list[5], (LATENTS, SEQ, D), 1.0, 6.0, ((0, 32),)),
    }


@jax.custom_vjp
def low(v):
    return lax.optimization_barrier(v.astype(jnp.bfloat16)).astype(jnp.float32)

@jax.custom_vjp
def low_back(v):
    return v

def low_keep(v):
    return (low(v), None)

def low_pass(kept, grad):
    return (grad,)

def back_keep(v):
    return (v, None)

def back_low(kept, grad):
    return (low(grad),)
low.defvjp(low_keep, low_pass)
low_back.defvjp(back_keep, back_low)

def split_flat(flat, shapes):
    pieces = []
    start = 0
    for shape in shapes:
        count = math.prod(shape)
        pieces.append(flat[start:start + count].reshape(shape))
        start = start + count
    return pieces

def attention_shapes():
    return [(D, 6 * D), (D, 3 * D), (D, D), (6 * D,), (2 * D,)]

def feedforward_shapes():
    return [(D, FF), (FF, D), (FF,), (D,), (D,)]

def matmul(left, right):
    return jnp.einsum('gsd,de->gse', left, right, precision=lax.Precision.HIGHEST)

def normalize(values):
    average = lax.optimization_barrier(jnp.mean(values, -1, keepdims=True))
    centered = values - average
    return centered * lax.rsqrt(lax.optimization_barrier(jnp.mean(centered * centered, -1, keepdims=True)) + 1e-06)

def block(inputs, cond, attn_flat, mlp_flat):
    w_ada, w_qkv, w_proj, b_ada, b_qv = split_flat(attn_flat, attention_shapes())
    w_fc1, w_fc2, b_fc1, b_fc2, b_proj = split_flat(mlp_flat, feedforward_shapes())
    cond_act = low(jax.nn.silu(cond))
    modulation = low_back(jnp.dot(cond_act, w_ada, precision=lax.Precision.HIGHEST) + b_ada)
    parts = [modulation[:, index * D:(index + 1) * D][:, None, :] for index in range(6)]
    shift_one, scale_one, gate_one, shift_two, scale_two, gate_two = parts
    mod_one = low(normalize(inputs) * (1.0 + scale_one) + shift_one)
    qkv = matmul(mod_one, w_qkv)
    queries = low_back(low(qkv[..., :D] + b_qv[:D]))
    keys_all = low_back(low(qkv[..., D:2 * D]))
    values = low_back(low(qkv[..., 2 * D:] + b_qv[D:]))
    batch = inputs.shape[0]
    shape_heads = (batch, SEQ, HEADS, HEAD_DIM)
    scores = jnp.einsum('gqhd,gkhd->ghqk', queries.reshape(shape_heads), keys_all.reshape(shape_heads), precision=lax.Precision.HIGHEST) * HEAD_DIM ** (-0.5)
    scores = low_back(scores)
    probs = low(jax.nn.softmax(scores, axis=-1))
    mixed = jnp.einsum('ghqk,gkhd->gqhd', probs, values.reshape(shape_heads), precision=lax.Precision.HIGHEST)
    mixed = low_back(low(mixed.reshape(batch, SEQ, D)))
    branch_one = low_back(matmul(mixed, w_proj) + b_proj)
    middle = inputs + gate_one * branch_one
    mod_two = low(normalize(middle) * (1.0 + scale_two) + shift_two)
    hidden_pre = low_back(matmul(mod_two, w_fc1) + b_fc1)
    hidden_act = low(jax.nn.gelu(hidden_pre, approximate=True))
    branch_two = low_back(matmul(hidden_act, w_fc2) + b_fc2)
    return middle + gate_two * branch_two

def reference(latents, condition, attn_params, mlp_params, counts, cotangent):
    attn_flat = attn_params.astype(jnp.float32)
    mlp_flat = mlp_params.astype(jnp.float32)
    live_mask = (jnp.arange(LAT_DEV)[None, :] < counts[:, None]).reshape(LATENTS).astype(jnp.float32)
    per_block = 16
    block_count = LATENTS // per_block

    def shaped(array):
        return array.reshape((block_count, per_block) + array.shape[1:])

    def one_block(totals, pieces):
        x_part, c_part, cot_part, mask_part = pieces
        result, pull = jax.vjp(block, x_part.astype(jnp.float32), c_part.astype(jnp.float32), attn_flat, mlp_flat)
        grad_x, grad_c, grad_a, grad_m = pull(cot_part.astype(jnp.float32) * mask_part[:, None, None])
        masked = (result * mask_part[:, None, None]).astype(jnp.bfloat16)
        return ((totals[0] + grad_a, totals[1] + grad_m), (masked, grad_x, grad_c))
    start = (jnp.zeros_like(attn_flat), jnp.zeros_like(mlp_flat))
    totals, outputs = lax.scan(one_block, start, (shaped(latents), shaped(condition), shaped(cotangent), shaped(live_mask)))
    output, grad_x, grad_c = outputs
    return (output.reshape(LATENTS, SEQ, D), grad_x.reshape(LATENTS, SEQ, D), grad_c.reshape(LATENTS, D), totals[0], totals[1])
```

```python
import jax
import jax.numpy as jnp
from jax import lax
from jax.experimental import pallas as pl
from jax.experimental.pallas import tpu as pltpu
from jax.sharding import PartitionSpec as P

D = 384
HEADS = 6
HEAD_DIM = 64
FF = 1536
EPSILON = 1e-06
AXIS = "fsdp"
LANES = 128
TILES = D // LANES
GROUP = 8 * D
FACTOR = HEAD_DIM ** (-0.5)
GELU_A = 0.7978845608028654
GELU_B = 0.044715

ADA_AT = 0
QKV_AT = 6 * D
PROJ_AT = 9 * D
B_ADA_AT = 10 * D
B_QV_AT = 10 * D + 6
ATTN_ROWS = 10 * D + 8
FC1_AT = 0
FC2_AT = FF
B_FC1_AT = 2 * FF
B_FC2_AT = 2 * FF + 4
B_PROJ_AT = 2 * FF + 5
MLP_ROWS = 2 * FF + 6

F32 = jnp.float32
BF16 = jnp.bfloat16


def round_up(value, unit):
    return -(-value // unit) * unit


def piece_rows(share, count):
    lead = max((share * index) % GROUP for index in range(count))
    return round_up(-(-(share + lead) // D), 16)


def mm(left, right):
    return jnp.dot(left, right, preferred_element_type=F32)


def mm_nt(left, right):
    return lax.dot_general(left, right, (((1,), (1,)), ((), ())), preferred_element_type=F32)


def mm_tn(left, right):
    return lax.dot_general(left, right, (((0,), (0,)), ((), ())), preferred_element_type=F32)


def col_sum(values):
    return jnp.sum(values, axis=0, keepdims=True)


def row_mean(values):
    return jnp.mean(values, axis=-1, keepdims=True)


def normalize(values):
    centered = values - row_mean(values)
    rstd = lax.rsqrt(row_mean(centered * centered) + EPSILON)
    return centered * rstd, rstd


def normalize_back(grad, normed, rstd):
    return rstd * (grad - row_mean(grad) - normed * row_mean(grad * normed))


def head_masks():
    lane = lax.broadcasted_iota(jnp.int32, (1, LANES), 1) // HEAD_DIM
    return [(lane == head).astype(F32).astype(BF16) for head in range(2)]


def assemble(scal_ref, base, piece_refs, rows_ref):
    rows_ref[...] = jnp.zeros_like(rows_ref)
    at = base
    for ref in piece_refs:
        slots, height = ref.shape[0], ref.shape[1]

        def one(slot, carry, ref=ref, at=at, height=height):
            start = pl.multiple_of(scal_ref[at + slot] * 8, 8)
            for tile in range(TILES):
                lanes = slice(tile * LANES, (tile + 1) * LANES)
                rows_ref[tile, pl.ds(start, height), :] += ref[slot, :, lanes].astype(F32)
            return carry

        lax.fori_loop(0, slots, one, 0)
        at += slots


def emit(scal_ref, base, out_refs, rows_ref):
    at = base
    for ref in out_refs:
        slots, height = ref.shape[0], ref.shape[1]

        def one(slot, carry, ref=ref, at=at, height=height):
            start = pl.multiple_of(scal_ref[at + slot] * 8, 8)
            for tile in range(TILES):
                lanes = slice(tile * LANES, (tile + 1) * LANES)
                ref[slot, :, lanes] = rows_ref[tile, pl.ds(start, height), :].astype(ref.dtype)
            return carry

        lax.fori_loop(0, slots, one, 0)
        at += slots


def lanes_of(tile, offset=0):
    return slice(offset + tile * LANES, offset + (tile + 1) * LANES)


def forward_kernel(n_pieces, scal_ref, cond_ref, x_ref, *refs):
    pieces = refs[:n_pieces]
    mod_ref, ada_ref, qkv_w_ref, proj_ref, bias_ref, qkv_ref, probs_ref, mixed_ref, branch_ref = refs[
        n_pieces : n_pieces + 9
    ]
    rows_ref = refs[n_pieces + 9]
    step = pl.program_id(0)

    @pl.when(step == 0)
    def _():
        assemble(scal_ref, 1, pieces, rows_ref)
        for block in range(6):
            for tile in range(TILES):
                ada_ref[block, :, lanes_of(tile)] = rows_ref[
                    tile, pl.ds(ADA_AT + block, D, stride=6), :
                ].astype(BF16)
        for block in range(3):
            for tile in range(TILES):
                qkv_w_ref[:, lanes_of(tile, block * D)] = rows_ref[
                    tile, pl.ds(QKV_AT + block, D, stride=3), :
                ].astype(BF16)
        for tile in range(TILES):
            proj_ref[:, lanes_of(tile)] = rows_ref[tile, pl.ds(PROJ_AT, D), :].astype(BF16)
            bias_ref[:, lanes_of(tile)] = rows_ref[tile, pl.ds(B_ADA_AT, 8), :]
        act = jax.nn.silu(cond_ref[...].astype(F32)).astype(BF16)
        for block in range(6):
            mod_ref[block] = mm(act, ada_ref[block]) + bias_ref[pl.ds(block, 1), :]

    @pl.when(step < scal_ref[0])
    def _():
        masks = head_masks()
        values = x_ref[0].astype(F32)
        normed, _ = normalize(values)
        shift = mod_ref[0, pl.ds(step, 1), :]
        scale = mod_ref[1, pl.ds(step, 1), :]
        modulated = (normed * (1.0 + scale) + shift).astype(BF16)
        qkv = mm(modulated, qkv_w_ref[...])
        queries = (qkv[:, :D] + bias_ref[6:7, :]).astype(BF16)
        keys_all = qkv[:, D : 2 * D].astype(BF16)
        values_all = (qkv[:, 2 * D :] + bias_ref[7:8, :]).astype(BF16)
        qkv_ref[0, :, :D] = queries
        qkv_ref[0, :, D : 2 * D] = keys_all
        qkv_ref[0, :, 2 * D :] = values_all
        values_t = values_all.T
        for pair in range(HEADS // 2):
            lanes = lanes_of(pair)
            query, key = queries[:, lanes], keys_all[:, lanes]
            for half in range(2):
                head = 2 * pair + half
                scores = mm_nt(key, query * masks[half]) * FACTOR
                expo = jnp.exp(scores - jnp.max(scores, axis=0, keepdims=True))
                probs = expo * (1.0 / col_sum(expo))
                probs_ref[0, head] = probs
                rows = slice(head * HEAD_DIM, (head + 1) * HEAD_DIM)
                mixed_ref[0, rows, :] = mm(values_t[rows, :], probs.astype(BF16)).astype(BF16)
        branch_ref[0] = mm_tn(mixed_ref[0], proj_ref[...])


def mlp_kernel(n_pieces, n_out, scal_ref, mod_ref, proj_ref, x_ref, branch_ref, mixed_ref, cot_ref, *refs):
    pieces = refs[:n_pieces]
    outs = refs[n_pieces : n_pieces + 5 + n_out]
    out_ref, dx_ref, dmixed_ref, dmod_ref, dproj_ref = outs[:5]
    send_refs = outs[5:]
    rows_ref, fc1_ref, fc2_ref, bias_ref, act_ref, slope_ref, dfc1_ref, dfc2_ref, dbias_ref = refs[
        n_pieces + 5 + n_out :
    ]
    step = pl.program_id(0)
    last = pl.num_programs(0) - 1

    @pl.when(step == 0)
    def _():
        assemble(scal_ref, 1, pieces, rows_ref)
        for block in range(4):
            for tile in range(TILES):
                fc1_ref[:, lanes_of(tile, block * D)] = rows_ref[
                    tile, pl.ds(FC1_AT + block, D, stride=4), :
                ].astype(BF16)
                bias_ref[0:1, lanes_of(tile, block * D)] = rows_ref[tile, pl.ds(B_FC1_AT + block, 1), :]
        for tile in range(TILES):
            fc2_ref[:, lanes_of(tile)] = rows_ref[tile, pl.ds(FC2_AT, FF), :].astype(BF16)
            bias_ref[1:2, lanes_of(tile)] = rows_ref[tile, pl.ds(B_FC2_AT, 1), :]
            bias_ref[2:3, lanes_of(tile)] = rows_ref[tile, pl.ds(B_PROJ_AT, 1), :]
        dfc1_ref[...] = jnp.zeros_like(dfc1_ref)
        dfc2_ref[...] = jnp.zeros_like(dfc2_ref)
        dbias_ref[...] = jnp.zeros_like(dbias_ref)
        dproj_ref[...] = jnp.zeros_like(dproj_ref)
        dmod_ref[...] = jnp.zeros_like(dmod_ref)

    @pl.when(step < scal_ref[0])
    def _():
        row = pl.ds(step, 1)
        gate_one, shift, scale, gate_two = [mod_ref[2 + part, row, :] for part in range(4)]
        branch_one = branch_ref[0] + bias_ref[2:3, :D]
        middle = x_ref[0].astype(F32) + gate_one * branch_one
        normed, rstd = normalize(middle)
        modulated = (normed * (1.0 + scale) + shift).astype(BF16)
        chunk = 512
        branch_two = jnp.zeros_like(middle)
        for start in range(0, FF, chunk):
            part = slice(start, start + chunk)
            pre = mm(modulated, fc1_ref[:, part]) + bias_ref[0:1, part]
            square = pre * pre
            bend = jnp.tanh(GELU_A * pre * (1.0 + GELU_B * square))
            half = 0.5 * (1.0 + bend)
            act = (pre * half).astype(BF16)
            act_ref[:, part] = act
            slope_ref[:, part] = half + (0.5 * GELU_A) * pre * (1.0 - bend * bend) * (
                1.0 + (3.0 * GELU_B) * square
            )
            branch_two += mm(act, fc2_ref[part, :])
        branch_two += bias_ref[1:2, :D]
        out_ref[0] = (middle + gate_two * branch_two).astype(BF16)
        grad_out = cot_ref[0].astype(F32)
        dmod_ref[3, row, :] = col_sum(grad_out * branch_two)
        grad_two = gate_two * grad_out
        grad_two_low = grad_two.astype(BF16)
        dbias_ref[1:2, :D] += col_sum(grad_two_low.astype(F32))
        grad_two_t = grad_two_low.T
        modulated_t = modulated.T
        grad_mod = jnp.zeros_like(middle)
        for start in range(0, FF, chunk):
            part = slice(start, start + chunk)
            du = (mm_nt(grad_two_low, fc2_ref[part, :]) * slope_ref[:, part]).astype(BF16)
            dbias_ref[0:1, part] += col_sum(du.astype(F32))
            dfc2_ref[:, part] += mm(grad_two_t, act_ref[:, part])
            dfc1_ref[:, part] += mm(modulated_t, du)
            grad_mod += mm_nt(du, fc1_ref[:, part])
        dmod_ref[1, row, :] = col_sum(grad_mod)
        dmod_ref[2, row, :] = col_sum(grad_mod * normed)
        grad_middle = grad_out + normalize_back(grad_mod * (1.0 + scale), normed, rstd)
        dx_ref[0] = grad_middle
        dmod_ref[0, row, :] = col_sum(grad_middle * branch_one)
        grad_one = (gate_one * grad_middle).astype(BF16)
        dbias_ref[2:3, :D] += col_sum(grad_one.astype(F32))
        dproj_ref[...] += mm(mixed_ref[0], grad_one)
        dmixed_ref[0] = mm_nt(grad_one, proj_ref[...]).astype(BF16)

    @pl.when(step >= scal_ref[0])
    def _():
        out_ref[...] = jnp.zeros_like(out_ref)
        dx_ref[...] = jnp.zeros_like(dx_ref)
        dmixed_ref[...] = jnp.zeros_like(dmixed_ref)

    @pl.when(step == last)
    def _():
        for block in range(4):
            for tile in range(TILES):
                rows_ref[tile, pl.ds(FC1_AT + block, D, stride=4), :] = dfc1_ref[
                    :, lanes_of(tile, block * D)
                ]
                rows_ref[tile, pl.ds(B_FC1_AT + block, 1), :] = dbias_ref[0:1, lanes_of(tile, block * D)]
        for tile in range(TILES):
            rows_ref[tile, pl.ds(FC2_AT, FF), :] = dfc2_ref[lanes_of(tile), :].T
            rows_ref[tile, pl.ds(B_FC2_AT, 1), :] = dbias_ref[1:2, lanes_of(tile)]
            rows_ref[tile, pl.ds(B_PROJ_AT, 1), :] = dbias_ref[2:3, lanes_of(tile)]
        emit(scal_ref, 1 + sum(ref.shape[0] for ref in pieces), send_refs, rows_ref)


def backward_kernel(
    n_out, base, scal_ref, cond_ref, mod_ref, ada_ref, qkv_w_ref, dmod_in_ref, dproj_ref,
    x_ref, qkv_ref, probs_ref, dx_ref, dmixed_ref, *refs
):
    grad_x_ref, grad_cond_ref = refs[:2]
    send_refs = refs[2 : 2 + n_out]
    rows_ref, dqkv_w_ref, dmod_ref, dbias_ref, dqkv_ref, dq_t_ref = refs[2 + n_out :]
    step = pl.program_id(0)
    last = pl.num_programs(0) - 1

    @pl.when(step == 0)
    def _():
        dqkv_w_ref[...] = jnp.zeros_like(dqkv_w_ref)
        dmod_ref[...] = jnp.zeros_like(dmod_ref)
        dbias_ref[...] = jnp.zeros_like(dbias_ref)

    @pl.when(step < scal_ref[0])
    def _():
        masks = head_masks()
        row = pl.ds(step, 1)
        shift = mod_ref[0, row, :]
        scale = mod_ref[1, row, :]
        normed, rstd = normalize(x_ref[0].astype(F32))
        modulated = (normed * (1.0 + scale) + shift).astype(BF16)
        keys_t = qkv_ref[0, :, D : 2 * D].T
        for pair in range(HEADS // 2):
            query = qkv_ref[0, :, lanes_of(pair)]
            value = qkv_ref[0, :, lanes_of(pair, 2 * D)]
            grad = dmixed_ref[0, :, lanes_of(pair)]
            grad_key = jnp.zeros((query.shape[0], LANES), F32)
            grad_value = jnp.zeros((query.shape[0], LANES), F32)
            for half in range(2):
                head = 2 * pair + half
                rows = slice(head * HEAD_DIM, (head + 1) * HEAD_DIM)
                query_own = query * masks[half]
                grad_own = grad * masks[half]
                probs = probs_ref[0, head]
                grad_value += mm(probs.astype(BF16), grad_own)
                grad_probs = mm_nt(value, grad_own)
                grad_scores = (probs * (grad_probs - col_sum(probs * grad_probs))).astype(BF16)
                grad_key += mm(grad_scores, query_own)
                dq_t_ref[rows, :] = mm(keys_t[rows, :], grad_scores)
            dqkv_ref[:, lanes_of(pair, D)] = (grad_key * FACTOR).astype(BF16)
            dqkv_ref[:, lanes_of(pair, 2 * D)] = grad_value.astype(BF16)
        dqkv_ref[:, :D] = (dq_t_ref[...] * FACTOR).astype(BF16).T
        grad_qkv = dqkv_ref[...]
        dbias_ref[0:1, :] += col_sum(grad_qkv.astype(F32))
        dqkv_w_ref[...] += mm(modulated.T, grad_qkv)
        grad_mod = mm_nt(grad_qkv, qkv_w_ref[...])
        dmod_ref[0, row, :] = col_sum(grad_mod)
        dmod_ref[1, row, :] = col_sum(grad_mod * normed)
        grad_x_ref[0] = dx_ref[0] + normalize_back(grad_mod * (1.0 + scale), normed, rstd)

    @pl.when(step >= scal_ref[0])
    def _():
        grad_x_ref[...] = jnp.zeros_like(grad_x_ref)

    @pl.when(step == last)
    def _():
        cond = cond_ref[...].astype(F32)
        gate = jax.nn.sigmoid(cond)
        act = (cond * gate).astype(BF16)
        grad_act = jnp.zeros_like(cond)
        for block in range(6):
            grad = (dmod_ref[block] if block < 2 else dmod_in_ref[block - 2]).astype(BF16)
            grad_act += mm_nt(grad, ada_ref[block])
            weight = mm_tn(act, grad)
            bias = col_sum(grad.astype(F32))
            for tile in range(TILES):
                rows_ref[tile, pl.ds(ADA_AT + block, D, stride=6), :] = weight[:, lanes_of(tile)]
                rows_ref[tile, pl.ds(B_ADA_AT + block, 1), :] = bias[:, lanes_of(tile)]
        grad_cond_ref[...] = grad_act * (gate * (1.0 + cond * (1.0 - gate)))
        for tile in range(TILES):
            for block in range(3):
                rows_ref[tile, pl.ds(QKV_AT + block, D, stride=3), :] = dqkv_w_ref[
                    :, lanes_of(tile, block * D)
                ]
            rows_ref[tile, pl.ds(PROJ_AT, D), :] = dproj_ref[:, lanes_of(tile)]
            rows_ref[tile, pl.ds(B_QV_AT, 1), :] = dbias_ref[0:1, lanes_of(tile)]
            rows_ref[tile, pl.ds(B_QV_AT + 1, 1), :] = dbias_ref[0:1, lanes_of(tile, 2 * D)]
        emit(scal_ref, base, send_refs, rows_ref)


class Direct:
    def __init__(self, count, me):
        self.count, self.me = count, me
        self.gathered = self.sent = [jnp.int32(index) for index in range(count)]
        self.slots = [(count, F32)]

    def gather(self, piece):
        return [lax.all_gather(piece, AXIS, axis=0)]

    def scatter(self, parts):
        return lax.psum_scatter(parts[0], AXIS, scatter_dimension=0)


class Stages:
    def __init__(self, count, me):
        self.me = me
        core, x, y, z = me % 2, me // 2 % 2, me // 4 % 2, me // 8

        def device(dz, dy, dx, dc):
            return (((z + dz) % 4 * 2 + (y + dy) % 2) * 2 + (x + dx) % 2) * 2 + (core + dc) % 2

        gathered = []
        for dc in range(2):
            gathered += [device(-k, 0, 0, dc) for k in (0, 1, 2, 3)]
            gathered += [device(-k, 0, 1, dc) for k in (0, 1)]
            gathered += [device(-k, 1, 0, dc) for k in (2, 3)]
            gathered += [device(-k, 1, dx, dc) for dx in (0, 1) for k in (0, 1)]
            gathered += [device(-k, dy, 1, dc) for dy in (0, 1) for k in (2, 3)]
        self.gathered = gathered
        sent = []
        for dc in (1, 0):
            sent += [device(k, dy, dx, dc) for dx in (0, 1) for k in (0, 1) for dy in (0, 1)]
            sent += [device(k, dy, dx, dc) for dy in (0, 1) for k in (2, 3) for dx in (0, 1)]
        self.sent = sent
        self.slots = [(8, BF16), (8, BF16), (8, F32), (8, F32)]

    def shift(self, values, dz=0, dy=0, dx=0, dc=0):
        pairs = []
        for source in range(32):
            core, x, y, z = source % 2, source // 2 % 2, source // 4 % 2, source // 8
            target = (((z + dz) % 4 * 2 + (y + dy) % 2) * 2 + (x + dx) % 2) * 2 + (core + dc) % 2
            pairs.append((source, target))
        return lax.ppermute(values, AXIS, pairs)

    def gather(self, piece):
        own = jnp.stack([piece] + [self.shift(piece, dz=k) for k in (1, 2, 3)])
        first, second = own[:2], own[2:]
        by_x = self.shift(first, dx=1)
        by_y = self.shift(second, dy=1)
        by_xy = self.shift(jnp.concatenate([first, by_x]), dy=1)
        by_yx = self.shift(jnp.concatenate([second, by_y]), dx=1)
        held = [own, by_x, by_y, by_xy, by_yx]
        return held + [self.shift(array, dc=1) for array in held]

    def scatter(self, parts):
        def send(values, **how):
            return self.shift(values.astype(BF16), **how).astype(F32)

        send_a, send_b, keep_a, keep_b = parts
        shape = keep_a.shape[1:]
        sum_a = (keep_a + send(send_a, dc=1)).reshape((2, 4) + shape)
        sum_b = (keep_b + send(send_b, dc=1)).reshape((2, 4) + shape)
        sum_a = (sum_a[0] + send(sum_a[1], dx=1)).reshape((2, 2) + shape)
        sum_b = (sum_b[0] + send(sum_b[1], dy=1)).reshape((2, 2) + shape)
        sum_a = sum_a[:, 0] + send(sum_a[:, 1], dy=1)
        sum_b = sum_b[:, 0] + send(sum_b[:, 1], dx=1)
        return (
            sum_a[0] + send(sum_a[1], dz=1) + send(sum_b[0], dz=2) + send(sum_b[1], dz=3)
        )


def to_piece(share, rows, me):
    size = share.shape[0]
    flat = jnp.zeros((rows * D,), share.dtype)
    return lax.dynamic_update_slice(flat, share, (size * me % GROUP,)).reshape(rows, D)


def from_piece(piece, size, me):
    return lax.dynamic_slice(piece.reshape(-1), (size * me % GROUP,), (size,))


def whole(shape=None):
    return pl.BlockSpec(memory_space=pltpu.VMEM)


def by_latent(*shape):
    zeros = (0,) * len(shape)
    return pl.BlockSpec((1,) + shape, lambda step, scal: (step,) + zeros)


def call(kernel, count, in_specs, out_specs, out_shape, scratch, args, flops):
    return pl.pallas_call(
        kernel,
        grid_spec=pltpu.PrefetchScalarGridSpec(
            num_scalar_prefetch=1,
            grid=(count,),
            in_specs=in_specs,
            out_specs=out_specs,
            scratch_shapes=scratch,
        ),
        out_shape=out_shape,
        compiler_params=pltpu.CompilerParams(
            vmem_limit_bytes=60 * 2**20, dimension_semantics=("arbitrary",)
        ),
        cost_estimate=pl.CostEstimate(flops=flops, bytes_accessed=20 * 2**20, transcendentals=0),
    )(*args)


def solution(mesh):
    devices = mesh.shape[AXIS]

    def body(latents, condition, attn_params, mlp_params, counts, cotangent):
        count, seq = latents.shape[0], latents.shape[1]
        me = lax.axis_index(AXIS)
        plan = (Stages if devices == 32 else Direct)(devices, me)
        attn_size, mlp_size = attn_params.shape[0], mlp_params.shape[0]
        attn_height = piece_rows(attn_size, devices)
        mlp_height = piece_rows(mlp_size, devices)

        def scalars(size):
            ids = jnp.stack(plan.gathered + plan.sent)
            return jnp.concatenate([counts.astype(jnp.int32), size * ids // GROUP]).astype(jnp.int32)

        attn_scal, mlp_scal = scalars(attn_size), scalars(mlp_size)
        attn_pieces = plan.gather(to_piece(attn_params, attn_height, me))
        mlp_pieces = plan.gather(to_piece(mlp_params, mlp_height, me))

        def struct(shape, kind):
            return jax.ShapeDtypeStruct(shape, kind)

        n_pieces = len(attn_pieces)
        n_out = len(plan.slots)
        mod, ada, qkv_w, proj, _, qkv, probs, mixed, branch = call(
            lambda *refs: forward_kernel(n_pieces, *refs),
            count,
            [whole(), by_latent(seq, D)] + [whole()] * n_pieces,
            [whole()] * 5
            + [
                by_latent(seq, 3 * D),
                by_latent(HEADS, seq, seq),
                by_latent(D, seq),
                by_latent(seq, D),
            ],
            [
                struct((6, count, D), F32),
                struct((6, D, D), BF16),
                struct((D, 3 * D), BF16),
                struct((D, D), BF16),
                struct((8, D), F32),
                struct((count, seq, 3 * D), BF16),
                struct((count, HEADS, seq, seq), F32),
                struct((count, D, seq), BF16),
                struct((count, seq, D), F32),
            ],
            [pltpu.VMEM((TILES, ATTN_ROWS + attn_height, LANES), F32)],
            [attn_scal, condition, latents] + attn_pieces,
            15 * 10**9,
        )
        results = call(
            lambda *refs: mlp_kernel(n_pieces, n_out, *refs),
            count,
            [whole(), whole(), by_latent(seq, D), by_latent(seq, D), by_latent(D, seq), by_latent(seq, D)]
            + [whole()] * n_pieces,
            [by_latent(seq, D), by_latent(seq, D), by_latent(seq, D), whole(), whole()]
            + [whole()] * n_out,
            [
                struct((count, seq, D), BF16),
                struct((count, seq, D), F32),
                struct((count, seq, D), BF16),
                struct((4, count, D), F32),
                struct((D, D), F32),
            ]
            + [struct((slots, mlp_height, D), kind) for slots, kind in plan.slots],
            [
                pltpu.VMEM((TILES, MLP_ROWS + 2 + mlp_height, LANES), F32),
                pltpu.VMEM((D, FF), BF16),
                pltpu.VMEM((FF, D), BF16),
                pltpu.VMEM((8, FF), F32),
                pltpu.VMEM((seq, FF), BF16),
                pltpu.VMEM((seq, FF), F32),
                pltpu.VMEM((D, FF), F32),
                pltpu.VMEM((D, FF), F32),
                pltpu.VMEM((8, FF), F32),
            ],
            [mlp_scal, mod, proj, latents, branch, mixed, cotangent] + mlp_pieces,
            30 * 10**9,
        )
        output, grad_middle, grad_mixed, dmod, dproj = results[:5]
        grad_mlp = plan.scatter(results[5:])
        results = call(
            lambda *refs: backward_kernel(n_out, 1 + devices, *refs),
            count,
            [whole()] * 6
            + [
                by_latent(seq, D),
                by_latent(seq, 3 * D),
                by_latent(HEADS, seq, seq),
                by_latent(seq, D),
                by_latent(seq, D),
            ],
            [by_latent(seq, D), whole()] + [whole()] * n_out,
            [struct((count, seq, D), F32), struct((count, D), F32)]
            + [struct((slots, attn_height, D), kind) for slots, kind in plan.slots],
            [
                pltpu.VMEM((TILES, ATTN_ROWS + attn_height, LANES), F32),
                pltpu.VMEM((D, 3 * D), F32),
                pltpu.VMEM((2, count, D), F32),
                pltpu.VMEM((8, 3 * D), F32),
                pltpu.VMEM((seq, 3 * D), BF16),
                pltpu.VMEM((D, seq), F32),
            ],
            [attn_scal, condition, mod, ada, qkv_w, dmod, dproj, latents, qkv, probs, grad_middle, grad_mixed],
            30 * 10**9,
        )
        grad_latents, grad_condition = results[:2]
        grad_attn = plan.scatter(results[2:])
        return (
            output,
            grad_latents,
            grad_condition,
            from_piece(grad_attn, attn_size, me),
            from_piece(grad_mlp, mlp_size, me),
        )

    in_specs = (
        P(AXIS, None, None),
        P(AXIS, None),
        P(AXIS),
        P(AXIS),
        P(AXIS),
        P(AXIS, None, None),
    )
    out_specs = (
        P(AXIS, None, None),
        P(AXIS, None, None),
        P(AXIS, None),
        P(AXIS),
        P(AXIS),
    )
    return jax.shard_map(body, mesh=mesh, in_specs=in_specs, out_specs=out_specs, check_vma=False)
```

```python
import jax
import jax.numpy as jnp
from jax import lax
from jax.experimental import pallas as pl
from jax.experimental.pallas import tpu as pltpu
from jax.sharding import PartitionSpec as P

D = 384
HEADS = 6
HEAD_DIM = 64
FF = 1536
EPSILON = 1e-06
AXIS = "fsdp"
LANES = 128
TILES = D // LANES
GROUP = 8 * D
FACTOR = HEAD_DIM ** (-0.5)
GELU_A = 0.7978845608028654
GELU_B = 0.044715
CHUNK = 512
PER_STEP = 2

ADA_AT = 0
QKV_AT = 6 * D
PROJ_AT = 9 * D
B_ADA_AT = 10 * D
B_QV_AT = 10 * D + 6
ATTN_ROWS = 10 * D + 8
FC1_AT = 0
FC2_AT = FF
B_FC1_AT = 2 * FF
B_FC2_AT = 2 * FF + 4
B_PROJ_AT = 2 * FF + 5
MLP_ROWS = 2 * FF + 6

F32 = jnp.float32
BF16 = jnp.bfloat16


def round_up(value, unit):
    return -(-value // unit) * unit


def piece_rows(share, count):
    lead = max((share * index) % GROUP for index in range(count))
    return round_up(-(-(share + lead) // D), 16)


def mm(left, right):
    return jnp.dot(left, right, preferred_element_type=F32)


def mm_nt(left, right):
    return lax.dot_general(left, right, (((1,), (1,)), ((), ())), preferred_element_type=F32)


def mm_tn(left, right):
    return lax.dot_general(left, right, (((0,), (0,)), ((), ())), preferred_element_type=F32)


def col_sum(values):
    return jnp.sum(values, axis=0, keepdims=True)


def row_mean(values):
    return jnp.mean(values, axis=-1, keepdims=True)


def normalize(values):
    centered = values - row_mean(values)
    rstd = lax.rsqrt(row_mean(centered * centered) + EPSILON)
    return centered * rstd, rstd


def normalize_back(grad, normed, rstd):
    return rstd * (grad - row_mean(grad) - normed * row_mean(grad * normed))


def flat(values):
    return values.reshape(-1, values.shape[-1])


def mod_rows(mod_ref, part, step, group):
    rows = [mod_ref[part, pl.ds(step * group + latent, 1), :] for latent in range(group)]
    return jnp.stack(rows)


def put_mod(ref, part, step, values):
    for latent in range(values.shape[0]):
        ref[part, pl.ds(step * values.shape[0] + latent, 1), :] = col_sum(values[latent])


def head_masks():
    lane = lax.broadcasted_iota(jnp.int32, (1, LANES), 1) // HEAD_DIM
    return [(lane == head).astype(F32).astype(BF16) for head in range(2)]


def assemble(scal_ref, base, piece_refs, rows_ref):
    rows_ref[...] = jnp.zeros_like(rows_ref)
    at = base
    for ref in piece_refs:
        slots, height = ref.shape[0], ref.shape[1]

        def one(slot, carry, ref=ref, at=at, height=height):
            start = pl.multiple_of(scal_ref[at + slot] * 8, 8)
            for tile in range(TILES):
                lanes = slice(tile * LANES, (tile + 1) * LANES)
                rows_ref[tile, pl.ds(start, height), :] += ref[slot, :, lanes].astype(F32)
            return carry

        lax.fori_loop(0, slots, one, 0)
        at += slots


def emit(scal_ref, base, out_refs, rows_ref):
    at = base
    for ref in out_refs:
        slots, height = ref.shape[0], ref.shape[1]

        def one(slot, carry, ref=ref, at=at, height=height):
            start = pl.multiple_of(scal_ref[at + slot] * 8, 8)
            for tile in range(TILES):
                lanes = slice(tile * LANES, (tile + 1) * LANES)
                ref[slot, :, lanes] = rows_ref[tile, pl.ds(start, height), :].astype(ref.dtype)
            return carry

        lax.fori_loop(0, slots, one, 0)
        at += slots


def lanes_of(tile, offset=0):
    return slice(offset + tile * LANES, offset + (tile + 1) * LANES)


def forward_kernel(n_pieces, scal_ref, cond_ref, x_ref, *refs):
    pieces = refs[:n_pieces]
    mod_ref, ada_ref, qkv_w_ref, proj_ref, bias_ref, qkv_ref, probs_ref, mixed_ref, branch_ref = refs[
        n_pieces : n_pieces + 9
    ]
    rows_ref, score_ref = refs[n_pieces + 9 :]
    step = pl.program_id(0)
    group, seq = x_ref.shape[0], x_ref.shape[1]

    @pl.when(step == 0)
    def _():
        assemble(scal_ref, 1, pieces, rows_ref)
        for tile in range(TILES):
            proj_ref[:, lanes_of(tile)] = rows_ref[tile, pl.ds(PROJ_AT, D), :].astype(BF16)
            bias_ref[:, lanes_of(tile)] = rows_ref[tile, pl.ds(B_ADA_AT, 8), :]
            for block in range(6):
                ada_ref[block, :, lanes_of(tile)] = rows_ref[
                    tile, pl.ds(ADA_AT + block, D, stride=6), :
                ].astype(BF16)
            for block in range(3):
                qkv_w_ref[:, lanes_of(tile, block * D)] = rows_ref[
                    tile, pl.ds(QKV_AT + block, D, stride=3), :
                ].astype(BF16)
        act = jax.nn.silu(cond_ref[...].astype(F32)).astype(BF16)
        for block in range(6):
            mod_ref[block] = mm(act, ada_ref[block]) + bias_ref[block : block + 1, :]

    @pl.when(step * group < scal_ref[0])
    def _():
        masks = head_masks()
        values = x_ref[...].astype(F32)
        normed, _ = normalize(values)
        shift, scale = [mod_rows(mod_ref, part, step, group) for part in range(2)]
        modulated = flat(normed * (1.0 + scale) + shift).astype(BF16)
        qkv = mm(modulated, qkv_w_ref[...])
        queries = (qkv[:, :D] + bias_ref[6:7, :]).astype(BF16)
        keys_all = qkv[:, D : 2 * D].astype(BF16)
        values_all = (qkv[:, 2 * D :] + bias_ref[7:8, :]).astype(BF16)
        for latent in range(group):
            tokens = slice(latent * seq, (latent + 1) * seq)
            qkv_ref[latent, :, :D] = queries[tokens]
            qkv_ref[latent, :, D : 2 * D] = keys_all[tokens]
            qkv_ref[latent, :, 2 * D :] = values_all[tokens]
            for head in range(HEADS):
                lanes = lanes_of(head // 2)
                own = queries[tokens, lanes] * (masks[head % 2] * FACTOR)
                score_ref[latent, head] = mm_nt(keys_all[tokens, lanes], own)
        for latent in range(group):
            tokens = slice(latent * seq, (latent + 1) * seq)
            values_t = values_all[tokens].T
            for head in range(HEADS):
                scores = score_ref[latent, head]
                expo = jnp.exp(scores - jnp.max(scores, axis=0, keepdims=True))
                probs_ref[latent, head] = (expo * (1.0 / col_sum(expo))).astype(BF16)
            for head in range(HEADS):
                rows = slice(head * HEAD_DIM, (head + 1) * HEAD_DIM)
                mixed_ref[latent, rows, :] = mm(values_t[rows, :], probs_ref[latent, head]).astype(BF16)
            branch_ref[latent] = mm_tn(mixed_ref[latent], proj_ref[...])


def mlp_kernel(n_pieces, n_out, scal_ref, mod_ref, proj_ref, x_ref, branch_ref, mixed_ref, cot_ref, *refs):
    pieces = refs[:n_pieces]
    outs = refs[n_pieces : n_pieces + 5 + n_out]
    out_ref, dx_ref, dmixed_ref, dmod_ref, dproj_ref = outs[:5]
    send_refs = outs[5:]
    rows_ref, fc1_ref, fc2_ref, bias_ref, act_ref, slope_ref, dfc1_ref, dfc2_ref, dbias_ref = refs[
        n_pieces + 5 + n_out :
    ]
    step = pl.program_id(0)
    last = pl.num_programs(0) - 1

    @pl.when(step == 0)
    def _():
        assemble(scal_ref, 1, pieces, rows_ref)
        for block in range(4):
            for tile in range(TILES):
                fc1_ref[:, lanes_of(tile, block * D)] = rows_ref[
                    tile, pl.ds(FC1_AT + block, D, stride=4), :
                ].astype(BF16)
                bias_ref[0:1, lanes_of(tile, block * D)] = rows_ref[tile, pl.ds(B_FC1_AT + block, 1), :]
        for tile in range(TILES):
            fc2_ref[:, lanes_of(tile)] = rows_ref[tile, pl.ds(FC2_AT, FF), :].astype(BF16)
            bias_ref[1:2, lanes_of(tile)] = rows_ref[tile, pl.ds(B_FC2_AT, 1), :]
            bias_ref[2:3, lanes_of(tile)] = rows_ref[tile, pl.ds(B_PROJ_AT, 1), :]
        dfc1_ref[...] = jnp.zeros_like(dfc1_ref)
        dfc2_ref[...] = jnp.zeros_like(dfc2_ref)
        dbias_ref[...] = jnp.zeros_like(dbias_ref)
        dproj_ref[...] = jnp.zeros_like(dproj_ref)
        dmod_ref[...] = jnp.zeros_like(dmod_ref)

    group, seq = x_ref.shape[0], x_ref.shape[1]

    @pl.when(step * group < scal_ref[0])
    def _():
        gate_one, shift, scale, gate_two = [mod_rows(mod_ref, 2 + part, step, group) for part in range(4)]
        slot = step * group + lax.broadcasted_iota(jnp.int32, (group, 1, 1), 0)
        live = (slot < scal_ref[0]).astype(F32)
        branch_one = branch_ref[...] + bias_ref[2:3, :D]
        middle = x_ref[...].astype(F32) + gate_one * branch_one
        normed, rstd = normalize(middle)
        modulated = flat(normed * (1.0 + scale) + shift).astype(BF16)
        chunk = CHUNK
        branch_two = jnp.zeros((group * seq, D), F32)
        for start in range(0, FF, chunk):
            part = slice(start, start + chunk)
            pre = mm(modulated, fc1_ref[:, part]) + bias_ref[0:1, part]
            square = pre * pre
            bend = jnp.tanh(pre * (GELU_A + (GELU_A * GELU_B) * square))
            half = 0.5 + 0.5 * bend
            act = (pre * half).astype(BF16)
            act_ref[:, part] = act
            slope_ref[:, part] = half + (pre * (0.5 - 0.5 * bend * bend)) * (
                GELU_A + (3.0 * GELU_A * GELU_B) * square
            )
            branch_two += mm(act, fc2_ref[part, :])
        branch_two = (branch_two + bias_ref[1:2, :D]).reshape(group, seq, D)
        out_ref[...] = (live * (middle + gate_two * branch_two)).astype(BF16)
        grad_out = live * cot_ref[...].astype(F32)
        put_mod(dmod_ref, 3, step, grad_out * branch_two)
        grad_two = flat(gate_two * grad_out).astype(BF16)
        dbias_ref[1:2, :D] += col_sum(grad_two.astype(F32))
        grad_two_t = grad_two.T
        modulated_t = modulated.T
        grad_mod = jnp.zeros((group * seq, D), F32)
        for start in range(0, FF, chunk):
            part = slice(start, start + chunk)
            du = (mm_nt(grad_two, fc2_ref[part, :]) * slope_ref[:, part]).astype(BF16)
            dbias_ref[0:1, part] += col_sum(du.astype(F32))
            dfc2_ref[:, part] += mm(grad_two_t, act_ref[:, part])
            dfc1_ref[:, part] += mm(modulated_t, du)
            grad_mod += mm_nt(du, fc1_ref[:, part])
        grad_mod = grad_mod.reshape(group, seq, D)
        put_mod(dmod_ref, 1, step, grad_mod)
        put_mod(dmod_ref, 2, step, grad_mod * normed)
        grad_middle = grad_out + normalize_back(grad_mod * (1.0 + scale), normed, rstd)
        dx_ref[...] = grad_middle
        put_mod(dmod_ref, 0, step, grad_middle * branch_one)
        grad_one = flat(gate_one * grad_middle).astype(BF16)
        dbias_ref[2:3, :D] += col_sum(grad_one.astype(F32))
        grad_mixed = mm_nt(grad_one, proj_ref[...]).astype(BF16)
        for latent in range(group):
            tokens = slice(latent * seq, (latent + 1) * seq)
            dproj_ref[...] += mm(mixed_ref[latent], grad_one[tokens])
            dmixed_ref[latent] = grad_mixed[tokens]

    @pl.when(step * group >= scal_ref[0])
    def _():
        out_ref[...] = jnp.zeros_like(out_ref)
        dx_ref[...] = jnp.zeros_like(dx_ref)
        dmixed_ref[...] = jnp.zeros_like(dmixed_ref)

    @pl.when(step == last)
    def _():
        for block in range(4):
            for tile in range(TILES):
                rows_ref[tile, pl.ds(FC1_AT + block, D, stride=4), :] = dfc1_ref[
                    :, lanes_of(tile, block * D)
                ]
                rows_ref[tile, pl.ds(B_FC1_AT + block, 1), :] = dbias_ref[0:1, lanes_of(tile, block * D)]
        for tile in range(TILES):
            rows_ref[tile, pl.ds(FC2_AT, FF), :] = dfc2_ref[lanes_of(tile), :].T
            rows_ref[tile, pl.ds(B_FC2_AT, 1), :] = dbias_ref[1:2, lanes_of(tile)]
            rows_ref[tile, pl.ds(B_PROJ_AT, 1), :] = dbias_ref[2:3, lanes_of(tile)]
        emit(scal_ref, 1 + sum(ref.shape[0] for ref in pieces), send_refs, rows_ref)


def attend_back_kernel(scal_ref, qkv_ref, probs_ref, dmixed_ref, dqkv_ref, dprobs_ref, low_ref, dq_t_ref):
    group, seq = qkv_ref.shape[0], qkv_ref.shape[1]

    @pl.when(pl.program_id(0) * group < scal_ref[0])
    def _():
        masks = head_masks()
        for latent in range(group):
            keys_t = qkv_ref[latent, :, D : 2 * D].T
            for head in range(HEADS):
                own = dmixed_ref[latent, :, lanes_of(head // 2)] * masks[head % 2]
                dprobs_ref[head] = mm_nt(qkv_ref[latent, :, lanes_of(head // 2, 2 * D)], own)
            for head in range(HEADS):
                probs, grad_probs = probs_ref[latent, head].astype(F32), dprobs_ref[head]
                low_ref[head] = (probs * (grad_probs - col_sum(probs * grad_probs))).astype(BF16)
            for pair in range(HEADS // 2):
                query = qkv_ref[latent, :, lanes_of(pair)]
                grad = dmixed_ref[latent, :, lanes_of(pair)]
                grad_key = jnp.zeros((seq, LANES), F32)
                grad_value = jnp.zeros((seq, LANES), F32)
                for half in range(2):
                    head = 2 * pair + half
                    rows = slice(head * HEAD_DIM, (head + 1) * HEAD_DIM)
                    grad_value += mm(probs_ref[latent, head], grad * masks[half])
                    grad_key += mm(low_ref[head], query * masks[half])
                    dq_t_ref[rows, :] = mm(keys_t[rows, :], low_ref[head])
                dqkv_ref[latent, :, lanes_of(pair, D)] = (grad_key * FACTOR).astype(BF16)
                dqkv_ref[latent, :, lanes_of(pair, 2 * D)] = grad_value.astype(BF16)
            dqkv_ref[latent, :, :D] = (dq_t_ref[...] * FACTOR).astype(BF16).T


def finish_kernel(
    n_out, base, scal_ref, mod_ref, qkv_w_ref, cond_ref, ada_ref, dmod_in_ref, dproj_ref,
    x_ref, dqkv_ref, dx_ref, *refs
):
    grad_x_ref, grad_cond_ref = refs[:2]
    send_refs = refs[2 : 2 + n_out]
    rows_ref, dqkv_w_ref, dmod_ref, dbias_ref = refs[2 + n_out :]
    step = pl.program_id(0)
    last = pl.num_programs(0) - 1
    group, seq = x_ref.shape[0], x_ref.shape[1]

    @pl.when(step == 0)
    def _():
        dqkv_w_ref[...] = jnp.zeros_like(dqkv_w_ref)
        dmod_ref[...] = jnp.zeros_like(dmod_ref)
        dbias_ref[...] = jnp.zeros_like(dbias_ref)

    @pl.when(step * group < scal_ref[0])
    def _():
        shift, scale = [mod_rows(mod_ref, part, step, group) for part in range(2)]
        normed, rstd = normalize(x_ref[...].astype(F32))
        modulated = flat(normed * (1.0 + scale) + shift).astype(BF16)
        grad_qkv = flat(dqkv_ref[...])
        dbias_ref[0:1, :] += col_sum(grad_qkv.astype(F32))
        dqkv_w_ref[...] += mm(modulated.T, grad_qkv)
        grad_mod = mm_nt(grad_qkv, qkv_w_ref[...]).reshape(group, seq, D)
        put_mod(dmod_ref, 0, step, grad_mod)
        put_mod(dmod_ref, 1, step, grad_mod * normed)
        grad_x_ref[...] = dx_ref[...] + normalize_back(grad_mod * (1.0 + scale), normed, rstd)

    @pl.when(step * group >= scal_ref[0])
    def _():
        grad_x_ref[...] = jnp.zeros_like(grad_x_ref)

    @pl.when(step == last)
    def _():
        cond = cond_ref[...].astype(F32)
        gate = jax.nn.sigmoid(cond)
        act = (cond * gate).astype(BF16)
        grad_act = jnp.zeros_like(cond)
        for block in range(6):
            grad = (dmod_ref[block] if block < 2 else dmod_in_ref[block - 2]).astype(BF16)
            grad_act += mm_nt(grad, ada_ref[block])
            weight = mm_tn(act, grad)
            bias = col_sum(grad.astype(F32))
            for tile in range(TILES):
                rows_ref[tile, pl.ds(ADA_AT + block, D, stride=6), :] = weight[:, lanes_of(tile)]
                rows_ref[tile, pl.ds(B_ADA_AT + block, 1), :] = bias[:, lanes_of(tile)]
        grad_cond_ref[...] = grad_act * (gate * (1.0 + cond * (1.0 - gate)))
        for tile in range(TILES):
            for block in range(3):
                rows_ref[tile, pl.ds(QKV_AT + block, D, stride=3), :] = dqkv_w_ref[
                    :, lanes_of(tile, block * D)
                ]
            rows_ref[tile, pl.ds(PROJ_AT, D), :] = dproj_ref[:, lanes_of(tile)]
            rows_ref[tile, pl.ds(B_QV_AT, 1), :] = dbias_ref[0:1, lanes_of(tile)]
            rows_ref[tile, pl.ds(B_QV_AT + 1, 1), :] = dbias_ref[0:1, lanes_of(tile, 2 * D)]
        emit(scal_ref, base, send_refs, rows_ref)


class Direct:
    def __init__(self, count, me):
        self.count, self.me = count, me
        self.gathered = self.sent = [jnp.int32(index) for index in range(count)]
        self.slots = [(count, F32)]

    def gather(self, piece):
        return [lax.all_gather(piece, AXIS, axis=0)]

    def pass_on(self, held):
        return held

    def begin(self, parts):
        return parts

    middle = send = begin

    def end(self, parts):
        return lax.psum_scatter(parts[0], AXIS, scatter_dimension=0)


class Stages:
    def __init__(self, count, me):
        self.me = me
        core, x, y, z = me % 2, me // 2 % 2, me // 4 % 2, me // 8

        def device(dz, dy, dx, dc):
            return (((z + dz) % 4 * 2 + (y + dy) % 2) * 2 + (x + dx) % 2) * 2 + (core + dc) % 2

        gathered = []
        for dc in range(2):
            gathered += [device(-k, 0, 0, dc) for k in (0, 1, 2, 3)]
            gathered += [device(-k, 0, 1, dc) for k in (0, 1)]
            gathered += [device(-k, 1, 0, dc) for k in (2, 3)]
            gathered += [device(-k, 1, dx, dc) for dx in (0, 1) for k in (0, 1)]
            gathered += [device(-k, dy, 1, dc) for dy in (0, 1) for k in (2, 3)]
        self.gathered = gathered
        sent = []
        for dc in (1, 0):
            sent += [device(k, dy, dx, dc) for dx in (0, 1) for k in (0, 1) for dy in (0, 1)]
            sent += [device(k, dy, dx, dc) for dy in (0, 1) for k in (2, 3) for dx in (0, 1)]
        self.sent = sent
        self.slots = [(8, BF16), (8, BF16), (8, F32), (8, F32)]

    def shift(self, values, dz=0, dy=0, dx=0, dc=0):
        pairs = []
        for source in range(32):
            core, x, y, z = source % 2, source // 2 % 2, source // 4 % 2, source // 8
            target = (((z + dz) % 4 * 2 + (y + dy) % 2) * 2 + (x + dx) % 2) * 2 + (core + dc) % 2
            pairs.append((source, target))
        return lax.ppermute(values, AXIS, pairs)

    def gather(self, piece):
        own = jnp.stack([piece] + [self.shift(piece, dz=k) for k in (1, 2, 3)])
        first, second = own[:2], own[2:]
        by_x = self.shift(first, dx=1)
        by_y = self.shift(second, dy=1)
        by_xy = self.shift(jnp.concatenate([first, by_x]), dy=1)
        by_yx = self.shift(jnp.concatenate([second, by_y]), dx=1)
        return [own, by_x, by_y, by_xy, by_yx]

    def pass_on(self, held):
        return held + [self.shift(array, dc=1) for array in held]

    def begin(self, parts):
        send_a, send_b, keep_a, keep_b = parts
        return self.shift(send_a, dc=1), self.shift(send_b, dc=1), keep_a, keep_b

    def middle(self, state):
        got_a, got_b, keep_a, keep_b = state
        shape = keep_a.shape[1:]
        sum_a = (keep_a + got_a.astype(F32)).reshape((2, 4) + shape)
        sum_b = (keep_b + got_b.astype(F32)).reshape((2, 4) + shape)
        return sum_a[0], sum_b[0], sum_a[1].astype(BF16), sum_b[1].astype(BF16)

    def send(self, state):
        sum_a, sum_b, out_a, out_b = state
        return sum_a, sum_b, self.shift(out_a, dx=1), self.shift(out_b, dy=1)

    def end(self, state):
        def swap(values, **how):
            return self.shift(values.astype(BF16), **how).astype(F32)

        sum_a, sum_b, got_a, got_b = state
        shape = sum_a.shape[1:]
        sum_a = (sum_a + got_a.astype(F32)).reshape((2, 2) + shape)
        sum_b = (sum_b + got_b.astype(F32)).reshape((2, 2) + shape)
        sum_a = sum_a[:, 0] + swap(sum_a[:, 1], dy=1)
        sum_b = sum_b[:, 0] + swap(sum_b[:, 1], dx=1)
        return (
            sum_a[0] + swap(sum_a[1], dz=1) + swap(sum_b[0], dz=2) + swap(sum_b[1], dz=3)
        )


def to_piece(share, rows, me):
    size = share.shape[0]
    flat = jnp.zeros((rows * D,), share.dtype)
    return lax.dynamic_update_slice(flat, share, (size * me % GROUP,)).reshape(rows, D)


def from_piece(piece, size, me):
    return lax.dynamic_slice(piece.reshape(-1), (size * me % GROUP,), (size,))


def whole(shape=None):
    return pl.BlockSpec(memory_space=pltpu.VMEM)


def by_latent(*shape):
    zeros = (0,) * len(shape)
    return pl.BlockSpec((PER_STEP,) + shape, lambda step, scal: (step,) + zeros)


def call(kernel, count, in_specs, out_specs, out_shape, scratch, args, flops):
    return pl.pallas_call(
        kernel,
        grid_spec=pltpu.PrefetchScalarGridSpec(
            num_scalar_prefetch=1,
            grid=(count,),
            in_specs=in_specs,
            out_specs=out_specs,
            scratch_shapes=scratch,
        ),
        out_shape=out_shape,
        compiler_params=pltpu.CompilerParams(
            vmem_limit_bytes=60 * 2**20, dimension_semantics=("arbitrary",)
        ),
        cost_estimate=pl.CostEstimate(flops=flops, bytes_accessed=20 * 2**20, transcendentals=0),
    )(*args)


def solution(mesh):
    devices = mesh.shape[AXIS]

    def body(latents, condition, attn_params, mlp_params, counts, cotangent):
        count, seq = latents.shape[0], latents.shape[1]
        me = lax.axis_index(AXIS)
        plan = (Stages if devices == 32 else Direct)(devices, me)
        attn_size, mlp_size = attn_params.shape[0], mlp_params.shape[0]
        attn_height = piece_rows(attn_size, devices)
        mlp_height = piece_rows(mlp_size, devices)

        def scalars(size):
            ids = jnp.stack(plan.gathered + plan.sent)
            return jnp.concatenate([counts.astype(jnp.int32), size * ids // GROUP]).astype(jnp.int32)

        attn_scal, mlp_scal = scalars(attn_size), scalars(mlp_size)
        attn_pieces = plan.pass_on(plan.gather(to_piece(attn_params, attn_height, me)))
        mlp_pieces = plan.gather(to_piece(mlp_params, mlp_height, me))

        def struct(shape, kind):
            return jax.ShapeDtypeStruct(shape, kind)

        n_pieces = len(attn_pieces)
        n_out = len(plan.slots)
        steps = count // PER_STEP
        mod, ada, qkv_w, proj, _, qkv, probs, mixed, branch = call(
            lambda *refs: forward_kernel(n_pieces, *refs),
            steps,
            [whole(), by_latent(seq, D)] + [whole()] * n_pieces,
            [whole()] * 5
            + [
                by_latent(seq, 3 * D),
                by_latent(HEADS, seq, seq),
                by_latent(D, seq),
                by_latent(seq, D),
            ],
            [
                struct((6, count, D), F32),
                struct((6, D, D), BF16),
                struct((D, 3 * D), BF16),
                struct((D, D), BF16),
                struct((8, D), F32),
                struct((count, seq, 3 * D), BF16),
                struct((count, HEADS, seq, seq), BF16),
                struct((count, D, seq), BF16),
                struct((count, seq, D), F32),
            ],
            [
                pltpu.VMEM((TILES, ATTN_ROWS + attn_height, LANES), F32),
                pltpu.VMEM((PER_STEP, HEADS, seq, seq), F32),
            ],
            [attn_scal, condition, latents] + attn_pieces,
            15 * 10**9,
        )
        mlp_pieces, mod = lax.optimization_barrier((mlp_pieces, mod))
        mlp_pieces = plan.pass_on(mlp_pieces)
        results = call(
            lambda *refs: mlp_kernel(n_pieces, n_out, *refs),
            steps,
            [whole(), whole(), by_latent(seq, D), by_latent(seq, D), by_latent(D, seq), by_latent(seq, D)]
            + [whole()] * n_pieces,
            [by_latent(seq, D), by_latent(seq, D), by_latent(seq, D), whole(), whole()]
            + [whole()] * n_out,
            [
                struct((count, seq, D), BF16),
                struct((count, seq, D), F32),
                struct((count, seq, D), BF16),
                struct((4, count, D), F32),
                struct((D, D), F32),
            ]
            + [struct((slots, mlp_height, D), kind) for slots, kind in plan.slots],
            [
                pltpu.VMEM((TILES, MLP_ROWS + 2 + mlp_height, LANES), F32),
                pltpu.VMEM((D, FF), BF16),
                pltpu.VMEM((FF, D), BF16),
                pltpu.VMEM((8, FF), F32),
                pltpu.VMEM((PER_STEP * seq, FF), BF16),
                pltpu.VMEM((PER_STEP * seq, FF), F32),
                pltpu.VMEM((D, FF), F32),
                pltpu.VMEM((D, FF), F32),
                pltpu.VMEM((8, FF), F32),
            ],
            [mlp_scal, mod, proj, latents, branch, mixed, cotangent] + mlp_pieces,
            30 * 10**9,
        )
        output, grad_middle, grad_mixed, dmod, dproj = results[:5]
        sums = plan.begin(results[5:])
        grad_qkv, = call(
            attend_back_kernel,
            steps,
            [by_latent(seq, 3 * D), by_latent(HEADS, seq, seq), by_latent(seq, D)],
            [by_latent(seq, 3 * D)],
            [struct((count, seq, 3 * D), BF16)],
            [
                pltpu.VMEM((HEADS, seq, seq), F32),
                pltpu.VMEM((HEADS, seq, seq), BF16),
                pltpu.VMEM((D, seq), F32),
            ],
            [attn_scal, qkv, probs, grad_mixed],
            13 * 10**9,
        )
        sums, grad_qkv = lax.optimization_barrier((sums, grad_qkv))
        sums = plan.middle(sums)
        sums, grad_qkv = lax.optimization_barrier((sums, grad_qkv))
        sums = plan.send(sums)
        results = call(
            lambda *refs: finish_kernel(n_out, 1 + devices, *refs),
            steps,
            [whole()] * 6 + [by_latent(seq, D), by_latent(seq, 3 * D), by_latent(seq, D)],
            [by_latent(seq, D), whole()] + [whole()] * n_out,
            [struct((count, seq, D), F32), struct((count, D), F32)]
            + [struct((slots, attn_height, D), kind) for slots, kind in plan.slots],
            [
                pltpu.VMEM((TILES, ATTN_ROWS + attn_height, LANES), F32),
                pltpu.VMEM((D, 3 * D), F32),
                pltpu.VMEM((2, count, D), F32),
                pltpu.VMEM((8, 3 * D), F32),
            ],
            [attn_scal, mod, qkv_w, condition, ada, dmod, dproj, latents, grad_qkv, grad_middle],
            15 * 10**9,
        )
        grad_latents, grad_condition = results[:2]
        grad_mlp = plan.end(sums)
        grad_attn = plan.end(plan.send(plan.middle(plan.begin(results[2:]))))
        return (
            output,
            grad_latents,
            grad_condition,
            from_piece(grad_attn, attn_size, me),
            from_piece(grad_mlp, mlp_size, me),
        )

    in_specs = (
        P(AXIS, None, None),
        P(AXIS, None),
        P(AXIS),
        P(AXIS),
        P(AXIS),
        P(AXIS, None, None),
    )
    out_specs = (
        P(AXIS, None, None),
        P(AXIS, None, None),
        P(AXIS, None),
        P(AXIS),
        P(AXIS),
    )
    return jax.shard_map(body, mesh=mesh, in_specs=in_specs, out_specs=out_specs, check_vma=False)
```

```python
import jax
import jax.numpy as jnp
from jax import lax
from jax.experimental import pallas as pl
from jax.experimental.pallas import tpu as pltpu
from jax.sharding import PartitionSpec as P

D = 384
HEADS = 6
HEAD_DIM = 64
FF = 1536
EPSILON = 1e-06
AXIS = "fsdp"
LANES = 128
TILES = D // LANES
GROUP = 8 * D
FACTOR = HEAD_DIM ** (-0.5)
GELU_A = 0.7978845608028654
GELU_B = 0.044715
CHUNK = 1536
FORWARD_STEP = 2
MLP_STEP = 2
ATTEND_STEP = 2
FINISH_STEP = 2

ADA_AT = 0
QKV_AT = 6 * D
PROJ_AT = 9 * D
B_ADA_AT = 10 * D
B_QV_AT = 10 * D + 6
ATTN_ROWS = 10 * D + 8
FC1_AT = 0
FC2_AT = FF
B_FC1_AT = 2 * FF
B_FC2_AT = 2 * FF + 4
B_PROJ_AT = 2 * FF + 5
MLP_ROWS = 2 * FF + 6

F32 = jnp.float32
BF16 = jnp.bfloat16


def round_up(value, unit):
    return -(-value // unit) * unit


def piece_rows(share, count):
    lead = max((share * index) % GROUP for index in range(count))
    return round_up(-(-(share + lead) // D), 16)


def mm(left, right):
    return jnp.dot(left, right, preferred_element_type=F32)


def mm_nt(left, right):
    return lax.dot_general(left, right, (((1,), (1,)), ((), ())), preferred_element_type=F32)


def mm_tn(left, right):
    return lax.dot_general(left, right, (((0,), (0,)), ((), ())), preferred_element_type=F32)


def col_sum(values):
    return jnp.sum(values, axis=0, keepdims=True)


def row_mean(values):
    return jnp.mean(values, axis=-1, keepdims=True)


def normalize(values):
    centered = values - row_mean(values)
    rstd = lax.rsqrt(row_mean(centered * centered) + EPSILON)
    return centered * rstd, rstd


def normalize_back(grad, normed, rstd):
    return rstd * (grad - row_mean(grad) - normed * row_mean(grad * normed))


def flat(values):
    return values.reshape(-1, values.shape[-1])


def mod_rows(mod_ref, part, step, group):
    rows = [mod_ref[part, pl.ds(step * group + latent, 1), :] for latent in range(group)]
    return jnp.stack(rows)


def put_mod(ref, part, step, values):
    for latent in range(values.shape[0]):
        ref[part, pl.ds(step * values.shape[0] + latent, 1), :] = col_sum(values[latent])


def head_masks():
    lane = lax.broadcasted_iota(jnp.int32, (1, LANES), 1) // HEAD_DIM
    return [(lane == head).astype(F32).astype(BF16) for head in range(2)]


def assemble(scal_ref, base, piece_refs, rows_ref):
    rows_ref[...] = jnp.zeros_like(rows_ref)
    at = base
    for ref in piece_refs:
        slots, height = ref.shape[0], ref.shape[1]

        def one(slot, carry, ref=ref, at=at, height=height):
            start = pl.multiple_of(scal_ref[at + slot] * 8, 8)
            for tile in range(TILES):
                lanes = slice(tile * LANES, (tile + 1) * LANES)
                rows_ref[tile, pl.ds(start, height), :] += ref[slot, :, lanes].astype(F32)
            return carry

        lax.fori_loop(0, slots, one, 0)
        at += slots


def emit(scal_ref, base, out_refs, rows_ref):
    at = base
    for ref in out_refs:
        slots, height = ref.shape[0], ref.shape[1]

        def one(slot, carry, ref=ref, at=at, height=height):
            start = pl.multiple_of(scal_ref[at + slot] * 8, 8)
            for tile in range(TILES):
                lanes = slice(tile * LANES, (tile + 1) * LANES)
                ref[slot, :, lanes] = rows_ref[tile, pl.ds(start, height), :].astype(ref.dtype)
            return carry

        lax.fori_loop(0, slots, one, 0)
        at += slots


def lanes_of(tile, offset=0):
    return slice(offset + tile * LANES, offset + (tile + 1) * LANES)


def forward_kernel(n_pieces, scal_ref, cond_ref, x_ref, *refs):
    pieces = refs[:n_pieces]
    mod_ref, ada_ref, qkv_w_ref, proj_ref, bias_ref, qkv_ref, probs_ref, mixed_ref, branch_ref = refs[
        n_pieces : n_pieces + 9
    ]
    rows_ref, score_ref = refs[n_pieces + 9 :]
    step = pl.program_id(0)
    group, seq = x_ref.shape[0], x_ref.shape[1]

    @pl.when(step == 0)
    def _():
        assemble(scal_ref, 1, pieces, rows_ref)
        for tile in range(TILES):
            proj_ref[:, lanes_of(tile)] = rows_ref[tile, pl.ds(PROJ_AT, D), :].astype(BF16)
            bias_ref[:, lanes_of(tile)] = rows_ref[tile, pl.ds(B_ADA_AT, 8), :]
            for block in range(6):
                ada_ref[block, :, lanes_of(tile)] = rows_ref[
                    tile, pl.ds(ADA_AT + block, D, stride=6), :
                ].astype(BF16)
            for block in range(3):
                qkv_w_ref[:, lanes_of(tile, block * D)] = rows_ref[
                    tile, pl.ds(QKV_AT + block, D, stride=3), :
                ].astype(BF16)
        act = jax.nn.silu(cond_ref[...].astype(F32)).astype(BF16)
        for block in range(6):
            mod_ref[block] = mm(act, ada_ref[block]) + bias_ref[block : block + 1, :]

    @pl.when(step * group < scal_ref[0])
    def _():
        masks = head_masks()
        values = x_ref[...].astype(F32)
        normed, _ = normalize(values)
        shift, scale = [mod_rows(mod_ref, part, step, group) for part in range(2)]
        modulated = flat(normed * (1.0 + scale) + shift).astype(BF16)
        qkv = mm(modulated, qkv_w_ref[...])
        queries = (qkv[:, :D] + bias_ref[6:7, :]).astype(BF16)
        keys_all = qkv[:, D : 2 * D].astype(BF16)
        values_all = (qkv[:, 2 * D :] + bias_ref[7:8, :]).astype(BF16)
        for latent in range(group):
            tokens = slice(latent * seq, (latent + 1) * seq)
            qkv_ref[latent, :, :D] = queries[tokens]
            qkv_ref[latent, :, D : 2 * D] = keys_all[tokens]
            qkv_ref[latent, :, 2 * D :] = values_all[tokens]
            for head in range(HEADS):
                lanes = lanes_of(head // 2)
                own = queries[tokens, lanes] * (masks[head % 2] * FACTOR)
                score_ref[latent, head] = mm_nt(keys_all[tokens, lanes], own)
        for latent in range(group):
            tokens = slice(latent * seq, (latent + 1) * seq)
            values_t = values_all[tokens].T
            for head in range(HEADS):
                scores = score_ref[latent, head]
                expo = jnp.exp(scores - jnp.max(scores, axis=0, keepdims=True))
                probs_ref[latent, head] = (expo * (1.0 / col_sum(expo))).astype(BF16)
            for head in range(HEADS):
                rows = slice(head * HEAD_DIM, (head + 1) * HEAD_DIM)
                mixed_ref[latent, rows, :] = mm(values_t[rows, :], probs_ref[latent, head]).astype(BF16)
            branch_ref[latent] = mm_tn(mixed_ref[latent], proj_ref[...])


def mlp_kernel(n_pieces, n_out, scal_ref, mod_ref, proj_ref, x_ref, branch_ref, mixed_ref, cot_ref, *refs):
    pieces = refs[:n_pieces]
    outs = refs[n_pieces : n_pieces + 5 + n_out]
    out_ref, dx_ref, dmixed_ref, dmod_ref, dproj_ref = outs[:5]
    send_refs = outs[5:]
    rows_ref, fc1_ref, fc2_ref, bias_ref, act_ref, slope_ref, du_ref, dfc1_ref, dfc2_ref, dbias_ref = refs[
        n_pieces + 5 + n_out :
    ]
    step = pl.program_id(0)
    last = pl.num_programs(0) - 1

    @pl.when(step == 0)
    def _():
        assemble(scal_ref, 1, pieces, rows_ref)
        for block in range(4):
            for tile in range(TILES):
                fc1_ref[:, lanes_of(tile, block * D)] = rows_ref[
                    tile, pl.ds(FC1_AT + block, D, stride=4), :
                ].astype(BF16)
                bias_ref[0:1, lanes_of(tile, block * D)] = rows_ref[tile, pl.ds(B_FC1_AT + block, 1), :]
        for tile in range(TILES):
            fc2_ref[:, lanes_of(tile)] = rows_ref[tile, pl.ds(FC2_AT, FF), :].astype(BF16)
            bias_ref[1:2, lanes_of(tile)] = rows_ref[tile, pl.ds(B_FC2_AT, 1), :]
            bias_ref[2:3, lanes_of(tile)] = rows_ref[tile, pl.ds(B_PROJ_AT, 1), :]
        dfc1_ref[...] = jnp.zeros_like(dfc1_ref)
        dfc2_ref[...] = jnp.zeros_like(dfc2_ref)
        dbias_ref[...] = jnp.zeros_like(dbias_ref)
        dproj_ref[...] = jnp.zeros_like(dproj_ref)
        dmod_ref[...] = jnp.zeros_like(dmod_ref)

    group, seq = x_ref.shape[0], x_ref.shape[1]

    @pl.when(step * group < scal_ref[0])
    def _():
        gate_one, shift, scale, gate_two = [mod_rows(mod_ref, 2 + part, step, group) for part in range(4)]
        slot = step * group + lax.broadcasted_iota(jnp.int32, (group, 1, 1), 0)
        live = (slot < scal_ref[0]).astype(F32)
        branch_one = branch_ref[...] + bias_ref[2:3, :D]
        middle = x_ref[...].astype(F32) + gate_one * branch_one
        normed, rstd = normalize(middle)
        modulated = flat(normed * (1.0 + scale) + shift).astype(BF16)
        chunk = CHUNK
        for start in range(0, FF, chunk):
            part = slice(start, start + chunk)
            pre = mm(modulated, fc1_ref[:, part]) + bias_ref[0:1, part]
            square = pre * pre
            bend = jnp.tanh(pre * (GELU_A + (GELU_A * GELU_B) * square))
            half = 0.5 + 0.5 * bend
            act = (pre * half).astype(BF16)
            act_ref[:, part] = act
            slope_ref[:, part] = half + (pre * (0.5 - 0.5 * bend * bend)) * (
                GELU_A + (3.0 * GELU_A * GELU_B) * square
            )
        branch_two = mm(act_ref[...], fc2_ref[...])
        branch_two = (branch_two + bias_ref[1:2, :D]).reshape(group, seq, D)
        out_ref[...] = (live * (middle + gate_two * branch_two)).astype(BF16)
        grad_out = live * cot_ref[...].astype(F32)
        put_mod(dmod_ref, 3, step, grad_out * branch_two)
        grad_two = flat(gate_two * grad_out).astype(BF16)
        dbias_ref[1:2, :D] += col_sum(grad_two.astype(F32))
        grad_two_t = grad_two.T
        modulated_t = modulated.T
        for start in range(0, FF, chunk):
            part = slice(start, start + chunk)
            du = (mm_nt(grad_two, fc2_ref[part, :]) * slope_ref[:, part]).astype(BF16)
            dbias_ref[0:1, part] += col_sum(du.astype(F32))
            du_ref[:, part] = du
        grad_mod = mm_nt(du_ref[...], fc1_ref[...]).reshape(group, seq, D)
        dfc2_ref[...] += mm(grad_two_t, act_ref[...])
        dfc1_ref[...] += mm(modulated_t, du_ref[...])
        put_mod(dmod_ref, 1, step, grad_mod)
        put_mod(dmod_ref, 2, step, grad_mod * normed)
        grad_middle = grad_out + normalize_back(grad_mod * (1.0 + scale), normed, rstd)
        dx_ref[...] = grad_middle
        put_mod(dmod_ref, 0, step, grad_middle * branch_one)
        grad_one = flat(gate_one * grad_middle).astype(BF16)
        dbias_ref[2:3, :D] += col_sum(grad_one.astype(F32))
        grad_mixed = mm_nt(grad_one, proj_ref[...]).astype(BF16)
        for latent in range(group):
            tokens = slice(latent * seq, (latent + 1) * seq)
            dproj_ref[...] += mm(mixed_ref[latent], grad_one[tokens])
            dmixed_ref[latent] = grad_mixed[tokens]

    @pl.when(step * group >= scal_ref[0])
    def _():
        out_ref[...] = jnp.zeros_like(out_ref)
        dx_ref[...] = jnp.zeros_like(dx_ref)
        dmixed_ref[...] = jnp.zeros_like(dmixed_ref)

    @pl.when(step == last)
    def _():
        for block in range(4):
            for tile in range(TILES):
                rows_ref[tile, pl.ds(FC1_AT + block, D, stride=4), :] = dfc1_ref[
                    :, lanes_of(tile, block * D)
                ]
                rows_ref[tile, pl.ds(B_FC1_AT + block, 1), :] = dbias_ref[0:1, lanes_of(tile, block * D)]
        for tile in range(TILES):
            rows_ref[tile, pl.ds(FC2_AT, FF), :] = dfc2_ref[lanes_of(tile), :].T
            rows_ref[tile, pl.ds(B_FC2_AT, 1), :] = dbias_ref[1:2, lanes_of(tile)]
            rows_ref[tile, pl.ds(B_PROJ_AT, 1), :] = dbias_ref[2:3, lanes_of(tile)]
        emit(scal_ref, 1 + sum(ref.shape[0] for ref in pieces), send_refs, rows_ref)


def attend_back_kernel(scal_ref, qkv_ref, probs_ref, dmixed_ref, dqkv_ref, dprobs_ref, low_ref, dq_t_ref):
    group, seq = qkv_ref.shape[0], qkv_ref.shape[1]

    @pl.when(pl.program_id(0) * group < scal_ref[0])
    def _():
        masks = head_masks()
        for latent in range(group):
            keys_t = qkv_ref[latent, :, D : 2 * D].T
            for head in range(HEADS):
                own = dmixed_ref[latent, :, lanes_of(head // 2)] * masks[head % 2]
                dprobs_ref[head] = mm_nt(qkv_ref[latent, :, lanes_of(head // 2, 2 * D)], own)
            for head in range(HEADS):
                probs, grad_probs = probs_ref[latent, head].astype(F32), dprobs_ref[head]
                low_ref[head] = (probs * (grad_probs - col_sum(probs * grad_probs))).astype(BF16)
            for pair in range(HEADS // 2):
                query = qkv_ref[latent, :, lanes_of(pair)]
                grad = dmixed_ref[latent, :, lanes_of(pair)]
                grad_key = jnp.zeros((seq, LANES), F32)
                grad_value = jnp.zeros((seq, LANES), F32)
                for half in range(2):
                    head = 2 * pair + half
                    rows = slice(head * HEAD_DIM, (head + 1) * HEAD_DIM)
                    grad_value += mm(probs_ref[latent, head], grad * masks[half])
                    grad_key += mm(low_ref[head], query * masks[half])
                    dq_t_ref[rows, :] = mm(keys_t[rows, :], low_ref[head])
                dqkv_ref[latent, :, lanes_of(pair, D)] = (grad_key * FACTOR).astype(BF16)
                dqkv_ref[latent, :, lanes_of(pair, 2 * D)] = grad_value.astype(BF16)
            dqkv_ref[latent, :, :D] = (dq_t_ref[...] * FACTOR).astype(BF16).T


def finish_kernel(
    n_out, base, scal_ref, mod_ref, qkv_w_ref, cond_ref, ada_ref, dmod_in_ref, dproj_ref,
    x_ref, dqkv_ref, dx_ref, *refs
):
    grad_x_ref, grad_cond_ref = refs[:2]
    send_refs = refs[2 : 2 + n_out]
    rows_ref, dqkv_w_ref, dmod_ref, dbias_ref = refs[2 + n_out :]
    step = pl.program_id(0)
    last = pl.num_programs(0) - 1
    group, seq = x_ref.shape[0], x_ref.shape[1]

    @pl.when(step == 0)
    def _():
        dqkv_w_ref[...] = jnp.zeros_like(dqkv_w_ref)
        dmod_ref[...] = jnp.zeros_like(dmod_ref)
        dbias_ref[...] = jnp.zeros_like(dbias_ref)

    @pl.when(step * group < scal_ref[0])
    def _():
        shift, scale = [mod_rows(mod_ref, part, step, group) for part in range(2)]
        normed, rstd = normalize(x_ref[...].astype(F32))
        modulated = flat(normed * (1.0 + scale) + shift).astype(BF16)
        grad_qkv = flat(dqkv_ref[...])
        dbias_ref[0:1, :] += col_sum(grad_qkv.astype(F32))
        dqkv_w_ref[...] += mm(modulated.T, grad_qkv)
        grad_mod = mm_nt(grad_qkv, qkv_w_ref[...]).reshape(group, seq, D)
        put_mod(dmod_ref, 0, step, grad_mod)
        put_mod(dmod_ref, 1, step, grad_mod * normed)
        grad_x_ref[...] = dx_ref[...] + normalize_back(grad_mod * (1.0 + scale), normed, rstd)

    @pl.when(step * group >= scal_ref[0])
    def _():
        grad_x_ref[...] = jnp.zeros_like(grad_x_ref)

    @pl.when(step == last)
    def _():
        cond = cond_ref[...].astype(F32)
        gate = jax.nn.sigmoid(cond)
        act = (cond * gate).astype(BF16)
        grad_act = jnp.zeros_like(cond)
        for block in range(6):
            grad = (dmod_ref[block] if block < 2 else dmod_in_ref[block - 2]).astype(BF16)
            grad_act += mm_nt(grad, ada_ref[block])
            weight = mm_tn(act, grad)
            bias = col_sum(grad.astype(F32))
            for tile in range(TILES):
                rows_ref[tile, pl.ds(ADA_AT + block, D, stride=6), :] = weight[:, lanes_of(tile)]
                rows_ref[tile, pl.ds(B_ADA_AT + block, 1), :] = bias[:, lanes_of(tile)]
        grad_cond_ref[...] = grad_act * (gate * (1.0 + cond * (1.0 - gate)))
        for tile in range(TILES):
            for block in range(3):
                rows_ref[tile, pl.ds(QKV_AT + block, D, stride=3), :] = dqkv_w_ref[
                    :, lanes_of(tile, block * D)
                ]
            rows_ref[tile, pl.ds(PROJ_AT, D), :] = dproj_ref[:, lanes_of(tile)]
            rows_ref[tile, pl.ds(B_QV_AT, 1), :] = dbias_ref[0:1, lanes_of(tile)]
            rows_ref[tile, pl.ds(B_QV_AT + 1, 1), :] = dbias_ref[0:1, lanes_of(tile, 2 * D)]
        emit(scal_ref, base, send_refs, rows_ref)


class Direct:
    def __init__(self, count, me):
        self.count, self.me = count, me
        self.gathered = self.sent = [jnp.int32(index) for index in range(count)]
        self.slots = [(count, F32)]

    def start(self, piece):
        return piece

    def gather(self, piece):
        return [lax.all_gather(piece, AXIS, axis=0)]

    def pass_on(self, held):
        return held

    def join(self, own, others):
        return own

    def begin(self, parts):
        return parts

    middle = send = begin

    def end(self, parts):
        return lax.psum_scatter(parts[0], AXIS, scatter_dimension=0)


class Stages:
    def __init__(self, count, me):
        self.me = me
        core, x, y, z = me % 2, me // 2 % 2, me // 4 % 2, me // 8

        def device(dz, dy, dx, dc):
            return (((z + dz) % 4 * 2 + (y + dy) % 2) * 2 + (x + dx) % 2) * 2 + (core + dc) % 2

        self.order(device)

    def order(self, device):
        gathered = []
        for dc in range(2):
            gathered += [device(-k, 0, 0, dc) for k in (0, 1, 2, 3)]
            gathered += [device(-k, 0, 1, dc) for k in (0, 1)]
            gathered += [device(-k, 1, 0, dc) for k in (2, 3)]
            gathered += [device(-k, 1, dx, dc) for dx in (0, 1) for k in (0, 1)]
            gathered += [device(-k, dy, 1, dc) for dy in (0, 1) for k in (2, 3)]
        self.gathered = gathered
        sent = []
        for dc in (1, 0):
            sent += [device(k, dy, dx, dc) for dx in (0, 1) for k in (0, 1) for dy in (0, 1)]
            sent += [device(k, dy, dx, dc) for dy in (0, 1) for k in (2, 3) for dx in (0, 1)]
        self.sent = sent
        self.slots = [(8, BF16), (8, BF16), (8, F32), (8, F32)]

    def shift(self, values, dz=0, dy=0, dx=0, dc=0):
        pairs = []
        for source in range(32):
            core, x, y, z = source % 2, source // 2 % 2, source // 4 % 2, source // 8
            target = (((z + dz) % 4 * 2 + (y + dy) % 2) * 2 + (x + dx) % 2) * 2 + (core + dc) % 2
            pairs.append((source, target))
        return lax.ppermute(values, AXIS, pairs)

    def start(self, piece):
        return jnp.stack([piece] + [self.shift(piece, dz=k) for k in (1, 2, 3)])

    def gather(self, own):
        first, second = own[:2], own[2:]
        by_x = self.shift(first, dx=1)
        by_y = self.shift(second, dy=1)
        by_xy = self.shift(jnp.concatenate([first, by_x]), dy=1)
        by_yx = self.shift(jnp.concatenate([second, by_y]), dx=1)
        return [own, by_x, by_y, by_xy, by_yx]

    def pass_on(self, held):
        return held + [self.shift(array, dc=1) for array in held]

    def begin(self, parts):
        send_a, send_b, keep_a, keep_b = parts
        return self.shift(send_a, dc=1), self.shift(send_b, dc=1), keep_a, keep_b

    def middle(self, state):
        got_a, got_b, keep_a, keep_b = state
        shape = keep_a.shape[1:]
        sum_a = (keep_a + got_a.astype(F32)).reshape((2, 4) + shape)
        sum_b = (keep_b + got_b.astype(F32)).reshape((2, 4) + shape)
        return sum_a[0], sum_b[0], sum_a[1].astype(BF16), sum_b[1].astype(BF16)

    def send(self, state):
        sum_a, sum_b, out_a, out_b = state
        return sum_a, sum_b, self.shift(out_a, dx=1), self.shift(out_b, dy=1)

    def end(self, state):
        def swap(values, **how):
            return self.shift(values.astype(BF16), **how).astype(F32)

        sum_a, sum_b, got_a, got_b = state
        shape = sum_a.shape[1:]
        sum_a = (sum_a + got_a.astype(F32)).reshape((2, 2) + shape)
        sum_b = (sum_b + got_b.astype(F32)).reshape((2, 2) + shape)
        sum_a = sum_a[:, 0] + swap(sum_a[:, 1], dy=1)
        sum_b = sum_b[:, 0] + swap(sum_b[:, 1], dx=1)
        return (
            sum_a[0] + swap(sum_a[1], dz=1) + swap(sum_b[0], dz=2) + swap(sum_b[1], dz=3)
        )


class Straight(Stages):
    def order(self, device):
        sides = [(0, 0), (0, 1), (1, 0), (1, 1)]
        self.gathered = [device(-k, dy, dx, dc) for dc in (0, 1) for dy, dx in sides for k in range(4)]
        self.sent = [device(k, dy, dx, dc) for dc in (1, 0) for dy, dx in sides for k in range(4)]
        self.slots = [(16, BF16), (16, F32)]

    def join(self, own, others):
        half = len(others) // 2
        return own[:1] + others[:half] + own[1:] + others[half:]

    def gather(self, own):
        return [own, self.shift(own, dx=1), self.shift(own, dy=1), self.shift(own, dx=1, dy=1)]

    def begin(self, parts):
        return self.shift(parts[0], dc=1), parts[1]

    def middle(self, state):
        got, keep = state
        total = (keep + got.astype(F32)).reshape((4, 4) + keep.shape[1:])
        return total[0], total[1].astype(BF16), total[2].astype(BF16), total[3].astype(BF16)

    def send(self, state):
        total, by_x, by_y, by_both = state
        return total, self.shift(by_x, dx=1), self.shift(by_y, dy=1), self.shift(by_both, dx=1, dy=1)

    def end(self, state):
        total = state[0]
        for got in state[1:]:
            total = total + got.astype(F32)
        low = total[1:].astype(BF16)
        out = total[0]
        for k in (1, 2, 3):
            out = out + self.shift(low[k - 1], dz=k).astype(F32)
        return out


def to_piece(share, rows, me):
    size = share.shape[0]
    flat = jnp.zeros((rows * D,), share.dtype)
    return lax.dynamic_update_slice(flat, share, (size * me % GROUP,)).reshape(rows, D)


def from_piece(piece, size, me):
    return lax.dynamic_slice(piece.reshape(-1), (size * me % GROUP,), (size,))


def whole(shape=None):
    return pl.BlockSpec(memory_space=pltpu.VMEM)


def by_latent(group, *shape):
    zeros = (0,) * len(shape)
    return pl.BlockSpec((group,) + shape, lambda step, scal: (step,) + zeros)


def call(kernel, count, in_specs, out_specs, out_shape, scratch, args, flops):
    return pl.pallas_call(
        kernel,
        grid_spec=pltpu.PrefetchScalarGridSpec(
            num_scalar_prefetch=1,
            grid=(count,),
            in_specs=in_specs,
            out_specs=out_specs,
            scratch_shapes=scratch,
        ),
        out_shape=out_shape,
        compiler_params=pltpu.CompilerParams(
            vmem_limit_bytes=60 * 2**20, dimension_semantics=("arbitrary",)
        ),
        cost_estimate=pl.CostEstimate(flops=flops, bytes_accessed=20 * 2**20, transcendentals=0),
    )(*args)


def solution(mesh):
    devices = mesh.shape[AXIS]

    def body(latents, condition, attn_params, mlp_params, counts, cotangent):
        count, seq = latents.shape[0], latents.shape[1]
        me = lax.axis_index(AXIS)
        known = devices == 32
        plan = (Stages if known else Direct)(devices, me)
        mlp_plan = (Straight if known else Direct)(devices, me)
        attn_size, mlp_size = attn_params.shape[0], mlp_params.shape[0]
        attn_height = piece_rows(attn_size, devices)
        mlp_height = piece_rows(mlp_size, devices)

        def scalars(size, order):
            ids = jnp.stack(order.gathered + order.sent)
            return jnp.concatenate([counts.astype(jnp.int32), size * ids // GROUP]).astype(jnp.int32)

        attn_scal, mlp_scal = scalars(attn_size, plan), scalars(mlp_size, mlp_plan)
        attn_own, mlp_piece = plan.start(to_piece(attn_params, attn_height, me)), to_piece(mlp_params, mlp_height, me)
        attn_own, mlp_piece = lax.optimization_barrier((attn_own, mlp_piece))
        attn_pieces = plan.gather(attn_own)
        mlp_own = mlp_plan.start(mlp_piece)
        mlp_own, attn_pieces, attn_scal, mlp_scal = lax.optimization_barrier(
            (mlp_own, attn_pieces, attn_scal, mlp_scal)
        )
        attn_pieces = plan.pass_on(attn_pieces)
        mlp_pieces = mlp_plan.gather(mlp_own)

        def struct(shape, kind):
            return jax.ShapeDtypeStruct(shape, kind)

        n_pieces = len(attn_pieces)
        n_mlp_pieces = len(mlp_pieces) * (2 if known else 1)
        n_out, n_mlp_out = len(plan.slots), len(mlp_plan.slots)
        mod, ada, qkv_w, proj, _, qkv, probs, mixed, branch = call(
            lambda *refs: forward_kernel(n_pieces, *refs),
            count // FORWARD_STEP,
            [whole(), by_latent(FORWARD_STEP, seq, D)] + [whole()] * n_pieces,
            [whole()] * 5
            + [
                by_latent(FORWARD_STEP, seq, 3 * D),
                by_latent(FORWARD_STEP, HEADS, seq, seq),
                by_latent(FORWARD_STEP, D, seq),
                by_latent(FORWARD_STEP, seq, D),
            ],
            [
                struct((6, count, D), F32),
                struct((6, D, D), BF16),
                struct((D, 3 * D), BF16),
                struct((D, D), BF16),
                struct((8, D), F32),
                struct((count, seq, 3 * D), BF16),
                struct((count, HEADS, seq, seq), BF16),
                struct((count, D, seq), BF16),
                struct((count, seq, D), F32),
            ],
            [
                pltpu.VMEM((TILES, ATTN_ROWS + attn_height, LANES), F32),
                pltpu.VMEM((FORWARD_STEP, HEADS, seq, seq), F32),
            ],
            [attn_scal, condition, latents] + attn_pieces,
            15 * 10**9,
        )
        mlp_own = mlp_plan.pass_on(mlp_pieces[:1])
        mlp_pieces, mod = lax.optimization_barrier((mlp_pieces[1:], mod))
        mlp_pieces = mlp_plan.join(mlp_own, mlp_plan.pass_on(mlp_pieces))
        results = call(
            lambda *refs: mlp_kernel(n_mlp_pieces, n_mlp_out, *refs),
            count // MLP_STEP,
            [whole(), whole(), by_latent(MLP_STEP, seq, D), by_latent(MLP_STEP, seq, D), by_latent(MLP_STEP, D, seq), by_latent(MLP_STEP, seq, D)]
            + [whole()] * n_mlp_pieces,
            [by_latent(MLP_STEP, seq, D), by_latent(MLP_STEP, seq, D), by_latent(MLP_STEP, seq, D), whole(), whole()]
            + [whole()] * n_mlp_out,
            [
                struct((count, seq, D), BF16),
                struct((count, seq, D), F32),
                struct((count, seq, D), BF16),
                struct((4, count, D), F32),
                struct((D, D), F32),
            ]
            + [struct((slots, mlp_height, D), kind) for slots, kind in mlp_plan.slots],
            [
                pltpu.VMEM((TILES, MLP_ROWS + 2 + mlp_height, LANES), F32),
                pltpu.VMEM((D, FF), BF16),
                pltpu.VMEM((FF, D), BF16),
                pltpu.VMEM((8, FF), F32),
                pltpu.VMEM((MLP_STEP * seq, FF), BF16),
                pltpu.VMEM((MLP_STEP * seq, FF), F32),
                pltpu.VMEM((MLP_STEP * seq, FF), BF16),
                pltpu.VMEM((D, FF), F32),
                pltpu.VMEM((D, FF), F32),
                pltpu.VMEM((8, FF), F32),
            ],
            [mlp_scal, mod, proj, latents, branch, mixed, cotangent] + mlp_pieces,
            30 * 10**9,
        )
        output, grad_middle, grad_mixed, dmod, dproj = results[:5]
        sums = mlp_plan.begin(results[5:])
        grad_qkv, = call(
            attend_back_kernel,
            count // ATTEND_STEP,
            [by_latent(ATTEND_STEP, seq, 3 * D), by_latent(ATTEND_STEP, HEADS, seq, seq), by_latent(ATTEND_STEP, seq, D)],
            [by_latent(ATTEND_STEP, seq, 3 * D)],
            [struct((count, seq, 3 * D), BF16)],
            [
                pltpu.VMEM((HEADS, seq, seq), F32),
                pltpu.VMEM((HEADS, seq, seq), BF16),
                pltpu.VMEM((D, seq), F32),
            ],
            [attn_scal, qkv, probs, grad_mixed],
            13 * 10**9,
        )
        sums, grad_qkv = lax.optimization_barrier((sums, grad_qkv))
        sums = mlp_plan.middle(sums)
        sums, grad_qkv = lax.optimization_barrier((sums, grad_qkv))
        sums = mlp_plan.send(sums)
        results = call(
            lambda *refs: finish_kernel(n_out, 1 + devices, *refs),
            count // FINISH_STEP,
            [whole()] * 6 + [by_latent(FINISH_STEP, seq, D), by_latent(FINISH_STEP, seq, 3 * D), by_latent(FINISH_STEP, seq, D)],
            [by_latent(FINISH_STEP, seq, D), whole()] + [whole()] * n_out,
            [struct((count, seq, D), F32), struct((count, D), F32)]
            + [struct((slots, attn_height, D), kind) for slots, kind in plan.slots],
            [
                pltpu.VMEM((TILES, ATTN_ROWS + attn_height, LANES), F32),
                pltpu.VMEM((D, 3 * D), F32),
                pltpu.VMEM((2, count, D), F32),
                pltpu.VMEM((8, 3 * D), F32),
            ],
            [attn_scal, mod, qkv_w, condition, ada, dmod, dproj, latents, grad_qkv, grad_middle],
            15 * 10**9,
        )
        grad_latents, grad_condition = results[:2]
        sums, attn_parts = lax.optimization_barrier((sums, results[2:]))
        grad_attn = plan.end(plan.send(plan.middle(plan.begin(attn_parts))))
        grad_mlp = mlp_plan.end(sums)
        return (
            output,
            grad_latents,
            grad_condition,
            from_piece(grad_attn, attn_size, me),
            from_piece(grad_mlp, mlp_size, me),
        )

    in_specs = (
        P(AXIS, None, None),
        P(AXIS, None),
        P(AXIS),
        P(AXIS),
        P(AXIS),
        P(AXIS, None, None),
    )
    out_specs = (
        P(AXIS, None, None),
        P(AXIS, None, None),
        P(AXIS, None),
        P(AXIS),
        P(AXIS),
    )
    return jax.shard_map(body, mesh=mesh, in_specs=in_specs, out_specs=out_specs, check_vma=False)
```

```python
import jax
import jax.numpy as jnp
from jax import lax
from jax.experimental import pallas as pl
from jax.experimental.pallas import tpu as pltpu
from jax.sharding import PartitionSpec as P

D = 384
HEADS = 6
HEAD_DIM = 64
FF = 1536
EPSILON = 1e-06
AXIS = "fsdp"
LANES = 128
TILES = D // LANES
GROUP = 8 * D
FACTOR = HEAD_DIM ** (-0.5)
GELU_A = 0.7978845608028654
GELU_B = 0.044715
CHUNK = 1536
FORWARD_STEP = 2
MLP_STEP = 2
ATTEND_STEP = 2
FINISH_STEP = 2

ADA_AT = 0
QKV_AT = 6 * D
PROJ_AT = 9 * D
B_ADA_AT = 10 * D
B_QV_AT = 10 * D + 6
ATTN_ROWS = 10 * D + 8
FC1_AT = 0
FC2_AT = FF
B_FC1_AT = 2 * FF
B_FC2_AT = 2 * FF + 4
B_PROJ_AT = 2 * FF + 5
MLP_ROWS = 2 * FF + 6

F32 = jnp.float32
BF16 = jnp.bfloat16


def round_up(value, unit):
    return -(-value // unit) * unit


def piece_rows(share, count):
    lead = max((share * index) % GROUP for index in range(count))
    return round_up(-(-(share + lead) // D), 16)


def mm(left, right):
    return jnp.dot(left, right, preferred_element_type=F32)


def mm_nt(left, right):
    return lax.dot_general(left, right, (((1,), (1,)), ((), ())), preferred_element_type=F32)


def mm_tn(left, right):
    return lax.dot_general(left, right, (((0,), (0,)), ((), ())), preferred_element_type=F32)


def col_sum(values):
    return jnp.sum(values, axis=0, keepdims=True)


def row_mean(values):
    return jnp.mean(values, axis=-1, keepdims=True)


def normalize(values):
    centered = values - row_mean(values)
    rstd = lax.rsqrt(row_mean(centered * centered) + EPSILON)
    return centered * rstd, rstd


def normalize_back(grad, normed, rstd):
    return rstd * (grad - row_mean(grad) - normed * row_mean(grad * normed))


def flat(values):
    return values.reshape(-1, values.shape[-1])


def mod_rows(mod_ref, part, step, group):
    rows = [mod_ref[part, pl.ds(step * group + latent, 1), :] for latent in range(group)]
    return jnp.stack(rows)


def put_mod(ref, part, step, values):
    for latent in range(values.shape[0]):
        ref[part, pl.ds(step * values.shape[0] + latent, 1), :] = col_sum(values[latent])


def head_masks():
    lane = lax.broadcasted_iota(jnp.int32, (1, LANES), 1) // HEAD_DIM
    return [(lane == head).astype(F32).astype(BF16) for head in range(2)]


def assemble(scal_ref, base, piece_refs, rows_ref):
    rows_ref[...] = jnp.zeros_like(rows_ref)
    at = base
    for ref in piece_refs:
        slots, height = ref.shape[0], ref.shape[1]

        def one(slot, carry, ref=ref, at=at, height=height):
            start = pl.multiple_of(scal_ref[at + slot] * 8, 8)
            for tile in range(TILES):
                lanes = slice(tile * LANES, (tile + 1) * LANES)
                rows_ref[tile, pl.ds(start, height), :] += ref[slot, :, lanes].astype(F32)
            return carry

        lax.fori_loop(0, slots, one, 0)
        at += slots


def emit(scal_ref, base, out_refs, rows_ref):
    at = base
    for ref in out_refs:
        slots, height = ref.shape[0], ref.shape[1]

        def one(slot, carry, ref=ref, at=at, height=height):
            start = pl.multiple_of(scal_ref[at + slot] * 8, 8)
            for tile in range(TILES):
                lanes = slice(tile * LANES, (tile + 1) * LANES)
                ref[slot, :, lanes] = rows_ref[tile, pl.ds(start, height), :].astype(ref.dtype)
            return carry

        lax.fori_loop(0, slots, one, 0)
        at += slots


def lanes_of(tile, offset=0):
    return slice(offset + tile * LANES, offset + (tile + 1) * LANES)


def forward_kernel(n_pieces, scal_ref, cond_ref, x_ref, *refs):
    pieces = refs[:n_pieces]
    mod_ref, ada_hbm_ref, qkv_w_ref, proj_ref, bias_ref, qkv_ref, probs_ref, mixed_ref, branch_ref = refs[
        n_pieces : n_pieces + 9
    ]
    rows_ref, score_ref, ada_ref, ada_sem = refs[n_pieces + 9 :]
    store = pltpu.make_async_copy(ada_ref, ada_hbm_ref, ada_sem)
    step = pl.program_id(0)
    group, seq = x_ref.shape[0], x_ref.shape[1]

    @pl.when(step == 0)
    def _():
        assemble(scal_ref, 1, pieces, rows_ref)
        for tile in range(TILES):
            proj_ref[:, lanes_of(tile)] = rows_ref[tile, pl.ds(PROJ_AT, D), :].astype(BF16)
            bias_ref[:, lanes_of(tile)] = rows_ref[tile, pl.ds(B_ADA_AT, 8), :]
            for block in range(6):
                ada_ref[block, :, lanes_of(tile)] = rows_ref[
                    tile, pl.ds(ADA_AT + block, D, stride=6), :
                ].astype(BF16)
            for block in range(3):
                qkv_w_ref[:, lanes_of(tile, block * D)] = rows_ref[
                    tile, pl.ds(QKV_AT + block, D, stride=3), :
                ].astype(BF16)
        store.start()
        act = jax.nn.silu(cond_ref[...].astype(F32)).astype(BF16)
        for block in range(6):
            mod_ref[block] = mm(act, ada_ref[block]) + bias_ref[block : block + 1, :]

    @pl.when(step * group < scal_ref[0])
    def _():
        masks = head_masks()
        values = x_ref[...].astype(F32)
        normed, _ = normalize(values)
        shift, scale = [mod_rows(mod_ref, part, step, group) for part in range(2)]
        modulated = flat(normed * (1.0 + scale) + shift).astype(BF16)
        qkv = mm(modulated, qkv_w_ref[...])
        queries = (qkv[:, :D] + bias_ref[6:7, :]).astype(BF16)
        keys_all = qkv[:, D : 2 * D].astype(BF16)
        values_all = (qkv[:, 2 * D :] + bias_ref[7:8, :]).astype(BF16)
        for latent in range(group):
            tokens = slice(latent * seq, (latent + 1) * seq)
            qkv_ref[latent, :, :D] = queries[tokens]
            qkv_ref[latent, :, D : 2 * D] = keys_all[tokens]
            qkv_ref[latent, :, 2 * D :] = values_all[tokens]
            for head in range(HEADS):
                lanes = lanes_of(head // 2)
                own = queries[tokens, lanes] * (masks[head % 2] * FACTOR)
                score_ref[latent, head] = mm_nt(keys_all[tokens, lanes], own)
        for latent in range(group):
            tokens = slice(latent * seq, (latent + 1) * seq)
            values_t = values_all[tokens].T
            for head in range(HEADS):
                scores = score_ref[latent, head]
                expo = jnp.exp(scores - jnp.max(scores, axis=0, keepdims=True))
                probs_ref[latent, head] = (expo * (1.0 / col_sum(expo))).astype(BF16)
            for head in range(HEADS):
                rows = slice(head * HEAD_DIM, (head + 1) * HEAD_DIM)
                mixed_ref[latent, rows, :] = mm(values_t[rows, :], probs_ref[latent, head]).astype(BF16)
            branch_ref[latent] = mm_tn(mixed_ref[latent], proj_ref[...])

    @pl.when(step == pl.num_programs(0) - 1)
    def _():
        store.wait()


def mlp_kernel(n_pieces, n_out, scal_ref, mod_ref, proj_ref, x_ref, branch_ref, mixed_ref, cot_ref, *refs):
    pieces = refs[:n_pieces]
    outs = refs[n_pieces : n_pieces + 5 + n_out]
    out_ref, dx_ref, dmixed_ref, dmod_ref, dproj_ref = outs[:5]
    send_refs = outs[5:]
    rows_ref, fc1_ref, fc2_ref, bias_ref, act_ref, slope_ref, du_ref, dfc1_ref, dfc2_ref, dbias_ref = refs[
        n_pieces + 5 + n_out :
    ]
    step = pl.program_id(0)
    last = pl.num_programs(0) - 1

    @pl.when(step == 0)
    def _():
        assemble(scal_ref, 1, pieces, rows_ref)
        for block in range(4):
            for tile in range(TILES):
                fc1_ref[:, lanes_of(tile, block * D)] = rows_ref[
                    tile, pl.ds(FC1_AT + block, D, stride=4), :
                ].astype(BF16)
                bias_ref[0:1, lanes_of(tile, block * D)] = rows_ref[tile, pl.ds(B_FC1_AT + block, 1), :]
        for tile in range(TILES):
            fc2_ref[:, lanes_of(tile)] = rows_ref[tile, pl.ds(FC2_AT, FF), :].astype(BF16)
            bias_ref[1:2, lanes_of(tile)] = rows_ref[tile, pl.ds(B_FC2_AT, 1), :]
            bias_ref[2:3, lanes_of(tile)] = rows_ref[tile, pl.ds(B_PROJ_AT, 1), :]
        dfc1_ref[...] = jnp.zeros_like(dfc1_ref)
        dfc2_ref[...] = jnp.zeros_like(dfc2_ref)
        dbias_ref[...] = jnp.zeros_like(dbias_ref)
        dproj_ref[...] = jnp.zeros_like(dproj_ref)
        dmod_ref[...] = jnp.zeros_like(dmod_ref)

    group, seq = x_ref.shape[0], x_ref.shape[1]

    @pl.when(step * group < scal_ref[0])
    def _():
        gate_one, shift, scale, gate_two = [mod_rows(mod_ref, 2 + part, step, group) for part in range(4)]
        slot = step * group + lax.broadcasted_iota(jnp.int32, (group, 1, 1), 0)
        live = (slot < scal_ref[0]).astype(F32)
        branch_one = branch_ref[...] + bias_ref[2:3, :D]
        middle = x_ref[...].astype(F32) + gate_one * branch_one
        normed, rstd = normalize(middle)
        modulated = flat(normed * (1.0 + scale) + shift).astype(BF16)
        chunk = CHUNK
        for start in range(0, FF, chunk):
            part = slice(start, start + chunk)
            pre = mm(modulated, fc1_ref[:, part]) + bias_ref[0:1, part]
            square = pre * pre
            bend = jnp.tanh(pre * (GELU_A + (GELU_A * GELU_B) * square))
            half = 0.5 + 0.5 * bend
            act = (pre * half).astype(BF16)
            act_ref[:, part] = act
            slope_ref[:, part] = half + (pre * (0.5 - 0.5 * bend * bend)) * (
                GELU_A + (3.0 * GELU_A * GELU_B) * square
            )
        branch_two = mm(act_ref[...], fc2_ref[...])
        branch_two = (branch_two + bias_ref[1:2, :D]).reshape(group, seq, D)
        out_ref[...] = (live * (middle + gate_two * branch_two)).astype(BF16)
        grad_out = live * cot_ref[...].astype(F32)
        put_mod(dmod_ref, 3, step, grad_out * branch_two)
        grad_two = flat(gate_two * grad_out).astype(BF16)
        dbias_ref[1:2, :D] += col_sum(grad_two.astype(F32))
        grad_two_t = grad_two.T
        modulated_t = modulated.T
        for start in range(0, FF, chunk):
            part = slice(start, start + chunk)
            du = (mm_nt(grad_two, fc2_ref[part, :]) * slope_ref[:, part]).astype(BF16)
            dbias_ref[0:1, part] += col_sum(du.astype(F32))
            du_ref[:, part] = du
        grad_mod = mm_nt(du_ref[...], fc1_ref[...]).reshape(group, seq, D)
        dfc2_ref[...] += mm(grad_two_t, act_ref[...])
        dfc1_ref[...] += mm(modulated_t, du_ref[...])
        put_mod(dmod_ref, 1, step, grad_mod)
        put_mod(dmod_ref, 2, step, grad_mod * normed)
        grad_middle = grad_out + normalize_back(grad_mod * (1.0 + scale), normed, rstd)
        dx_ref[...] = grad_middle
        put_mod(dmod_ref, 0, step, grad_middle * branch_one)
        grad_one = flat(gate_one * grad_middle).astype(BF16)
        dbias_ref[2:3, :D] += col_sum(grad_one.astype(F32))
        grad_mixed = mm_nt(grad_one, proj_ref[...]).astype(BF16)
        for latent in range(group):
            tokens = slice(latent * seq, (latent + 1) * seq)
            dproj_ref[...] += mm(mixed_ref[latent], grad_one[tokens])
            dmixed_ref[latent] = grad_mixed[tokens]

    @pl.when(step * group >= scal_ref[0])
    def _():
        out_ref[...] = jnp.zeros_like(out_ref)
        dx_ref[...] = jnp.zeros_like(dx_ref)
        dmixed_ref[...] = jnp.zeros_like(dmixed_ref)

    @pl.when(step == last)
    def _():
        for block in range(4):
            for tile in range(TILES):
                rows_ref[tile, pl.ds(FC1_AT + block, D, stride=4), :] = dfc1_ref[
                    :, lanes_of(tile, block * D)
                ]
                rows_ref[tile, pl.ds(B_FC1_AT + block, 1), :] = dbias_ref[0:1, lanes_of(tile, block * D)]
        for tile in range(TILES):
            rows_ref[tile, pl.ds(FC2_AT, FF), :] = dfc2_ref[lanes_of(tile), :].T
            rows_ref[tile, pl.ds(B_FC2_AT, 1), :] = dbias_ref[1:2, lanes_of(tile)]
            rows_ref[tile, pl.ds(B_PROJ_AT, 1), :] = dbias_ref[2:3, lanes_of(tile)]
        emit(scal_ref, 1 + sum(ref.shape[0] for ref in pieces), send_refs, rows_ref)


def attend_back_kernel(scal_ref, qkv_ref, probs_ref, dmixed_ref, dqkv_ref, dprobs_ref, low_ref, dq_t_ref):
    group, seq = qkv_ref.shape[0], qkv_ref.shape[1]

    @pl.when(pl.program_id(0) * group < scal_ref[0])
    def _():
        masks = head_masks()
        for latent in range(group):
            keys_t = qkv_ref[latent, :, D : 2 * D].T
            for head in range(HEADS):
                own = dmixed_ref[latent, :, lanes_of(head // 2)] * masks[head % 2]
                dprobs_ref[head] = mm_nt(qkv_ref[latent, :, lanes_of(head // 2, 2 * D)], own)
            for head in range(HEADS):
                probs, grad_probs = probs_ref[latent, head].astype(F32), dprobs_ref[head]
                low_ref[head] = (probs * (grad_probs - col_sum(probs * grad_probs))).astype(BF16)
            for pair in range(HEADS // 2):
                query = qkv_ref[latent, :, lanes_of(pair)]
                grad = dmixed_ref[latent, :, lanes_of(pair)]
                grad_key = jnp.zeros((seq, LANES), F32)
                grad_value = jnp.zeros((seq, LANES), F32)
                for half in range(2):
                    head = 2 * pair + half
                    rows = slice(head * HEAD_DIM, (head + 1) * HEAD_DIM)
                    grad_value += mm(probs_ref[latent, head], grad * masks[half])
                    grad_key += mm(low_ref[head], query * masks[half])
                    dq_t_ref[rows, :] = mm(keys_t[rows, :], low_ref[head])
                dqkv_ref[latent, :, lanes_of(pair, D)] = (grad_key * FACTOR).astype(BF16)
                dqkv_ref[latent, :, lanes_of(pair, 2 * D)] = grad_value.astype(BF16)
            dqkv_ref[latent, :, :D] = (dq_t_ref[...] * FACTOR).astype(BF16).T


def finish_kernel(
    n_out, base, scal_ref, mod_ref, qkv_w_ref, cond_ref, ada_hbm_ref, dmod_in_ref, dproj_ref,
    x_ref, dqkv_ref, dx_ref, *refs
):
    grad_x_ref, grad_cond_ref = refs[:2]
    send_refs = refs[2 : 2 + n_out]
    rows_ref, dqkv_w_ref, dmod_ref, dbias_ref, ada_ref, ada_sem = refs[2 + n_out :]
    fetch = pltpu.make_async_copy(ada_hbm_ref, ada_ref, ada_sem)
    step = pl.program_id(0)
    last = pl.num_programs(0) - 1
    group, seq = x_ref.shape[0], x_ref.shape[1]

    @pl.when(step == 0)
    def _():
        fetch.start()
        dqkv_w_ref[...] = jnp.zeros_like(dqkv_w_ref)
        dmod_ref[...] = jnp.zeros_like(dmod_ref)
        dbias_ref[...] = jnp.zeros_like(dbias_ref)

    @pl.when(step * group < scal_ref[0])
    def _():
        shift, scale = [mod_rows(mod_ref, part, step, group) for part in range(2)]
        normed, rstd = normalize(x_ref[...].astype(F32))
        modulated = flat(normed * (1.0 + scale) + shift).astype(BF16)
        grad_qkv = flat(dqkv_ref[...])
        dbias_ref[0:1, :] += col_sum(grad_qkv.astype(F32))
        dqkv_w_ref[...] += mm(modulated.T, grad_qkv)
        grad_mod = mm_nt(grad_qkv, qkv_w_ref[...]).reshape(group, seq, D)
        put_mod(dmod_ref, 0, step, grad_mod)
        put_mod(dmod_ref, 1, step, grad_mod * normed)
        grad_x_ref[...] = dx_ref[...] + normalize_back(grad_mod * (1.0 + scale), normed, rstd)

    @pl.when(step * group >= scal_ref[0])
    def _():
        grad_x_ref[...] = jnp.zeros_like(grad_x_ref)

    @pl.when(step == last)
    def _():
        fetch.wait()
        cond = cond_ref[...].astype(F32)
        gate = jax.nn.sigmoid(cond)
        act = (cond * gate).astype(BF16)
        grad_act = jnp.zeros_like(cond)
        for block in range(6):
            grad = (dmod_ref[block] if block < 2 else dmod_in_ref[block - 2]).astype(BF16)
            grad_act += mm_nt(grad, ada_ref[block])
            weight = mm_tn(act, grad)
            bias = col_sum(grad.astype(F32))
            for tile in range(TILES):
                rows_ref[tile, pl.ds(ADA_AT + block, D, stride=6), :] = weight[:, lanes_of(tile)]
                rows_ref[tile, pl.ds(B_ADA_AT + block, 1), :] = bias[:, lanes_of(tile)]
        grad_cond_ref[...] = grad_act * (gate * (1.0 + cond * (1.0 - gate)))
        for tile in range(TILES):
            for block in range(3):
                rows_ref[tile, pl.ds(QKV_AT + block, D, stride=3), :] = dqkv_w_ref[
                    :, lanes_of(tile, block * D)
                ]
            rows_ref[tile, pl.ds(PROJ_AT, D), :] = dproj_ref[:, lanes_of(tile)]
            rows_ref[tile, pl.ds(B_QV_AT, 1), :] = dbias_ref[0:1, lanes_of(tile)]
            rows_ref[tile, pl.ds(B_QV_AT + 1, 1), :] = dbias_ref[0:1, lanes_of(tile, 2 * D)]
        emit(scal_ref, base, send_refs, rows_ref)


class Direct:
    def __init__(self, count, me):
        self.count, self.me = count, me
        self.gathered = self.sent = [jnp.int32(index) for index in range(count)]
        self.slots = [(count, F32)]

    def start(self, piece):
        return piece

    def gather(self, piece):
        return [lax.all_gather(piece, AXIS, axis=0)]

    def pass_on(self, held):
        return held

    def join(self, own, others):
        return own

    def begin(self, parts):
        return parts

    middle = send = begin

    def end(self, parts):
        return lax.psum_scatter(parts[0], AXIS, scatter_dimension=0)


class Stages:
    def __init__(self, count, me):
        self.me = me
        core, x, y, z = me % 2, me // 2 % 2, me // 4 % 2, me // 8

        def device(dz, dy, dx, dc):
            return (((z + dz) % 4 * 2 + (y + dy) % 2) * 2 + (x + dx) % 2) * 2 + (core + dc) % 2

        self.order(device)

    def order(self, device):
        gathered = []
        for dc in range(2):
            gathered += [device(-k, 0, 0, dc) for k in (0, 1, 2, 3)]
            gathered += [device(-k, 0, 1, dc) for k in (0, 1)]
            gathered += [device(-k, 1, 0, dc) for k in (2, 3)]
            gathered += [device(-k, 1, dx, dc) for dx in (0, 1) for k in (0, 1)]
            gathered += [device(-k, dy, 1, dc) for dy in (0, 1) for k in (2, 3)]
        self.gathered = gathered
        sent = []
        for dc in (1, 0):
            sent += [device(k, dy, dx, dc) for dx in (0, 1) for k in (0, 1) for dy in (0, 1)]
            sent += [device(k, dy, dx, dc) for dy in (0, 1) for k in (2, 3) for dx in (0, 1)]
        self.sent = sent
        self.slots = [(8, BF16)] * 4

    def shift(self, values, dz=0, dy=0, dx=0, dc=0):
        pairs = []
        for source in range(32):
            core, x, y, z = source % 2, source // 2 % 2, source // 4 % 2, source // 8
            target = (((z + dz) % 4 * 2 + (y + dy) % 2) * 2 + (x + dx) % 2) * 2 + (core + dc) % 2
            pairs.append((source, target))
        return lax.ppermute(values, AXIS, pairs)

    def start(self, piece):
        return jnp.stack([piece] + [self.shift(piece, dz=k) for k in (1, 2, 3)])

    def gather(self, own):
        first, second = own[:2], own[2:]
        by_x = self.shift(first, dx=1)
        by_y = self.shift(second, dy=1)
        by_xy = self.shift(jnp.concatenate([first, by_x]), dy=1)
        by_yx = self.shift(jnp.concatenate([second, by_y]), dx=1)
        return [own, by_x, by_y, by_xy, by_yx]

    def pass_on(self, held):
        return held + [self.shift(array, dc=1) for array in held]

    def begin(self, parts):
        send_a, send_b, keep_a, keep_b = parts
        return self.shift(send_a, dc=1), self.shift(send_b, dc=1), keep_a, keep_b

    def middle(self, state):
        got_a, got_b, keep_a, keep_b = state
        shape = keep_a.shape[1:]
        sum_a = (keep_a.astype(F32) + got_a.astype(F32)).reshape((2, 4) + shape)
        sum_b = (keep_b.astype(F32) + got_b.astype(F32)).reshape((2, 4) + shape)
        return sum_a[0], sum_b[0], sum_a[1].astype(BF16), sum_b[1].astype(BF16)

    def send(self, state):
        sum_a, sum_b, out_a, out_b = state
        return sum_a, sum_b, self.shift(out_a, dx=1), self.shift(out_b, dy=1)

    def end(self, state):
        def swap(values, **how):
            return self.shift(values.astype(BF16), **how).astype(F32)

        sum_a, sum_b, got_a, got_b = state
        shape = sum_a.shape[1:]
        sum_a = (sum_a + got_a.astype(F32)).reshape((2, 2) + shape)
        sum_b = (sum_b + got_b.astype(F32)).reshape((2, 2) + shape)
        sum_a = sum_a[:, 0] + swap(sum_a[:, 1], dy=1)
        sum_b = sum_b[:, 0] + swap(sum_b[:, 1], dx=1)
        return (
            sum_a[0] + swap(sum_a[1], dz=1) + swap(sum_b[0], dz=2) + swap(sum_b[1], dz=3)
        )


class Straight(Stages):
    def order(self, device):
        sides = [(0, 0), (0, 1), (1, 0), (1, 1)]
        self.gathered = [device(-k, dy, dx, dc) for dc in (0, 1) for dy, dx in sides for k in range(4)]
        self.sent = [device(k, dy, dx, dc) for dc in (1, 0) for dy, dx in sides for k in range(4)]
        self.slots = [(16, BF16)] * 2

    def join(self, own, others):
        half = len(others) // 2
        return own[:1] + others[:half] + own[1:] + others[half:]

    def gather(self, own):
        return [own, self.shift(own, dx=1), self.shift(own, dy=1), self.shift(own, dx=1, dy=1)]

    def begin(self, parts):
        return self.shift(parts[0], dc=1), parts[1]

    def middle(self, state):
        got, keep = state
        total = (keep.astype(F32) + got.astype(F32)).reshape((4, 4) + keep.shape[1:])
        return total[0], total[1].astype(BF16), total[2].astype(BF16), total[3].astype(BF16)

    def send(self, state):
        total, by_x, by_y, by_both = state
        return total, self.shift(by_x, dx=1), self.shift(by_y, dy=1), self.shift(by_both, dx=1, dy=1)

    def end(self, state):
        total = state[0]
        for got in state[1:]:
            total = total + got.astype(F32)
        low = total[1:].astype(BF16)
        out = total[0]
        for k in (1, 2, 3):
            out = out + self.shift(low[k - 1], dz=k).astype(F32)
        return out


def to_piece(share, rows, me):
    size = share.shape[0]
    flat = jnp.zeros((rows * D,), share.dtype)
    return lax.dynamic_update_slice(flat, share, (size * me % GROUP,)).reshape(rows, D)


def from_piece(piece, size, me):
    return lax.dynamic_slice(piece.reshape(-1), (size * me % GROUP,), (size,))


def whole(shape=None):
    return pl.BlockSpec(memory_space=pltpu.VMEM)


def by_latent(group, *shape):
    zeros = (0,) * len(shape)
    return pl.BlockSpec((group,) + shape, lambda step, scal: (step,) + zeros)


def call(kernel, count, in_specs, out_specs, out_shape, scratch, args, flops):
    return pl.pallas_call(
        kernel,
        grid_spec=pltpu.PrefetchScalarGridSpec(
            num_scalar_prefetch=1,
            grid=(count,),
            in_specs=in_specs,
            out_specs=out_specs,
            scratch_shapes=scratch,
        ),
        out_shape=out_shape,
        compiler_params=pltpu.CompilerParams(
            vmem_limit_bytes=60 * 2**20, dimension_semantics=("arbitrary",)
        ),
        cost_estimate=pl.CostEstimate(flops=flops, bytes_accessed=20 * 2**20, transcendentals=0),
    )(*args)


def solution(mesh):
    devices = mesh.shape[AXIS]

    def body(latents, condition, attn_params, mlp_params, counts, cotangent):
        count, seq = latents.shape[0], latents.shape[1]
        me = lax.axis_index(AXIS)
        known = devices == 32
        plan = (Stages if known else Direct)(devices, me)
        mlp_plan = (Straight if known else Direct)(devices, me)
        attn_size, mlp_size = attn_params.shape[0], mlp_params.shape[0]
        attn_height = piece_rows(attn_size, devices)
        mlp_height = piece_rows(mlp_size, devices)

        def scalars(size, order):
            ids = jnp.stack(order.gathered + order.sent)
            return jnp.concatenate([counts.astype(jnp.int32), size * ids // GROUP]).astype(jnp.int32)

        attn_scal, mlp_scal = scalars(attn_size, plan), scalars(mlp_size, mlp_plan)
        attn_own, mlp_piece = plan.start(to_piece(attn_params, attn_height, me)), to_piece(mlp_params, mlp_height, me)
        attn_own, mlp_piece = lax.optimization_barrier((attn_own, mlp_piece))
        attn_pieces = plan.gather(attn_own)
        mlp_own = mlp_plan.start(mlp_piece)
        mlp_own, attn_pieces, attn_scal, mlp_scal = lax.optimization_barrier(
            (mlp_own, attn_pieces, attn_scal, mlp_scal)
        )
        attn_pieces = plan.pass_on(attn_pieces)
        mlp_pieces = mlp_plan.gather(mlp_own)

        def struct(shape, kind):
            return jax.ShapeDtypeStruct(shape, kind)

        n_pieces = len(attn_pieces)
        n_mlp_pieces = len(mlp_pieces) * (2 if known else 1)
        n_out, n_mlp_out = len(plan.slots), len(mlp_plan.slots)
        mod, ada, qkv_w, proj, _, qkv, probs, mixed, branch = call(
            lambda *refs: forward_kernel(n_pieces, *refs),
            count // FORWARD_STEP,
            [whole(), by_latent(FORWARD_STEP, seq, D)] + [whole()] * n_pieces,
            [whole(), pl.BlockSpec(memory_space=pl.ANY)] + [whole()] * 3
            + [
                by_latent(FORWARD_STEP, seq, 3 * D),
                by_latent(FORWARD_STEP, HEADS, seq, seq),
                by_latent(FORWARD_STEP, D, seq),
                by_latent(FORWARD_STEP, seq, D),
            ],
            [
                struct((6, count, D), F32),
                struct((6, D, D), BF16),
                struct((D, 3 * D), BF16),
                struct((D, D), BF16),
                struct((8, D), F32),
                struct((count, seq, 3 * D), BF16),
                struct((count, HEADS, seq, seq), BF16),
                struct((count, D, seq), BF16),
                struct((count, seq, D), F32),
            ],
            [
                pltpu.VMEM((TILES, ATTN_ROWS + attn_height, LANES), F32),
                pltpu.VMEM((FORWARD_STEP, HEADS, seq, seq), F32),
                pltpu.VMEM((6, D, D), BF16),
                pltpu.SemaphoreType.DMA,
            ],
            [attn_scal, condition, latents] + attn_pieces,
            15 * 10**9,
        )
        mlp_own = mlp_plan.pass_on(mlp_pieces[:1])
        mlp_pieces, mod = lax.optimization_barrier((mlp_pieces[1:], mod))
        mlp_pieces = mlp_plan.join(mlp_own, mlp_plan.pass_on(mlp_pieces))
        results = call(
            lambda *refs: mlp_kernel(n_mlp_pieces, n_mlp_out, *refs),
            count // MLP_STEP,
            [whole(), whole(), by_latent(MLP_STEP, seq, D), by_latent(MLP_STEP, seq, D), by_latent(MLP_STEP, D, seq), by_latent(MLP_STEP, seq, D)]
            + [whole()] * n_mlp_pieces,
            [by_latent(MLP_STEP, seq, D), by_latent(MLP_STEP, seq, D), by_latent(MLP_STEP, seq, D), whole(), whole()]
            + [whole()] * n_mlp_out,
            [
                struct((count, seq, D), BF16),
                struct((count, seq, D), F32),
                struct((count, seq, D), BF16),
                struct((4, count, D), F32),
                struct((D, D), F32),
            ]
            + [struct((slots, mlp_height, D), kind) for slots, kind in mlp_plan.slots],
            [
                pltpu.VMEM((TILES, MLP_ROWS + 2 + mlp_height, LANES), F32),
                pltpu.VMEM((D, FF), BF16),
                pltpu.VMEM((FF, D), BF16),
                pltpu.VMEM((8, FF), F32),
                pltpu.VMEM((MLP_STEP * seq, FF), BF16),
                pltpu.VMEM((MLP_STEP * seq, FF), F32),
                pltpu.VMEM((MLP_STEP * seq, FF), BF16),
                pltpu.VMEM((D, FF), F32),
                pltpu.VMEM((D, FF), F32),
                pltpu.VMEM((8, FF), F32),
            ],
            [mlp_scal, mod, proj, latents, branch, mixed, cotangent] + mlp_pieces,
            30 * 10**9,
        )
        output, grad_middle, grad_mixed, dmod, dproj = results[:5]
        sums = mlp_plan.begin(results[5:])
        grad_qkv, = call(
            attend_back_kernel,
            count // ATTEND_STEP,
            [by_latent(ATTEND_STEP, seq, 3 * D), by_latent(ATTEND_STEP, HEADS, seq, seq), by_latent(ATTEND_STEP, seq, D)],
            [by_latent(ATTEND_STEP, seq, 3 * D)],
            [struct((count, seq, 3 * D), BF16)],
            [
                pltpu.VMEM((HEADS, seq, seq), F32),
                pltpu.VMEM((HEADS, seq, seq), BF16),
                pltpu.VMEM((D, seq), F32),
            ],
            [attn_scal, qkv, probs, grad_mixed],
            13 * 10**9,
        )
        sums, grad_qkv = lax.optimization_barrier((sums, grad_qkv))
        sums = mlp_plan.middle(sums)
        sums, grad_qkv = lax.optimization_barrier((sums, grad_qkv))
        sums = mlp_plan.send(sums)
        results = call(
            lambda *refs: finish_kernel(n_out, 1 + devices, *refs),
            count // FINISH_STEP,
            [whole()] * 3 + [pl.BlockSpec(memory_space=pl.ANY)] + [whole()] * 2 + [by_latent(FINISH_STEP, seq, D), by_latent(FINISH_STEP, seq, 3 * D), by_latent(FINISH_STEP, seq, D)],
            [by_latent(FINISH_STEP, seq, D), whole()] + [whole()] * n_out,
            [struct((count, seq, D), F32), struct((count, D), F32)]
            + [struct((slots, attn_height, D), kind) for slots, kind in plan.slots],
            [
                pltpu.VMEM((TILES, ATTN_ROWS + attn_height, LANES), F32),
                pltpu.VMEM((D, 3 * D), F32),
                pltpu.VMEM((2, count, D), F32),
                pltpu.VMEM((8, 3 * D), F32),
                pltpu.VMEM((6, D, D), BF16),
                pltpu.SemaphoreType.DMA,
            ],
            [attn_scal, mod, qkv_w, condition, ada, dmod, dproj, latents, grad_qkv, grad_middle],
            15 * 10**9,
        )
        grad_latents, grad_condition = results[:2]
        sums, attn_parts = lax.optimization_barrier((sums, results[2:]))
        attn_parts = plan.middle(plan.begin(attn_parts))
        out_last, sums = lax.optimization_barrier((attn_parts[-1], sums))
        grad_attn = plan.end(plan.send([*attn_parts[:-1], out_last]))
        grad_mlp = mlp_plan.end(sums)
        return (
            output,
            grad_latents,
            grad_condition,
            from_piece(grad_attn, attn_size, me),
            from_piece(grad_mlp, mlp_size, me),
        )

    in_specs = (
        P(AXIS, None, None),
        P(AXIS, None),
        P(AXIS),
        P(AXIS),
        P(AXIS),
        P(AXIS, None, None),
    )
    out_specs = (
        P(AXIS, None, None),
        P(AXIS, None, None),
        P(AXIS, None),
        P(AXIS),
        P(AXIS),
    )
    return jax.shard_map(body, mesh=mesh, in_specs=in_specs, out_specs=out_specs, check_vma=False)
```

```python
import jax
import jax.numpy as jnp
from jax import lax
from jax.experimental import pallas as pl
from jax.experimental.pallas import tpu as pltpu
from jax.sharding import PartitionSpec as P

D = 384
HEADS = 6
HEAD_DIM = 64
FF = 1536
EPSILON = 1e-06
AXIS = "fsdp"
LANES = 128
TILES = D // LANES
GROUP = 8 * D
FACTOR = HEAD_DIM ** (-0.5)
GELU_A = 0.7978845608028654
GELU_B = 0.044715
CHUNK = 1536
FORWARD_STEP = 2
MLP_STEP = 2
ATTEND_STEP = 2
FINISH_STEP = 2

ADA_AT = 0
QKV_AT = 6 * D
PROJ_AT = 9 * D
B_ADA_AT = 10 * D
B_QV_AT = 10 * D + 6
ATTN_ROWS = 10 * D + 8
FC1_AT = 0
FC2_AT = FF
B_FC1_AT = 2 * FF
B_FC2_AT = 2 * FF + 4
B_PROJ_AT = 2 * FF + 5
MLP_ROWS = 2 * FF + 6

F32 = jnp.float32
BF16 = jnp.bfloat16


def round_up(value, unit):
    return -(-value // unit) * unit


def piece_rows(share, count):
    lead = max((share * index) % GROUP for index in range(count))
    return round_up(-(-(share + lead) // D), 16)


def mm(left, right):
    return jnp.dot(left, right, preferred_element_type=F32)


def mm_nt(left, right):
    return lax.dot_general(left, right, (((1,), (1,)), ((), ())), preferred_element_type=F32)


def mm_tn(left, right):
    return lax.dot_general(left, right, (((0,), (0,)), ((), ())), preferred_element_type=F32)


def col_sum(values):
    return jnp.sum(values, axis=0, keepdims=True)


def row_mean(values):
    return jnp.mean(values, axis=-1, keepdims=True)


def normalize(values):
    centered = values - row_mean(values)
    rstd = lax.rsqrt(row_mean(centered * centered) + EPSILON)
    return centered * rstd, rstd


def normalize_back(grad, normed, rstd):
    return rstd * (grad - row_mean(grad) - normed * row_mean(grad * normed))


def flat(values):
    return values.reshape(-1, values.shape[-1])


def mod_rows(mod_ref, part, step, group):
    rows = [mod_ref[part, pl.ds(step * group + latent, 1), :] for latent in range(group)]
    return jnp.stack(rows)


def put_mod(ref, part, step, values):
    for latent in range(values.shape[0]):
        ref[part, pl.ds(step * values.shape[0] + latent, 1), :] = col_sum(values[latent])


def head_masks():
    lane = lax.broadcasted_iota(jnp.int32, (1, LANES), 1) // HEAD_DIM
    return [(lane == head).astype(F32).astype(BF16) for head in range(2)]


def assemble(scal_ref, base, piece_refs, rows_ref):
    rows_ref[...] = jnp.zeros_like(rows_ref)
    at = base
    for ref in piece_refs:
        slots, height = ref.shape[0], ref.shape[1]

        def one(slot, carry, ref=ref, at=at, height=height):
            start = pl.multiple_of(scal_ref[at + slot] * 8, 8)
            for tile in range(TILES):
                lanes = slice(tile * LANES, (tile + 1) * LANES)
                rows_ref[tile, pl.ds(start, height), :] += ref[slot, :, lanes].astype(F32)
            return carry

        lax.fori_loop(0, slots, one, 0)
        at += slots


def emit(scal_ref, base, out_refs, stage_refs, sem_refs, rows_ref):
    at = base
    for out_ref, ref, sem in zip(out_refs, stage_refs, sem_refs):
        slots, height = ref.shape[0], ref.shape[1]

        def one(slot, carry, out_ref=out_ref, ref=ref, sem=sem, at=at, height=height):
            start = pl.multiple_of(scal_ref[at + slot] * 8, 8)
            for tile in range(TILES):
                ref[slot, :, lanes_of(tile)] = rows_ref[tile, pl.ds(start, height), :].astype(ref.dtype)
            pltpu.make_async_copy(ref.at[slot], out_ref.at[slot], sem).start()
            return carry

        lax.fori_loop(0, slots, one, 0)
        at += slots
    for out_ref, ref, sem in zip(out_refs, stage_refs, sem_refs):
        pltpu.make_async_copy(ref, out_ref, sem).wait()


def lanes_of(tile, offset=0):
    return slice(offset + tile * LANES, offset + (tile + 1) * LANES)


def forward_kernel(n_pieces, scal_ref, cond_ref, x_ref, *refs):
    pieces = refs[:n_pieces]
    mod_ref, ada_hbm_ref, qkv_w_ref, proj_ref, bias_ref, qkv_ref, probs_ref, mixed_ref, branch_ref = refs[
        n_pieces : n_pieces + 9
    ]
    rows_ref, score_ref, ada_ref, ada_sem = refs[n_pieces + 9 :]
    store = pltpu.make_async_copy(ada_ref, ada_hbm_ref, ada_sem)
    step = pl.program_id(0)
    group, seq = x_ref.shape[0], x_ref.shape[1]

    @pl.when(step == 0)
    def _():
        assemble(scal_ref, 1, pieces, rows_ref)
        for tile in range(TILES):
            proj_ref[:, lanes_of(tile)] = rows_ref[tile, pl.ds(PROJ_AT, D), :].astype(BF16)
            bias_ref[:, lanes_of(tile)] = rows_ref[tile, pl.ds(B_ADA_AT, 8), :]
            for block in range(6):
                ada_ref[block, :, lanes_of(tile)] = rows_ref[
                    tile, pl.ds(ADA_AT + block, D, stride=6), :
                ].astype(BF16)
            for block in range(3):
                qkv_w_ref[:, lanes_of(tile, block * D)] = rows_ref[
                    tile, pl.ds(QKV_AT + block, D, stride=3), :
                ].astype(BF16)
        store.start()
        act = jax.nn.silu(cond_ref[...].astype(F32)).astype(BF16)
        for block in range(6):
            mod_ref[block] = mm(act, ada_ref[block]) + bias_ref[block : block + 1, :]

    @pl.when(step * group < scal_ref[0])
    def _():
        masks = head_masks()
        values = x_ref[...].astype(F32)
        normed, _ = normalize(values)
        shift, scale = [mod_rows(mod_ref, part, step, group) for part in range(2)]
        modulated = flat(normed * (1.0 + scale) + shift).astype(BF16)
        qkv = mm(modulated, qkv_w_ref[...])
        queries = (qkv[:, :D] + bias_ref[6:7, :]).astype(BF16)
        keys_all = qkv[:, D : 2 * D].astype(BF16)
        values_all = (qkv[:, 2 * D :] + bias_ref[7:8, :]).astype(BF16)
        for latent in range(group):
            tokens = slice(latent * seq, (latent + 1) * seq)
            qkv_ref[latent, :, :D] = queries[tokens]
            qkv_ref[latent, :, D : 2 * D] = keys_all[tokens]
            qkv_ref[latent, :, 2 * D :] = values_all[tokens]
            for head in range(HEADS):
                lanes = lanes_of(head // 2)
                own = queries[tokens, lanes] * (masks[head % 2] * FACTOR)
                score_ref[latent, head] = mm_nt(keys_all[tokens, lanes], own)
        for latent in range(group):
            tokens = slice(latent * seq, (latent + 1) * seq)
            values_t = values_all[tokens].T
            for head in range(HEADS):
                scores = score_ref[latent, head]
                expo = jnp.exp(scores - jnp.max(scores, axis=0, keepdims=True))
                probs_ref[latent, head] = (expo * (1.0 / col_sum(expo))).astype(BF16)
            for head in range(HEADS):
                rows = slice(head * HEAD_DIM, (head + 1) * HEAD_DIM)
                mixed_ref[latent, rows, :] = mm(values_t[rows, :], probs_ref[latent, head]).astype(BF16)
            branch_ref[latent] = mm_tn(mixed_ref[latent], proj_ref[...])

    @pl.when(step == pl.num_programs(0) - 1)
    def _():
        store.wait()


def mlp_kernel(n_pieces, n_out, scal_ref, mod_ref, proj_ref, x_ref, branch_ref, mixed_ref, cot_ref, *refs):
    pieces = refs[:n_pieces]
    outs = refs[n_pieces : n_pieces + 5 + n_out]
    out_ref, dx_ref, dmixed_ref, dmod_ref, dproj_ref = outs[:5]
    send_refs = outs[5:]
    scratch = refs[n_pieces + 5 + n_out :]
    rows_ref, fc1_ref, fc2_ref, bias_ref, act_ref, slope_ref, du_ref, dfc1_ref, dfc2_ref, dbias_ref = scratch[:10]
    stage_refs, sem_refs = scratch[10 : 10 + n_out], scratch[10 + n_out :]
    step = pl.program_id(0)
    last = pl.num_programs(0) - 1

    @pl.when(step == 0)
    def _():
        assemble(scal_ref, 1, pieces, rows_ref)
        for block in range(4):
            for tile in range(TILES):
                fc1_ref[:, lanes_of(tile, block * D)] = rows_ref[
                    tile, pl.ds(FC1_AT + block, D, stride=4), :
                ].astype(BF16)
                bias_ref[0:1, lanes_of(tile, block * D)] = rows_ref[tile, pl.ds(B_FC1_AT + block, 1), :]
        for tile in range(TILES):
            fc2_ref[:, lanes_of(tile)] = rows_ref[tile, pl.ds(FC2_AT, FF), :].astype(BF16)
            bias_ref[1:2, lanes_of(tile)] = rows_ref[tile, pl.ds(B_FC2_AT, 1), :]
            bias_ref[2:3, lanes_of(tile)] = rows_ref[tile, pl.ds(B_PROJ_AT, 1), :]
        dfc1_ref[...] = jnp.zeros_like(dfc1_ref)
        dfc2_ref[...] = jnp.zeros_like(dfc2_ref)
        dbias_ref[...] = jnp.zeros_like(dbias_ref)
        dproj_ref[...] = jnp.zeros_like(dproj_ref)
        dmod_ref[...] = jnp.zeros_like(dmod_ref)

    group, seq = x_ref.shape[0], x_ref.shape[1]

    @pl.when(step * group < scal_ref[0])
    def _():
        gate_one, shift, scale, gate_two = [mod_rows(mod_ref, 2 + part, step, group) for part in range(4)]
        slot = step * group + lax.broadcasted_iota(jnp.int32, (group, 1, 1), 0)
        live = (slot < scal_ref[0]).astype(F32)
        branch_one = branch_ref[...] + bias_ref[2:3, :D]
        middle = x_ref[...].astype(F32) + gate_one * branch_one
        normed, rstd = normalize(middle)
        modulated = flat(normed * (1.0 + scale) + shift).astype(BF16)
        chunk = CHUNK
        for start in range(0, FF, chunk):
            part = slice(start, start + chunk)
            pre = mm(modulated, fc1_ref[:, part]) + bias_ref[0:1, part]
            square = pre * pre
            bend = jnp.tanh(pre * (GELU_A + (GELU_A * GELU_B) * square))
            half = 0.5 + 0.5 * bend
            act = (pre * half).astype(BF16)
            act_ref[:, part] = act
            slope_ref[:, part] = half + (pre * (0.5 - 0.5 * bend * bend)) * (
                GELU_A + (3.0 * GELU_A * GELU_B) * square
            )
        branch_two = mm(act_ref[...], fc2_ref[...])
        branch_two = (branch_two + bias_ref[1:2, :D]).reshape(group, seq, D)
        out_ref[...] = (live * (middle + gate_two * branch_two)).astype(BF16)
        grad_out = live * cot_ref[...].astype(F32)
        put_mod(dmod_ref, 3, step, grad_out * branch_two)
        grad_two = flat(gate_two * grad_out).astype(BF16)
        dbias_ref[1:2, :D] += col_sum(grad_two.astype(F32))
        grad_two_t = grad_two.T
        modulated_t = modulated.T
        for start in range(0, FF, chunk):
            part = slice(start, start + chunk)
            du = (mm_nt(grad_two, fc2_ref[part, :]) * slope_ref[:, part]).astype(BF16)
            dbias_ref[0:1, part] += col_sum(du.astype(F32))
            du_ref[:, part] = du
        grad_mod = mm_nt(du_ref[...], fc1_ref[...]).reshape(group, seq, D)
        dfc2_ref[...] += mm(grad_two_t, act_ref[...])
        dfc1_ref[...] += mm(modulated_t, du_ref[...])
        put_mod(dmod_ref, 1, step, grad_mod)
        put_mod(dmod_ref, 2, step, grad_mod * normed)
        grad_middle = grad_out + normalize_back(grad_mod * (1.0 + scale), normed, rstd)
        dx_ref[...] = grad_middle
        put_mod(dmod_ref, 0, step, grad_middle * branch_one)
        grad_one = flat(gate_one * grad_middle).astype(BF16)
        dbias_ref[2:3, :D] += col_sum(grad_one.astype(F32))
        grad_mixed = mm_nt(grad_one, proj_ref[...]).astype(BF16)
        for latent in range(group):
            tokens = slice(latent * seq, (latent + 1) * seq)
            dproj_ref[...] += mm(mixed_ref[latent], grad_one[tokens])
            dmixed_ref[latent] = grad_mixed[tokens]

    @pl.when(step * group >= scal_ref[0])
    def _():
        out_ref[...] = jnp.zeros_like(out_ref)
        dx_ref[...] = jnp.zeros_like(dx_ref)
        dmixed_ref[...] = jnp.zeros_like(dmixed_ref)

    @pl.when(step == last)
    def _():
        for block in range(4):
            for tile in range(TILES):
                rows_ref[tile, pl.ds(FC1_AT + block, D, stride=4), :] = dfc1_ref[
                    :, lanes_of(tile, block * D)
                ]
                rows_ref[tile, pl.ds(B_FC1_AT + block, 1), :] = dbias_ref[0:1, lanes_of(tile, block * D)]
        for tile in range(TILES):
            rows_ref[tile, pl.ds(FC2_AT, FF), :] = dfc2_ref[lanes_of(tile), :].T
            rows_ref[tile, pl.ds(B_FC2_AT, 1), :] = dbias_ref[1:2, lanes_of(tile)]
            rows_ref[tile, pl.ds(B_PROJ_AT, 1), :] = dbias_ref[2:3, lanes_of(tile)]
        emit(scal_ref, 1 + sum(ref.shape[0] for ref in pieces), send_refs, stage_refs, sem_refs, rows_ref)


def attend_back_kernel(scal_ref, qkv_ref, probs_ref, dmixed_ref, dqkv_ref, dprobs_ref, low_ref, dq_t_ref):
    group, seq = qkv_ref.shape[0], qkv_ref.shape[1]

    @pl.when(pl.program_id(0) * group < scal_ref[0])
    def _():
        masks = head_masks()
        for latent in range(group):
            keys_t = qkv_ref[latent, :, D : 2 * D].T
            for head in range(HEADS):
                own = dmixed_ref[latent, :, lanes_of(head // 2)] * masks[head % 2]
                dprobs_ref[head] = mm_nt(qkv_ref[latent, :, lanes_of(head // 2, 2 * D)], own)
            for head in range(HEADS):
                probs, grad_probs = probs_ref[latent, head].astype(F32), dprobs_ref[head]
                low_ref[head] = (probs * (grad_probs - col_sum(probs * grad_probs))).astype(BF16)
            for pair in range(HEADS // 2):
                query = qkv_ref[latent, :, lanes_of(pair)]
                grad = dmixed_ref[latent, :, lanes_of(pair)]
                grad_key = jnp.zeros((seq, LANES), F32)
                grad_value = jnp.zeros((seq, LANES), F32)
                for half in range(2):
                    head = 2 * pair + half
                    rows = slice(head * HEAD_DIM, (head + 1) * HEAD_DIM)
                    grad_value += mm(probs_ref[latent, head], grad * masks[half])
                    grad_key += mm(low_ref[head], query * masks[half])
                    dq_t_ref[rows, :] = mm(keys_t[rows, :], low_ref[head])
                dqkv_ref[latent, :, lanes_of(pair, D)] = (grad_key * FACTOR).astype(BF16)
                dqkv_ref[latent, :, lanes_of(pair, 2 * D)] = grad_value.astype(BF16)
            dqkv_ref[latent, :, :D] = (dq_t_ref[...] * FACTOR).astype(BF16).T


def finish_kernel(
    n_out, base, scal_ref, mod_ref, qkv_w_ref, cond_ref, ada_hbm_ref, dmod_in_ref, dproj_ref,
    x_ref, dqkv_ref, dx_ref, *refs
):
    grad_x_ref, grad_cond_ref = refs[:2]
    send_refs = refs[2 : 2 + n_out]
    scratch = refs[2 + n_out :]
    rows_ref, dqkv_w_ref, dmod_ref, dbias_ref, ada_ref, ada_sem = scratch[:6]
    stage_refs, sem_refs = scratch[6 : 6 + n_out], scratch[6 + n_out :]
    fetch = pltpu.make_async_copy(ada_hbm_ref, ada_ref, ada_sem)
    step = pl.program_id(0)
    last = pl.num_programs(0) - 1
    group, seq = x_ref.shape[0], x_ref.shape[1]

    @pl.when(step == 0)
    def _():
        fetch.start()
        dqkv_w_ref[...] = jnp.zeros_like(dqkv_w_ref)
        dmod_ref[...] = jnp.zeros_like(dmod_ref)
        dbias_ref[...] = jnp.zeros_like(dbias_ref)

    @pl.when(step * group < scal_ref[0])
    def _():
        shift, scale = [mod_rows(mod_ref, part, step, group) for part in range(2)]
        normed, rstd = normalize(x_ref[...].astype(F32))
        modulated = flat(normed * (1.0 + scale) + shift).astype(BF16)
        grad_qkv = flat(dqkv_ref[...])
        dbias_ref[0:1, :] += col_sum(grad_qkv.astype(F32))
        dqkv_w_ref[...] += mm(modulated.T, grad_qkv)
        grad_mod = mm_nt(grad_qkv, qkv_w_ref[...]).reshape(group, seq, D)
        put_mod(dmod_ref, 0, step, grad_mod)
        put_mod(dmod_ref, 1, step, grad_mod * normed)
        grad_x_ref[...] = dx_ref[...] + normalize_back(grad_mod * (1.0 + scale), normed, rstd)

    @pl.when(step * group >= scal_ref[0])
    def _():
        grad_x_ref[...] = jnp.zeros_like(grad_x_ref)

    @pl.when(step == last)
    def _():
        fetch.wait()
        cond = cond_ref[...].astype(F32)
        gate = jax.nn.sigmoid(cond)
        act = (cond * gate).astype(BF16)
        grad_act = jnp.zeros_like(cond)
        for block in range(6):
            grad = (dmod_ref[block] if block < 2 else dmod_in_ref[block - 2]).astype(BF16)
            grad_act += mm_nt(grad, ada_ref[block])
            weight = mm_tn(act, grad)
            bias = col_sum(grad.astype(F32))
            for tile in range(TILES):
                rows_ref[tile, pl.ds(ADA_AT + block, D, stride=6), :] = weight[:, lanes_of(tile)]
                rows_ref[tile, pl.ds(B_ADA_AT + block, 1), :] = bias[:, lanes_of(tile)]
        grad_cond_ref[...] = grad_act * (gate * (1.0 + cond * (1.0 - gate)))
        for tile in range(TILES):
            for block in range(3):
                rows_ref[tile, pl.ds(QKV_AT + block, D, stride=3), :] = dqkv_w_ref[
                    :, lanes_of(tile, block * D)
                ]
            rows_ref[tile, pl.ds(PROJ_AT, D), :] = dproj_ref[:, lanes_of(tile)]
            rows_ref[tile, pl.ds(B_QV_AT, 1), :] = dbias_ref[0:1, lanes_of(tile)]
            rows_ref[tile, pl.ds(B_QV_AT + 1, 1), :] = dbias_ref[0:1, lanes_of(tile, 2 * D)]
        emit(scal_ref, base, send_refs, stage_refs, sem_refs, rows_ref)


class Direct:
    def __init__(self, count, me):
        self.count, self.me = count, me
        self.gathered = self.sent = [jnp.int32(index) for index in range(count)]
        self.slots = [(count, F32)]

    def start(self, piece):
        return piece

    def gather(self, piece):
        return [lax.all_gather(piece, AXIS, axis=0)]

    def pass_on(self, held):
        return held

    def join(self, own, others):
        return own

    def begin(self, parts):
        return parts

    middle = send = begin

    def end(self, parts):
        return lax.psum_scatter(parts[0], AXIS, scatter_dimension=0)


class Stages:
    def __init__(self, count, me):
        self.me = me
        core, x, y, z = me % 2, me // 2 % 2, me // 4 % 2, me // 8

        def device(dz, dy, dx, dc):
            return (((z + dz) % 4 * 2 + (y + dy) % 2) * 2 + (x + dx) % 2) * 2 + (core + dc) % 2

        self.order(device)

    def order(self, device):
        gathered = []
        for dc in range(2):
            gathered += [device(-k, 0, 0, dc) for k in (0, 1, 2, 3)]
            gathered += [device(-k, 0, 1, dc) for k in (0, 1)]
            gathered += [device(-k, 1, 0, dc) for k in (2, 3)]
            gathered += [device(-k, 1, dx, dc) for dx in (0, 1) for k in (0, 1)]
            gathered += [device(-k, dy, 1, dc) for dy in (0, 1) for k in (2, 3)]
        self.gathered = gathered
        sent = []
        for dc in (1, 0):
            sent += [device(k, dy, dx, dc) for dx in (0, 1) for k in (0, 1) for dy in (0, 1)]
            sent += [device(k, dy, dx, dc) for dy in (0, 1) for k in (2, 3) for dx in (0, 1)]
        self.sent = sent
        self.slots = [(8, BF16)] * 4

    def shift(self, values, dz=0, dy=0, dx=0, dc=0):
        pairs = []
        for source in range(32):
            core, x, y, z = source % 2, source // 2 % 2, source // 4 % 2, source // 8
            target = (((z + dz) % 4 * 2 + (y + dy) % 2) * 2 + (x + dx) % 2) * 2 + (core + dc) % 2
            pairs.append((source, target))
        return lax.ppermute(values, AXIS, pairs)

    def start(self, piece):
        return jnp.stack([piece] + [self.shift(piece, dz=k) for k in (1, 2, 3)])

    def gather(self, own):
        first, second = own[:2], own[2:]
        by_x = self.shift(first, dx=1)
        by_y = self.shift(second, dy=1)
        by_xy = self.shift(jnp.concatenate([first, by_x]), dy=1)
        by_yx = self.shift(jnp.concatenate([second, by_y]), dx=1)
        return [own, by_x, by_y, by_xy, by_yx, jnp.concatenate([own, by_x, by_y])]

    def pass_on(self, held):
        early = held[-1]
        held = held[:-1]
        return held + [self.shift(array, dc=1) for array in (early, *held[3:])]

    def begin(self, parts):
        send_a, send_b, keep_a, keep_b = parts
        return self.shift(send_a, dc=1), self.shift(send_b, dc=1), keep_a, keep_b

    def middle(self, state):
        got_a, got_b, keep_a, keep_b = state
        shape = keep_a.shape[1:]
        sum_a = (keep_a.astype(F32) + got_a.astype(F32)).reshape((2, 4) + shape)
        sum_b = (keep_b.astype(F32) + got_b.astype(F32)).reshape((2, 4) + shape)
        return sum_a[0], sum_b[0], sum_a[1].astype(BF16), sum_b[1].astype(BF16)

    def send(self, state):
        sum_a, sum_b, out_a, out_b = state
        return sum_a, sum_b, self.shift(out_a, dx=1), self.shift(out_b, dy=1)

    def end(self, state):
        def swap(values, **how):
            return self.shift(values.astype(BF16), **how).astype(F32)

        sum_a, sum_b, got_a, got_b = state
        shape = sum_a.shape[1:]
        sum_a = (sum_a + got_a.astype(F32)).reshape((2, 2) + shape)
        sum_b = (sum_b + got_b.astype(F32)).reshape((2, 2) + shape)
        sum_a = sum_a[:, 0] + swap(sum_a[:, 1], dy=1)
        sum_b = sum_b[:, 0] + swap(sum_b[:, 1], dx=1)
        return (
            sum_a[0] + swap(sum_a[1], dz=1) + swap(sum_b[0], dz=2) + swap(sum_b[1], dz=3)
        )


class Straight(Stages):
    def order(self, device):
        sides = [(0, 0), (0, 1), (1, 0), (1, 1)]
        self.gathered = [device(-k, dy, dx, dc) for dc in (0, 1) for dy, dx in sides for k in range(4)]
        self.sent = [device(k, dy, dx, dc) for dc in (1, 0) for dy, dx in sides for k in range(4)]
        self.slots = [(16, BF16)] * 2

    def pass_on(self, held):
        return held + [self.shift(array, dc=1) for array in held]

    def join(self, own, others):
        half = len(others) // 2
        return own[:1] + others[:half] + own[1:] + others[half:]

    def gather(self, own):
        return [own, self.shift(own, dx=1), self.shift(own, dy=1), self.shift(own, dx=1, dy=1)]

    def begin(self, parts):
        return self.shift(parts[0], dc=1), parts[1]

    def middle(self, state):
        got, keep = state
        total = (keep.astype(F32) + got.astype(F32)).reshape((4, 4) + keep.shape[1:])
        return total[0], total[1].astype(BF16), total[2].astype(BF16), total[3].astype(BF16)

    def send(self, state):
        total, by_x, by_y, by_both = state
        return total, self.shift(by_x, dx=1), self.shift(by_y, dy=1), self.shift(by_both, dx=1, dy=1)

    def end(self, state):
        total = state[0]
        for got in state[1:]:
            total = total + got.astype(F32)
        low = total[1:].astype(BF16)
        out = total[0]
        for k in (1, 2, 3):
            out = out + self.shift(low[k - 1], dz=k).astype(F32)
        return out


def to_piece(share, rows, me):
    size = share.shape[0]
    flat = jnp.zeros((rows * D,), share.dtype)
    return lax.dynamic_update_slice(flat, share, (size * me % GROUP,)).reshape(rows, D)


def from_piece(piece, size, me):
    return lax.dynamic_slice(piece.reshape(-1), (size * me % GROUP,), (size,))


def whole(shape=None):
    return pl.BlockSpec(memory_space=pltpu.VMEM)


def by_latent(group, *shape):
    zeros = (0,) * len(shape)
    return pl.BlockSpec((group,) + shape, lambda step, scal: (step,) + zeros)


def call(kernel, count, in_specs, out_specs, out_shape, scratch, args, flops):
    return pl.pallas_call(
        kernel,
        grid_spec=pltpu.PrefetchScalarGridSpec(
            num_scalar_prefetch=1,
            grid=(count,),
            in_specs=in_specs,
            out_specs=out_specs,
            scratch_shapes=scratch,
        ),
        out_shape=out_shape,
        compiler_params=pltpu.CompilerParams(
            vmem_limit_bytes=60 * 2**20, dimension_semantics=("arbitrary",)
        ),
        cost_estimate=pl.CostEstimate(flops=flops, bytes_accessed=20 * 2**20, transcendentals=0),
    )(*args)


def solution(mesh):
    devices = mesh.shape[AXIS]

    def body(latents, condition, attn_params, mlp_params, counts, cotangent):
        count, seq = latents.shape[0], latents.shape[1]
        me = lax.axis_index(AXIS)
        known = devices == 32
        plan = (Stages if known else Direct)(devices, me)
        mlp_plan = (Straight if known else Direct)(devices, me)
        attn_size, mlp_size = attn_params.shape[0], mlp_params.shape[0]
        attn_height = piece_rows(attn_size, devices)
        mlp_height = piece_rows(mlp_size, devices)

        def scalars(size, order):
            ids = jnp.stack(order.gathered + order.sent)
            return jnp.concatenate([counts.astype(jnp.int32), size * ids // GROUP]).astype(jnp.int32)

        attn_scal, mlp_scal = scalars(attn_size, plan), scalars(mlp_size, mlp_plan)
        attn_own, mlp_piece = plan.start(to_piece(attn_params, attn_height, me)), to_piece(mlp_params, mlp_height, me)
        attn_own, mlp_piece = lax.optimization_barrier((attn_own, mlp_piece))
        attn_pieces = plan.gather(attn_own)
        mlp_own = mlp_plan.start(mlp_piece)
        mlp_own, attn_pieces, attn_scal, mlp_scal = lax.optimization_barrier(
            (mlp_own, attn_pieces, attn_scal, mlp_scal)
        )
        attn_pieces = plan.pass_on(attn_pieces)
        mlp_pieces = mlp_plan.gather(mlp_own)

        def struct(shape, kind):
            return jax.ShapeDtypeStruct(shape, kind)

        n_pieces = len(attn_pieces)
        n_mlp_pieces = len(mlp_pieces) * (2 if known else 1)
        n_out, n_mlp_out = len(plan.slots), len(mlp_plan.slots)
        mod, ada, qkv_w, proj, _, qkv, probs, mixed, branch = call(
            lambda *refs: forward_kernel(n_pieces, *refs),
            count // FORWARD_STEP,
            [whole(), by_latent(FORWARD_STEP, seq, D)] + [whole()] * n_pieces,
            [whole(), pl.BlockSpec(memory_space=pl.ANY)] + [whole()] * 3
            + [
                by_latent(FORWARD_STEP, seq, 3 * D),
                by_latent(FORWARD_STEP, HEADS, seq, seq),
                by_latent(FORWARD_STEP, D, seq),
                by_latent(FORWARD_STEP, seq, D),
            ],
            [
                struct((6, count, D), F32),
                struct((6, D, D), BF16),
                struct((D, 3 * D), BF16),
                struct((D, D), BF16),
                struct((8, D), F32),
                struct((count, seq, 3 * D), BF16),
                struct((count, HEADS, seq, seq), BF16),
                struct((count, D, seq), BF16),
                struct((count, seq, D), F32),
            ],
            [
                pltpu.VMEM((TILES, ATTN_ROWS + attn_height, LANES), F32),
                pltpu.VMEM((FORWARD_STEP, HEADS, seq, seq), F32),
                pltpu.VMEM((6, D, D), BF16),
                pltpu.SemaphoreType.DMA,
            ],
            [attn_scal, condition, latents] + attn_pieces,
            15 * 10**9,
        )
        mlp_own = mlp_plan.pass_on(mlp_pieces[:1])
        mlp_pieces, mod = lax.optimization_barrier((mlp_pieces[1:], mod))
        mlp_pieces = mlp_plan.join(mlp_own, mlp_plan.pass_on(mlp_pieces))
        results = call(
            lambda *refs: mlp_kernel(n_mlp_pieces, n_mlp_out, *refs),
            count // MLP_STEP,
            [whole(), whole(), by_latent(MLP_STEP, seq, D), by_latent(MLP_STEP, seq, D), by_latent(MLP_STEP, D, seq), by_latent(MLP_STEP, seq, D)]
            + [whole()] * n_mlp_pieces,
            [by_latent(MLP_STEP, seq, D), by_latent(MLP_STEP, seq, D), by_latent(MLP_STEP, seq, D), whole(), whole()]
            + [pl.BlockSpec(memory_space=pl.ANY)] * n_mlp_out,
            [
                struct((count, seq, D), BF16),
                struct((count, seq, D), F32),
                struct((count, seq, D), BF16),
                struct((4, count, D), F32),
                struct((D, D), F32),
            ]
            + [struct((slots, mlp_height, D), kind) for slots, kind in mlp_plan.slots],
            [
                pltpu.VMEM((TILES, MLP_ROWS + 2 + mlp_height, LANES), F32),
                pltpu.VMEM((D, FF), BF16),
                pltpu.VMEM((FF, D), BF16),
                pltpu.VMEM((8, FF), F32),
                pltpu.VMEM((MLP_STEP * seq, FF), BF16),
                pltpu.VMEM((MLP_STEP * seq, FF), F32),
                pltpu.VMEM((MLP_STEP * seq, FF), BF16),
                pltpu.VMEM((D, FF), F32),
                pltpu.VMEM((D, FF), F32),
                pltpu.VMEM((8, FF), F32),
            ]
            + [pltpu.VMEM((slots, mlp_height, D), kind) for slots, kind in mlp_plan.slots]
            + [pltpu.SemaphoreType.DMA] * n_mlp_out,
            [mlp_scal, mod, proj, latents, branch, mixed, cotangent] + mlp_pieces,
            30 * 10**9,
        )
        output, grad_middle, grad_mixed, dmod, dproj = results[:5]
        sums = mlp_plan.begin(results[5:])
        grad_qkv, = call(
            attend_back_kernel,
            count // ATTEND_STEP,
            [by_latent(ATTEND_STEP, seq, 3 * D), by_latent(ATTEND_STEP, HEADS, seq, seq), by_latent(ATTEND_STEP, seq, D)],
            [by_latent(ATTEND_STEP, seq, 3 * D)],
            [struct((count, seq, 3 * D), BF16)],
            [
                pltpu.VMEM((HEADS, seq, seq), F32),
                pltpu.VMEM((HEADS, seq, seq), BF16),
                pltpu.VMEM((D, seq), F32),
            ],
            [attn_scal, qkv, probs, grad_mixed],
            13 * 10**9,
        )
        sums, grad_qkv = lax.optimization_barrier((sums, grad_qkv))
        sums = mlp_plan.middle(sums)
        sums, grad_qkv = lax.optimization_barrier((sums, grad_qkv))
        sums = mlp_plan.send(sums)
        results = call(
            lambda *refs: finish_kernel(n_out, 1 + devices, *refs),
            count // FINISH_STEP,
            [whole()] * 3 + [pl.BlockSpec(memory_space=pl.ANY)] + [whole()] * 2 + [by_latent(FINISH_STEP, seq, D), by_latent(FINISH_STEP, seq, 3 * D), by_latent(FINISH_STEP, seq, D)],
            [by_latent(FINISH_STEP, seq, D), whole()] + [pl.BlockSpec(memory_space=pl.ANY)] * n_out,
            [struct((count, seq, D), F32), struct((count, D), F32)]
            + [struct((slots, attn_height, D), kind) for slots, kind in plan.slots],
            [
                pltpu.VMEM((TILES, ATTN_ROWS + attn_height, LANES), F32),
                pltpu.VMEM((D, 3 * D), F32),
                pltpu.VMEM((2, count, D), F32),
                pltpu.VMEM((8, 3 * D), F32),
                pltpu.VMEM((6, D, D), BF16),
                pltpu.SemaphoreType.DMA,
            ]
            + [pltpu.VMEM((slots, attn_height, D), kind) for slots, kind in plan.slots]
            + [pltpu.SemaphoreType.DMA] * n_out,
            [attn_scal, mod, qkv_w, condition, ada, dmod, dproj, latents, grad_qkv, grad_middle],
            15 * 10**9,
        )
        grad_latents, grad_condition = results[:2]
        sums, attn_parts = lax.optimization_barrier((sums, results[2:]))
        attn_parts = plan.middle(plan.begin(attn_parts))
        out_last, sums = lax.optimization_barrier((attn_parts[-1], sums))
        grad_attn = plan.end(plan.send([*attn_parts[:-1], out_last]))
        grad_mlp = mlp_plan.end(sums)
        return (
            output,
            grad_latents,
            grad_condition,
            from_piece(grad_attn, attn_size, me),
            from_piece(grad_mlp, mlp_size, me),
        )

    in_specs = (
        P(AXIS, None, None),
        P(AXIS, None),
        P(AXIS),
        P(AXIS),
        P(AXIS),
        P(AXIS, None, None),
    )
    out_specs = (
        P(AXIS, None, None),
        P(AXIS, None, None),
        P(AXIS, None),
        P(AXIS),
        P(AXIS),
    )
    return jax.shard_map(body, mesh=mesh, in_specs=in_specs, out_specs=out_specs, check_vma=False)
```

```python
import jax
import jax.numpy as jnp
from jax import lax
from jax.experimental import pallas as pl
from jax.experimental.pallas import tpu as pltpu
from jax.sharding import PartitionSpec as P

D = 384
HEADS = 6
HEAD_DIM = 64
FF = 1536
EPSILON = 1e-06
AXIS = "fsdp"
LANES = 128
TILES = D // LANES
GROUP = 8 * D
FACTOR = HEAD_DIM ** (-0.5)
GELU_A = 0.7978845608028654
GELU_B = 0.044715
CHUNK = 1536
FORWARD_STEP = 2
MLP_STEP = 2
ATTEND_STEP = 2
FINISH_STEP = 2

ADA_AT = 0
QKV_AT = 6 * D
PROJ_AT = 9 * D
B_ADA_AT = 10 * D
B_QV_AT = 10 * D + 6
ATTN_ROWS = 10 * D + 8
FC1_AT = 0
FC2_AT = FF
B_FC1_AT = 2 * FF
B_FC2_AT = 2 * FF + 4
B_PROJ_AT = 2 * FF + 5
MLP_ROWS = 2 * FF + 6

F32 = jnp.float32
BF16 = jnp.bfloat16


def round_up(value, unit):
    return -(-value // unit) * unit


def piece_rows(share, count):
    lead = max((share * index) % GROUP for index in range(count))
    return round_up(-(-(share + lead) // D), 16)


def mm(left, right):
    return jnp.dot(left, right, preferred_element_type=F32)


def mm_nt(left, right):
    return lax.dot_general(left, right, (((1,), (1,)), ((), ())), preferred_element_type=F32)


def mm_tn(left, right):
    return lax.dot_general(left, right, (((0,), (0,)), ((), ())), preferred_element_type=F32)


def col_sum(values):
    return jnp.sum(values, axis=0, keepdims=True)


def row_mean(values):
    return jnp.mean(values, axis=-1, keepdims=True)


def normalize(values):
    centered = values - row_mean(values)
    rstd = lax.rsqrt(row_mean(centered * centered) + EPSILON)
    return centered * rstd, rstd


def normalize_back(grad, normed, rstd):
    return rstd * (grad - row_mean(grad) - normed * row_mean(grad * normed))


def flat(values):
    return values.reshape(-1, values.shape[-1])


def mod_rows(mod_ref, part, step, group):
    rows = [mod_ref[part, pl.ds(step * group + latent, 1), :] for latent in range(group)]
    return jnp.stack(rows)


def put_mod(ref, part, step, values):
    for latent in range(values.shape[0]):
        ref[part, pl.ds(step * values.shape[0] + latent, 1), :] = col_sum(values[latent])


def head_masks():
    lane = lax.broadcasted_iota(jnp.int32, (1, LANES), 1) // HEAD_DIM
    return [(lane == head).astype(F32).astype(BF16) for head in range(2)]


def assemble(scal_ref, base, piece_refs, rows_ref):
    rows_ref[...] = jnp.zeros_like(rows_ref)
    at = base
    for ref in piece_refs:
        slots, height = ref.shape[0], ref.shape[1]

        def one(slot, carry, ref=ref, at=at, height=height):
            start = pl.multiple_of(scal_ref[at + slot] * 8, 8)
            for tile in range(TILES):
                lanes = slice(tile * LANES, (tile + 1) * LANES)
                rows_ref[tile, pl.ds(start, height), :] += ref[slot, :, lanes].astype(F32)
            return carry

        lax.fori_loop(0, slots, one, 0)
        at += slots


def emit(scal_ref, base, out_refs, stage_refs, sem_refs, rows_ref):
    at = base
    for out_ref, ref, sem in zip(out_refs, stage_refs, sem_refs):
        slots, height = ref.shape[0], ref.shape[1]

        def one(slot, carry, out_ref=out_ref, ref=ref, sem=sem, at=at, height=height):
            start = pl.multiple_of(scal_ref[at + slot] * 8, 8)
            for tile in range(TILES):
                ref[slot, :, lanes_of(tile)] = rows_ref[tile, pl.ds(start, height), :].astype(ref.dtype)
            pltpu.make_async_copy(ref.at[slot], out_ref.at[slot], sem).start()
            return carry

        lax.fori_loop(0, slots, one, 0)
        at += slots
    for out_ref, ref, sem in zip(out_refs, stage_refs, sem_refs):
        pltpu.make_async_copy(ref, out_ref, sem).wait()


def lanes_of(tile, offset=0):
    return slice(offset + tile * LANES, offset + (tile + 1) * LANES)


def forward_kernel(n_pieces, scal_ref, cond_ref, x_ref, *refs):
    pieces = refs[:n_pieces]
    mod_ref, ada_hbm_ref, qkv_w_ref, proj_ref, bias_ref, qkv_ref, probs_ref, mixed_ref, branch_ref = refs[
        n_pieces : n_pieces + 9
    ]
    rows_ref, score_ref, ada_ref, ada_sem = refs[n_pieces + 9 :]
    store = pltpu.make_async_copy(ada_ref, ada_hbm_ref, ada_sem)
    step = pl.program_id(0)
    group, seq = x_ref.shape[0], x_ref.shape[1]

    @pl.when(step == 0)
    def _():
        assemble(scal_ref, 1, pieces, rows_ref)
        for tile in range(TILES):
            proj_ref[:, lanes_of(tile)] = rows_ref[tile, pl.ds(PROJ_AT, D), :].astype(BF16)
            bias_ref[:, lanes_of(tile)] = rows_ref[tile, pl.ds(B_ADA_AT, 8), :]
            for block in range(6):
                ada_ref[block, :, lanes_of(tile)] = rows_ref[
                    tile, pl.ds(ADA_AT + block, D, stride=6), :
                ].astype(BF16)
            for block in range(3):
                qkv_w_ref[:, lanes_of(tile, block * D)] = rows_ref[
                    tile, pl.ds(QKV_AT + block, D, stride=3), :
                ].astype(BF16)
        store.start()
        act = jax.nn.silu(cond_ref[...].astype(F32)).astype(BF16)
        for block in range(6):
            mod_ref[block] = mm(act, ada_ref[block]) + bias_ref[block : block + 1, :]

    @pl.when(step * group < scal_ref[0])
    def _():
        masks = head_masks()
        values = x_ref[...].astype(F32)
        normed, _ = normalize(values)
        shift, scale = [mod_rows(mod_ref, part, step, group) for part in range(2)]
        modulated = flat(normed * (1.0 + scale) + shift).astype(BF16)
        qkv = mm(modulated, qkv_w_ref[...])
        queries = (qkv[:, :D] + bias_ref[6:7, :]).astype(BF16)
        keys_all = qkv[:, D : 2 * D].astype(BF16)
        values_all = (qkv[:, 2 * D :] + bias_ref[7:8, :]).astype(BF16)
        for latent in range(group):
            tokens = slice(latent * seq, (latent + 1) * seq)
            qkv_ref[latent, :, :D] = queries[tokens]
            qkv_ref[latent, :, D : 2 * D] = keys_all[tokens]
            qkv_ref[latent, :, 2 * D :] = values_all[tokens]
            for head in range(HEADS):
                lanes = lanes_of(head // 2)
                own = queries[tokens, lanes] * (masks[head % 2] * FACTOR)
                score_ref[latent, head] = mm_nt(keys_all[tokens, lanes], own)
        for latent in range(group):
            tokens = slice(latent * seq, (latent + 1) * seq)
            values_t = values_all[tokens].T
            for head in range(HEADS):
                scores = score_ref[latent, head]
                expo = jnp.exp(scores - jnp.max(scores, axis=0, keepdims=True))
                probs_ref[latent, head] = (expo * (1.0 / col_sum(expo))).astype(BF16)
            for head in range(HEADS):
                rows = slice(head * HEAD_DIM, (head + 1) * HEAD_DIM)
                mixed_ref[latent, rows, :] = mm(values_t[rows, :], probs_ref[latent, head]).astype(BF16)
            branch_ref[latent] = mm_tn(mixed_ref[latent], proj_ref[...])

    @pl.when(step == pl.num_programs(0) - 1)
    def _():
        store.wait()


def mlp_kernel(n_pieces, n_out, scal_ref, mod_ref, proj_ref, x_ref, branch_ref, mixed_ref, cot_ref, *refs):
    pieces = refs[:n_pieces]
    outs = refs[n_pieces : n_pieces + 5 + n_out]
    out_ref, dx_ref, dmixed_ref, dmod_ref, dproj_ref = outs[:5]
    send_refs = outs[5:]
    scratch = refs[n_pieces + 5 + n_out :]
    rows_ref, fc1_ref, fc2_ref, bias_ref, act_ref, slope_ref, du_ref, dfc1_ref, dfc2_ref, dbias_ref = scratch[:10]
    stage_refs, sem_refs = scratch[10 : 10 + n_out], scratch[10 + n_out :]
    step = pl.program_id(0)
    last = pl.num_programs(0) - 1

    @pl.when(step == 0)
    def _():
        assemble(scal_ref, 1, pieces, rows_ref)
        for block in range(4):
            for tile in range(TILES):
                fc1_ref[:, lanes_of(tile, block * D)] = rows_ref[
                    tile, pl.ds(FC1_AT + block, D, stride=4), :
                ].astype(BF16)
                bias_ref[0:1, lanes_of(tile, block * D)] = rows_ref[tile, pl.ds(B_FC1_AT + block, 1), :]
        for tile in range(TILES):
            fc2_ref[:, lanes_of(tile)] = rows_ref[tile, pl.ds(FC2_AT, FF), :].astype(BF16)
            bias_ref[1:2, lanes_of(tile)] = rows_ref[tile, pl.ds(B_FC2_AT, 1), :]
            bias_ref[2:3, lanes_of(tile)] = rows_ref[tile, pl.ds(B_PROJ_AT, 1), :]
        dfc1_ref[...] = jnp.zeros_like(dfc1_ref)
        dfc2_ref[...] = jnp.zeros_like(dfc2_ref)
        dbias_ref[...] = jnp.zeros_like(dbias_ref)
        dproj_ref[...] = jnp.zeros_like(dproj_ref)
        dmod_ref[...] = jnp.zeros_like(dmod_ref)

    group, seq = x_ref.shape[0], x_ref.shape[1]

    @pl.when(step * group < scal_ref[0])
    def _():
        gate_one, shift, scale, gate_two = [mod_rows(mod_ref, 2 + part, step, group) for part in range(4)]
        slot = step * group + lax.broadcasted_iota(jnp.int32, (group, 1, 1), 0)
        live = (slot < scal_ref[0]).astype(F32)
        branch_one = branch_ref[...] + bias_ref[2:3, :D]
        middle = x_ref[...].astype(F32) + gate_one * branch_one
        normed, rstd = normalize(middle)
        modulated = flat(normed * (1.0 + scale) + shift).astype(BF16)
        chunk = CHUNK
        for start in range(0, FF, chunk):
            part = slice(start, start + chunk)
            pre = mm(modulated, fc1_ref[:, part]) + bias_ref[0:1, part]
            square = pre * pre
            bend = jnp.tanh(pre * (GELU_A + (GELU_A * GELU_B) * square))
            half = 0.5 + 0.5 * bend
            act = (pre * half).astype(BF16)
            act_ref[:, part] = act
            slope_ref[:, part] = half + (pre * (0.5 - 0.5 * bend * bend)) * (
                GELU_A + (3.0 * GELU_A * GELU_B) * square
            )
        branch_two = mm(act_ref[...], fc2_ref[...])
        branch_two = (branch_two + bias_ref[1:2, :D]).reshape(group, seq, D)
        out_ref[...] = (live * (middle + gate_two * branch_two)).astype(BF16)
        grad_out = live * cot_ref[...].astype(F32)
        put_mod(dmod_ref, 3, step, grad_out * branch_two)
        grad_two = flat(gate_two * grad_out).astype(BF16)
        dbias_ref[1:2, :D] += col_sum(grad_two.astype(F32))
        grad_two_t = grad_two.T
        modulated_t = modulated.T
        for start in range(0, FF, chunk):
            part = slice(start, start + chunk)
            du = (mm_nt(grad_two, fc2_ref[part, :]) * slope_ref[:, part]).astype(BF16)
            dbias_ref[0:1, part] += col_sum(du.astype(F32))
            du_ref[:, part] = du
        grad_mod = mm_nt(du_ref[...], fc1_ref[...]).reshape(group, seq, D)
        dfc2_ref[...] += mm(grad_two_t, act_ref[...])
        dfc1_ref[...] += mm(modulated_t, du_ref[...])
        put_mod(dmod_ref, 1, step, grad_mod)
        put_mod(dmod_ref, 2, step, grad_mod * normed)
        grad_middle = grad_out + normalize_back(grad_mod * (1.0 + scale), normed, rstd)
        dx_ref[...] = grad_middle
        put_mod(dmod_ref, 0, step, grad_middle * branch_one)
        grad_one = flat(gate_one * grad_middle).astype(BF16)
        dbias_ref[2:3, :D] += col_sum(grad_one.astype(F32))
        grad_mixed = mm_nt(grad_one, proj_ref[...]).astype(BF16)
        for latent in range(group):
            tokens = slice(latent * seq, (latent + 1) * seq)
            dproj_ref[...] += mm(mixed_ref[latent], grad_one[tokens])
            dmixed_ref[latent] = grad_mixed[tokens]

    @pl.when(step * group >= scal_ref[0])
    def _():
        out_ref[...] = jnp.zeros_like(out_ref)
        dx_ref[...] = jnp.zeros_like(dx_ref)
        dmixed_ref[...] = jnp.zeros_like(dmixed_ref)

    @pl.when(step == last)
    def _():
        for block in range(4):
            for tile in range(TILES):
                rows_ref[tile, pl.ds(FC1_AT + block, D, stride=4), :] = dfc1_ref[
                    :, lanes_of(tile, block * D)
                ]
                rows_ref[tile, pl.ds(B_FC1_AT + block, 1), :] = dbias_ref[0:1, lanes_of(tile, block * D)]
        for tile in range(TILES):
            rows_ref[tile, pl.ds(FC2_AT, FF), :] = dfc2_ref[lanes_of(tile), :].T
            rows_ref[tile, pl.ds(B_FC2_AT, 1), :] = dbias_ref[1:2, lanes_of(tile)]
            rows_ref[tile, pl.ds(B_PROJ_AT, 1), :] = dbias_ref[2:3, lanes_of(tile)]
        emit(scal_ref, 1 + sum(ref.shape[0] for ref in pieces), send_refs, stage_refs, sem_refs, rows_ref)


def attend_back_kernel(scal_ref, qkv_ref, probs_ref, dmixed_ref, dqkv_ref, dprobs_ref, low_ref, dq_t_ref):
    group, seq = qkv_ref.shape[0], qkv_ref.shape[1]

    @pl.when(pl.program_id(0) * group < scal_ref[0])
    def _():
        masks = head_masks()
        for latent in range(group):
            keys_t = qkv_ref[latent, :, D : 2 * D].T
            for head in range(HEADS):
                own = dmixed_ref[latent, :, lanes_of(head // 2)] * masks[head % 2]
                dprobs_ref[head] = mm_nt(qkv_ref[latent, :, lanes_of(head // 2, 2 * D)], own)
            for head in range(HEADS):
                probs, grad_probs = probs_ref[latent, head].astype(F32), dprobs_ref[head]
                low_ref[head] = (probs * (grad_probs - col_sum(probs * grad_probs))).astype(BF16)
            for pair in range(HEADS // 2):
                query = qkv_ref[latent, :, lanes_of(pair)]
                grad = dmixed_ref[latent, :, lanes_of(pair)]
                grad_key = jnp.zeros((seq, LANES), F32)
                grad_value = jnp.zeros((seq, LANES), F32)
                for half in range(2):
                    head = 2 * pair + half
                    rows = slice(head * HEAD_DIM, (head + 1) * HEAD_DIM)
                    grad_value += mm(probs_ref[latent, head], grad * masks[half])
                    grad_key += mm(low_ref[head], query * masks[half])
                    dq_t_ref[rows, :] = mm(keys_t[rows, :], low_ref[head])
                dqkv_ref[latent, :, lanes_of(pair, D)] = (grad_key * FACTOR).astype(BF16)
                dqkv_ref[latent, :, lanes_of(pair, 2 * D)] = grad_value.astype(BF16)
            dqkv_ref[latent, :, :D] = (dq_t_ref[...] * FACTOR).astype(BF16).T


def finish_kernel(
    n_out, base, scal_ref, mod_ref, qkv_w_ref, cond_ref, ada_hbm_ref, dmod_in_ref, dproj_ref,
    x_ref, dqkv_ref, dx_ref, *refs
):
    grad_x_ref, grad_cond_ref = refs[:2]
    send_refs = refs[2 : 2 + n_out]
    scratch = refs[2 + n_out :]
    rows_ref, dqkv_w_ref, dmod_ref, dbias_ref, ada_ref, ada_sem = scratch[:6]
    stage_refs, sem_refs = scratch[6 : 6 + n_out], scratch[6 + n_out :]
    fetch = pltpu.make_async_copy(ada_hbm_ref, ada_ref, ada_sem)
    step = pl.program_id(0)
    last = pl.num_programs(0) - 1
    group, seq = x_ref.shape[0], x_ref.shape[1]

    @pl.when(step == 0)
    def _():
        fetch.start()
        dqkv_w_ref[...] = jnp.zeros_like(dqkv_w_ref)
        dmod_ref[...] = jnp.zeros_like(dmod_ref)
        dbias_ref[...] = jnp.zeros_like(dbias_ref)

    @pl.when(step * group < scal_ref[0])
    def _():
        shift, scale = [mod_rows(mod_ref, part, step, group) for part in range(2)]
        normed, rstd = normalize(x_ref[...].astype(F32))
        modulated = flat(normed * (1.0 + scale) + shift).astype(BF16)
        grad_qkv = flat(dqkv_ref[...])
        dbias_ref[0:1, :] += col_sum(grad_qkv.astype(F32))
        dqkv_w_ref[...] += mm(modulated.T, grad_qkv)
        grad_mod = mm_nt(grad_qkv, qkv_w_ref[...]).reshape(group, seq, D)
        put_mod(dmod_ref, 0, step, grad_mod)
        put_mod(dmod_ref, 1, step, grad_mod * normed)
        grad_x_ref[...] = dx_ref[...] + normalize_back(grad_mod * (1.0 + scale), normed, rstd)

    @pl.when(step * group >= scal_ref[0])
    def _():
        grad_x_ref[...] = jnp.zeros_like(grad_x_ref)

    @pl.when(step == last)
    def _():
        fetch.wait()
        cond = cond_ref[...].astype(F32)
        gate = jax.nn.sigmoid(cond)
        act = (cond * gate).astype(BF16)
        grad_act = jnp.zeros_like(cond)
        for block in range(6):
            grad = (dmod_ref[block] if block < 2 else dmod_in_ref[block - 2]).astype(BF16)
            grad_act += mm_nt(grad, ada_ref[block])
            weight = mm_tn(act, grad)
            bias = col_sum(grad.astype(F32))
            for tile in range(TILES):
                rows_ref[tile, pl.ds(ADA_AT + block, D, stride=6), :] = weight[:, lanes_of(tile)]
                rows_ref[tile, pl.ds(B_ADA_AT + block, 1), :] = bias[:, lanes_of(tile)]
        grad_cond_ref[...] = grad_act * (gate * (1.0 + cond * (1.0 - gate)))
        for tile in range(TILES):
            for block in range(3):
                rows_ref[tile, pl.ds(QKV_AT + block, D, stride=3), :] = dqkv_w_ref[
                    :, lanes_of(tile, block * D)
                ]
            rows_ref[tile, pl.ds(PROJ_AT, D), :] = dproj_ref[:, lanes_of(tile)]
            rows_ref[tile, pl.ds(B_QV_AT, 1), :] = dbias_ref[0:1, lanes_of(tile)]
            rows_ref[tile, pl.ds(B_QV_AT + 1, 1), :] = dbias_ref[0:1, lanes_of(tile, 2 * D)]
        emit(scal_ref, base, send_refs, stage_refs, sem_refs, rows_ref)


class Direct:
    def __init__(self, count, me):
        self.count, self.me = count, me
        self.gathered = self.sent = [jnp.int32(index) for index in range(count)]
        self.slots = [(count, F32)]

    def start(self, piece):
        return piece

    def gather(self, piece):
        return [lax.all_gather(piece, AXIS, axis=0)]

    def pass_on(self, held):
        return held

    def join(self, own, others):
        return own

    def begin(self, parts):
        return parts

    middle = send = begin

    def end(self, parts):
        return lax.psum_scatter(parts[0], AXIS, scatter_dimension=0)


class Stages:
    def __init__(self, count, me):
        self.me = me
        core, x, y, z = me % 2, me // 2 % 2, me // 4 % 2, me // 8

        def device(dz, dy, dx, dc):
            return (((z + dz) % 4 * 2 + (y + dy) % 2) * 2 + (x + dx) % 2) * 2 + (core + dc) % 2

        self.order(device)

    def order(self, device):
        gathered = []
        for dc in range(2):
            gathered += [device(-k, 0, 0, dc) for k in (0, 1, 2, 3)]
            gathered += [device(-k, 0, 1, dc) for k in (0, 1)]
            gathered += [device(-k, 1, 0, dc) for k in (2, 3)]
            gathered += [device(-k, 1, dx, dc) for dx in (0, 1) for k in (0, 1)]
            gathered += [device(-k, dy, 1, dc) for dy in (0, 1) for k in (2, 3)]
        self.gathered = gathered
        sent = []
        for dc in (1, 0):
            sent += [device(k, dy, dx, dc) for dx in (0, 1) for k in (0, 1) for dy in (0, 1)]
            sent += [device(k, dy, dx, dc) for dy in (0, 1) for k in (2, 3) for dx in (0, 1)]
        self.sent = sent
        self.slots = [(8, BF16)] * 4

    def shift(self, values, dz=0, dy=0, dx=0, dc=0):
        pairs = []
        for source in range(32):
            core, x, y, z = source % 2, source // 2 % 2, source // 4 % 2, source // 8
            target = (((z + dz) % 4 * 2 + (y + dy) % 2) * 2 + (x + dx) % 2) * 2 + (core + dc) % 2
            pairs.append((source, target))
        return lax.ppermute(values, AXIS, pairs)

    def start(self, piece):
        return jnp.stack([piece] + [self.shift(piece, dz=k) for k in (1, 2, 3)])

    def gather(self, own):
        first, second = own[:2], own[2:]
        by_x = self.shift(first, dx=1)
        by_y = self.shift(second, dy=1)
        by_xy = self.shift(jnp.concatenate([first, by_x]), dy=1)
        by_yx = self.shift(jnp.concatenate([second, by_y]), dx=1)
        return [own, by_x, by_y, by_xy, by_yx, jnp.concatenate([own, by_x, by_y])]

    def pass_on(self, held):
        early = held[-1]
        held = held[:-1]
        return held + [self.shift(array, dc=1) for array in (early, *held[3:])]

    def begin(self, parts):
        send_a, send_b, keep_a, keep_b = parts
        return self.shift(send_a, dc=1), self.shift(send_b, dc=1), keep_a, keep_b

    def middle(self, state):
        got_a, got_b, keep_a, keep_b = state
        shape = keep_a.shape[1:]
        sum_a = (keep_a.astype(F32) + got_a.astype(F32)).reshape((2, 4) + shape)
        sum_b = (keep_b.astype(F32) + got_b.astype(F32)).reshape((2, 4) + shape)
        return sum_a[0], sum_b[0], sum_a[1].astype(BF16), sum_b[1].astype(BF16)

    def send(self, state):
        sum_a, sum_b, out_a, out_b = state
        return sum_a, sum_b, self.shift(out_a, dx=1), self.shift(out_b, dy=1)

    def end(self, state):
        def swap(values, **how):
            return self.shift(values.astype(BF16), **how).astype(F32)

        sum_a, sum_b, got_a, got_b = state
        shape = sum_a.shape[1:]
        sum_a = (sum_a + got_a.astype(F32)).reshape((2, 2) + shape)
        sum_b = (sum_b + got_b.astype(F32)).reshape((2, 2) + shape)
        sum_a = sum_a[:, 0] + swap(sum_a[:, 1], dy=1)
        sum_b = sum_b[:, 0] + swap(sum_b[:, 1], dx=1)
        return (
            sum_a[0] + swap(sum_a[1], dz=1) + swap(sum_b[0], dz=2) + swap(sum_b[1], dz=3)
        )


class Straight(Stages):
    def order(self, device):
        sides = [(0, 0), (0, 1), (1, 0), (1, 1)]
        self.gathered = [device(-k, dy, dx, dc) for dc in (0, 1) for dy, dx in sides for k in range(4)]
        self.sent = [device(k, dy, dx, dc) for dc in (1, 0) for dy, dx in sides for k in range(4)]
        self.slots = [(16, BF16)] * 2

    def pass_on(self, held):
        return held + [self.shift(array, dc=1) for array in held]

    def join(self, own, others):
        half = len(others) // 2
        return own[:1] + others[:half] + own[1:] + others[half:]

    def gather(self, own):
        return [own, self.shift(own, dx=1), self.shift(own, dy=1), self.shift(own, dx=1, dy=1)]

    def begin(self, parts):
        return self.shift(parts[0], dc=1), parts[1]

    def middle(self, state):
        got, keep = state
        total = (keep.astype(F32) + got.astype(F32)).reshape((4, 4) + keep.shape[1:])
        return total[0], total[1].astype(BF16), total[2].astype(BF16), total[3].astype(BF16)

    def send(self, state):
        total, by_x, by_y, by_both = state
        return total, self.shift(by_x, dx=1), self.shift(by_y, dy=1), self.shift(by_both, dx=1, dy=1)

    def end(self, state):
        total = state[0]
        for got in state[1:]:
            total = total + got.astype(F32)
        low = total[1:].astype(BF16)
        out = total[0]
        for k in (1, 2, 3):
            out = out + self.shift(low[k - 1], dz=k).astype(F32)
        return out


def to_piece(share, rows, me):
    size = share.shape[0]
    padded = jnp.pad(share, (GROUP, rows * D - size))
    return lax.dynamic_slice(padded, (GROUP - size * me % GROUP,), (rows * D,)).reshape(rows, D)


def from_piece(piece, size, me):
    return lax.dynamic_slice(piece.reshape(-1), (size * me % GROUP,), (size,))


def whole(shape=None):
    return pl.BlockSpec(memory_space=pltpu.VMEM)


def by_latent(group, *shape):
    zeros = (0,) * len(shape)
    return pl.BlockSpec((group,) + shape, lambda step, scal: (step,) + zeros)


def call(kernel, count, in_specs, out_specs, out_shape, scratch, args, flops):
    return pl.pallas_call(
        kernel,
        grid_spec=pltpu.PrefetchScalarGridSpec(
            num_scalar_prefetch=1,
            grid=(count,),
            in_specs=in_specs,
            out_specs=out_specs,
            scratch_shapes=scratch,
        ),
        out_shape=out_shape,
        compiler_params=pltpu.CompilerParams(
            vmem_limit_bytes=60 * 2**20, dimension_semantics=("arbitrary",)
        ),
        cost_estimate=pl.CostEstimate(flops=flops, bytes_accessed=20 * 2**20, transcendentals=0),
    )(*args)


def solution(mesh):
    devices = mesh.shape[AXIS]

    def body(latents, condition, attn_params, mlp_params, counts, cotangent):
        count, seq = latents.shape[0], latents.shape[1]
        me = lax.axis_index(AXIS)
        known = devices == 32
        plan = (Stages if known else Direct)(devices, me)
        mlp_plan = (Straight if known else Direct)(devices, me)
        attn_size, mlp_size = attn_params.shape[0], mlp_params.shape[0]
        attn_height = piece_rows(attn_size, devices)
        mlp_height = piece_rows(mlp_size, devices)

        def scalars(size, order):
            ids = jnp.stack(order.gathered + order.sent)
            return jnp.concatenate([counts.astype(jnp.int32), size * ids // GROUP]).astype(jnp.int32)

        attn_scal, mlp_scal = scalars(attn_size, plan), scalars(mlp_size, mlp_plan)
        attn_own, mlp_piece = plan.start(to_piece(attn_params, attn_height, me)), to_piece(mlp_params, mlp_height, me)
        attn_own, mlp_piece = lax.optimization_barrier((attn_own, mlp_piece))
        attn_pieces = plan.gather(attn_own)
        mlp_own = mlp_plan.start(mlp_piece)
        mlp_own, attn_pieces, attn_scal, mlp_scal = lax.optimization_barrier(
            (mlp_own, attn_pieces, attn_scal, mlp_scal)
        )
        attn_pieces = plan.pass_on(attn_pieces)
        mlp_pieces = mlp_plan.gather(mlp_own)

        def struct(shape, kind):
            return jax.ShapeDtypeStruct(shape, kind)

        n_pieces = len(attn_pieces)
        n_mlp_pieces = len(mlp_pieces) * (2 if known else 1)
        n_out, n_mlp_out = len(plan.slots), len(mlp_plan.slots)
        mod, ada, qkv_w, proj, _, qkv, probs, mixed, branch = call(
            lambda *refs: forward_kernel(n_pieces, *refs),
            count // FORWARD_STEP,
            [whole(), by_latent(FORWARD_STEP, seq, D)] + [whole()] * n_pieces,
            [whole(), pl.BlockSpec(memory_space=pl.ANY)] + [whole()] * 3
            + [
                by_latent(FORWARD_STEP, seq, 3 * D),
                by_latent(FORWARD_STEP, HEADS, seq, seq),
                by_latent(FORWARD_STEP, D, seq),
                by_latent(FORWARD_STEP, seq, D),
            ],
            [
                struct((6, count, D), F32),
                struct((6, D, D), BF16),
                struct((D, 3 * D), BF16),
                struct((D, D), BF16),
                struct((8, D), F32),
                struct((count, seq, 3 * D), BF16),
                struct((count, HEADS, seq, seq), BF16),
                struct((count, D, seq), BF16),
                struct((count, seq, D), F32),
            ],
            [
                pltpu.VMEM((TILES, ATTN_ROWS + attn_height, LANES), F32),
                pltpu.VMEM((FORWARD_STEP, HEADS, seq, seq), F32),
                pltpu.VMEM((6, D, D), BF16),
                pltpu.SemaphoreType.DMA,
            ],
            [attn_scal, condition, latents] + attn_pieces,
            15 * 10**9,
        )
        mlp_own = mlp_plan.pass_on(mlp_pieces[:1])
        mlp_pieces, mod = lax.optimization_barrier((mlp_pieces[1:], mod))
        mlp_pieces = mlp_plan.join(mlp_own, mlp_plan.pass_on(mlp_pieces))
        results = call(
            lambda *refs: mlp_kernel(n_mlp_pieces, n_mlp_out, *refs),
            count // MLP_STEP,
            [whole(), whole(), by_latent(MLP_STEP, seq, D), by_latent(MLP_STEP, seq, D), by_latent(MLP_STEP, D, seq), by_latent(MLP_STEP, seq, D)]
            + [whole()] * n_mlp_pieces,
            [by_latent(MLP_STEP, seq, D), by_latent(MLP_STEP, seq, D), by_latent(MLP_STEP, seq, D), whole(), whole()]
            + [pl.BlockSpec(memory_space=pl.ANY)] * n_mlp_out,
            [
                struct((count, seq, D), BF16),
                struct((count, seq, D), F32),
                struct((count, seq, D), BF16),
                struct((4, count, D), F32),
                struct((D, D), F32),
            ]
            + [struct((slots, mlp_height, D), kind) for slots, kind in mlp_plan.slots],
            [
                pltpu.VMEM((TILES, MLP_ROWS + 2 + mlp_height, LANES), F32),
                pltpu.VMEM((D, FF), BF16),
                pltpu.VMEM((FF, D), BF16),
                pltpu.VMEM((8, FF), F32),
                pltpu.VMEM((MLP_STEP * seq, FF), BF16),
                pltpu.VMEM((MLP_STEP * seq, FF), F32),
                pltpu.VMEM((MLP_STEP * seq, FF), BF16),
                pltpu.VMEM((D, FF), F32),
                pltpu.VMEM((D, FF), F32),
                pltpu.VMEM((8, FF), F32),
            ]
            + [pltpu.VMEM((slots, mlp_height, D), kind) for slots, kind in mlp_plan.slots]
            + [pltpu.SemaphoreType.DMA] * n_mlp_out,
            [mlp_scal, mod, proj, latents, branch, mixed, cotangent] + mlp_pieces,
            30 * 10**9,
        )
        output, grad_middle, grad_mixed, dmod, dproj = results[:5]
        sums = mlp_plan.begin(results[5:])
        grad_qkv, = call(
            attend_back_kernel,
            count // ATTEND_STEP,
            [by_latent(ATTEND_STEP, seq, 3 * D), by_latent(ATTEND_STEP, HEADS, seq, seq), by_latent(ATTEND_STEP, seq, D)],
            [by_latent(ATTEND_STEP, seq, 3 * D)],
            [struct((count, seq, 3 * D), BF16)],
            [
                pltpu.VMEM((HEADS, seq, seq), F32),
                pltpu.VMEM((HEADS, seq, seq), BF16),
                pltpu.VMEM((D, seq), F32),
            ],
            [attn_scal, qkv, probs, grad_mixed],
            13 * 10**9,
        )
        sums, grad_qkv = lax.optimization_barrier((sums, grad_qkv))
        sums = mlp_plan.middle(sums)
        sums, grad_qkv = lax.optimization_barrier((sums, grad_qkv))
        sums = mlp_plan.send(sums)
        results = call(
            lambda *refs: finish_kernel(n_out, 1 + devices, *refs),
            count // FINISH_STEP,
            [whole()] * 3 + [pl.BlockSpec(memory_space=pl.ANY)] + [whole()] * 2 + [by_latent(FINISH_STEP, seq, D), by_latent(FINISH_STEP, seq, 3 * D), by_latent(FINISH_STEP, seq, D)],
            [by_latent(FINISH_STEP, seq, D), whole()] + [pl.BlockSpec(memory_space=pl.ANY)] * n_out,
            [struct((count, seq, D), F32), struct((count, D), F32)]
            + [struct((slots, attn_height, D), kind) for slots, kind in plan.slots],
            [
                pltpu.VMEM((TILES, ATTN_ROWS + attn_height, LANES), F32),
                pltpu.VMEM((D, 3 * D), F32),
                pltpu.VMEM((2, count, D), F32),
                pltpu.VMEM((8, 3 * D), F32),
                pltpu.VMEM((6, D, D), BF16),
                pltpu.SemaphoreType.DMA,
            ]
            + [pltpu.VMEM((slots, attn_height, D), kind) for slots, kind in plan.slots]
            + [pltpu.SemaphoreType.DMA] * n_out,
            [attn_scal, mod, qkv_w, condition, ada, dmod, dproj, latents, grad_qkv, grad_middle],
            15 * 10**9,
        )
        grad_latents, grad_condition = results[:2]
        sums, attn_parts = lax.optimization_barrier((sums, results[2:]))
        attn_parts = plan.middle(plan.begin(attn_parts))
        out_last, sums = lax.optimization_barrier((attn_parts[-1], sums))
        grad_attn = plan.end(plan.send([*attn_parts[:-1], out_last]))
        grad_mlp = mlp_plan.end(sums)
        return (
            output,
            grad_latents,
            grad_condition,
            from_piece(grad_attn, attn_size, me),
            from_piece(grad_mlp, mlp_size, me),
        )

    in_specs = (
        P(AXIS, None, None),
        P(AXIS, None),
        P(AXIS),
        P(AXIS),
        P(AXIS),
        P(AXIS, None, None),
    )
    out_specs = (
        P(AXIS, None, None),
        P(AXIS, None, None),
        P(AXIS, None),
        P(AXIS),
        P(AXIS),
    )
    return jax.shard_map(body, mesh=mesh, in_specs=in_specs, out_specs=out_specs, check_vma=False)
```
